256 devices in a mesh: ctx: 128 (over z, x, y), head: 2 (over core).
Axes of the slice: x: 4, y: 4, z: 8, core: 2. Of those that a mesh axis runs over, the one named last changes fastest.
Arguments:
- context_query_array: bfloat16 [32768, 8192], P('ctx', 'head'), may hold values from -6.5 to 6.5
- context_key_array: bfloat16 [32768, 1024], P('ctx', 'head'), may hold values from -6 to 6
- context_value_array: bfloat16 [32768, 1024], P('ctx', 'head'), may hold values from -12 to 12
- block_lengths: int32 [128], P('ctx'), may hold values from 1 to 256, 24576 in all
- pending_request_queries: bfloat16 [4096, 8192], P(('ctx', 'head')), may hold values from -6.5 to 6.5
- pending_request_keys: bfloat16 [4096, 1024], P('ctx', 'head'), may hold values from -6 to 6
- pending_request_values: bfloat16 [4096, 1024], P('ctx', 'head'), may hold values from -6 to 6
- query_owner: int32 [1], replicated, may hold values from 0 to 127
Outputs:
- context_output: bfloat16 [32768, 8192], P('ctx', 'head')
- request_output: bfloat16 [4096, 8192], P('ctx', 'head')
The draws below stay inside these ranges and needn't reach their ends.
Inputs may be any that keep to these rules, and one draw needn't show every extreme that they name: `block_lengths`: they sum to 24576 and the largest is 256.
All inputs are finite; a program needn't handle non-finite values. No bound on the sum of `block_lengths` on one device may be relied on, other than what follows from the above.
Results may differ from the reference program's by a relative error of at most 0.0085.
Values may be sent and summed in bfloat16 or wider, within the bound.
No kernel may reach another device: no remote copies, remote signals or barrier semaphores. Data moves between devices by JAX's collectives and lax.ppermute only.
A program may use at most 320 MiB of HBM per device.

```python
import math
import jax
import jax.numpy as jnp
import numpy as np
from jax import lax

QUERY_HEADS = 64
KEY_VALUE_HEADS = 8
HEAD_SIZE = 128
BLOCK_SLOTS = 256
REQUEST_ROWS = 32
CONTEXT_SLOTS = 32768
N_CTX = 128


def draw_context_query_array(key, part):
    key = jax.random.fold_in(key, 11)
    base_offset = 1.2 * jnp.clip(jax.random.normal(key, (CONTEXT_SLOTS, QUERY_HEADS, HEAD_SIZE), jnp.float32), -5.0, 5.0)
    return base_offset.reshape(CONTEXT_SLOTS, QUERY_HEADS * HEAD_SIZE).astype(jnp.bfloat16)


def draw_context_key_array(key, part):
    key = jax.random.fold_in(key, 12)
    base_offset = 1.2 * jnp.clip(jax.random.normal(key, (CONTEXT_SLOTS, KEY_VALUE_HEADS, HEAD_SIZE), jnp.float32), -5.0, 5.0)
    return base_offset.reshape(CONTEXT_SLOTS, KEY_VALUE_HEADS * HEAD_SIZE).astype(jnp.bfloat16)


def draw_context_value_array(key, part):
    key = jax.random.fold_in(key, 13)
    scale_key, entry_random_key = jax.random.split(key)
    row_scale_factor = jnp.exp(jax.random.uniform(scale_key, (CONTEXT_SLOTS, 1), jnp.float32, jnp.log(0.3), jnp.log(3.0)))
    base_offset = jnp.clip(jax.random.normal(entry_random_key, (CONTEXT_SLOTS, KEY_VALUE_HEADS * HEAD_SIZE), jnp.float32), -4.0, 4.0) * row_scale_factor
    return base_offset.astype(jnp.bfloat16)


def draw_pending_request_queries(key, part):
    key = jax.random.fold_in(key, 14)
    total_rows = N_CTX * REQUEST_ROWS
    base_offset = 1.2 * jnp.clip(jax.random.normal(key, (total_rows, QUERY_HEADS, HEAD_SIZE), jnp.float32), -5.0, 5.0)
    return base_offset.reshape(total_rows, QUERY_HEADS * HEAD_SIZE).astype(jnp.bfloat16)


def block_scale(key, extent, cuts, least, largest):
    factor_of = 1.0
    for position, shards_of in cuts:
        heights = jax.random.uniform(jax.random.fold_in(jax.random.fold_in(key, 6), position), (shards_of,), jnp.float32, least / len(cuts), largest / len(cuts))
        factor_of = factor_of * jnp.repeat(jnp.exp(heights), extent[position] // shards_of).reshape((-1,) + (1,) * (len(extent) - 1 - position))
    return factor_of


def length_profile(amount, total, most, slope):
    weights = [(1 << 20) // math.isqrt(rank ** slope) + 1 for rank in range(2, amount + 1)]
    rest, counts = total - most - (amount - 1), [1] * (amount - 1)
    while rest > 0:
        movable = [i for i in range(amount - 1) if counts[i] < most]
        pool, budget = sum([weights[i] for i in movable]), rest
        for i in movable:
            addition = min(most - counts[i], max(1, budget * weights[i] // pool), rest)
            counts[i] = counts[i] + addition
            rest = rest - addition
    return np.array([most] + counts)


def ragged(rng, amount, total, limit, slope):
    if amount == 2:
        one = jax.random.randint(rng, (), max(1, total - limit), min(limit, total - 1) + 1)
        return jnp.stack([one, total - one])
    sizes = jnp.asarray(length_profile(amount, total, limit, slope), jnp.int32)
    couples = (amount - 1) // 2
    source_of, sink = sizes[1:1 + 2 * couples:2], sizes[2:2 + 2 * couples:2]
    slack = jnp.minimum(source_of - 1, limit - sink)
    moved = jax.random.randint(jax.random.fold_in(rng, 1), (couples,), 0, 1 << 20) % (slack + 1)
    sizes = sizes.at[1:1 + 2 * couples:2].set(source_of - moved).at[2:2 + 2 * couples:2].set(sink + moved)
    return sizes[jax.random.permutation(jax.random.fold_in(rng, 2), amount)]


def gaussian(stream_key, shape, width, most, pieces=(), held_as=jnp.bfloat16):
    drawn = jax.random.normal(stream_key, shape, jnp.float32) * width
    if len(pieces) > 0:
        drawn = block_scale(stream_key, shape, pieces, -0.22, 0.18) * drawn
    return jnp.clip(drawn, min=-most, max=most).astype(held_as)


def setup_inputs(seed: int = 0) -> dict:
    seeds = jax.random.split(jax.random.key(seed), 9)
    return {
        "context_query_array": draw_context_query_array(jax.random.fold_in(seeds[8], 71), 0),
        "context_key_array": draw_context_key_array(jax.random.fold_in(seeds[8], 71), 0),
        "context_value_array": draw_context_value_array(jax.random.fold_in(seeds[8], 71), 0),
        "block_lengths": ragged(seeds[3], N_CTX, 3 * N_CTX * BLOCK_SLOTS // 4, BLOCK_SLOTS, 2).astype(jnp.int32),
        "pending_request_queries": draw_pending_request_queries(jax.random.fold_in(seeds[8], 71), 0),
        "pending_request_keys": gaussian(seeds[5], (N_CTX * REQUEST_ROWS, KEY_VALUE_HEADS * HEAD_SIZE), 1.2, 6.0, ((0, 128), (1, 2))),
        "pending_request_values": gaussian(seeds[6], (N_CTX * REQUEST_ROWS, KEY_VALUE_HEADS * HEAD_SIZE), 1.0, 6.0, ((0, 128), (1, 2))),
        "query_owner": jax.random.randint(seeds[7], (1,), 0, N_CTX).astype(jnp.int32),
    }


def softmax_part(queries, key_rows, value_rows, usable):
    score_scale = queries.shape[-1] ** -0.5
    scores = jnp.einsum("rhgd,khd->hgrk", queries.astype(jnp.float32), key_rows.astype(jnp.float32)) * score_scale
    scores = jnp.where(usable[None, None], scores, -jnp.inf)
    row_max = jnp.max(scores, axis=3)
    weights = jnp.exp(scores - row_max[..., None]).astype(jnp.bfloat16)
    row_total = jnp.sum(weights.astype(jnp.float32), axis=3)
    weighted = jnp.einsum("hgrk,khd->hgrd", weights.astype(jnp.float32), value_rows.astype(jnp.float32))
    return row_max, row_total, weighted


def combine(first, second):
    max_a, total_a, acc_a = first
    max_b, total_b, acc_b = second
    peak = jnp.maximum(max_a, max_b)
    factor_a = jnp.exp(max_a - peak)
    factor_b = jnp.exp(max_b - peak)
    return peak, total_a * factor_a + total_b * factor_b, acc_a * factor_a[..., None] + acc_b * factor_b[..., None]


def reference(context_query_array, context_key_array, context_value_array, block_lengths, pending_request_queries, pending_request_keys, pending_request_values, query_owner):
    group_index = QUERY_HEADS // KEY_VALUE_HEADS
    every_query = context_query_array.reshape(N_CTX, BLOCK_SLOTS, KEY_VALUE_HEADS, group_index, HEAD_SIZE)
    every_key = context_key_array.reshape(N_CTX, BLOCK_SLOTS, KEY_VALUE_HEADS, HEAD_SIZE)
    every_value = context_value_array.reshape(N_CTX, BLOCK_SLOTS, KEY_VALUE_HEADS, HEAD_SIZE)
    anchor_keys = every_key[0]
    anchor_values = every_value[0]
    anchor_len = block_lengths[0]
    row_ids = jnp.arange(BLOCK_SLOTS, dtype=jnp.int32)

    def one_block(items):
        queries, key_rows, value_rows, own_len, block_id = items
        sees_anchor = (row_ids[None, :] < anchor_len) & (block_id > 0)
        usable = jnp.concatenate([jnp.broadcast_to(sees_anchor, (BLOCK_SLOTS, BLOCK_SLOTS)), row_ids[None, :] <= row_ids[:, None]], axis=1)
        part = softmax_part(queries, jnp.concatenate([anchor_keys, key_rows], axis=0), jnp.concatenate([anchor_values, value_rows], axis=0), usable)
        result = (part[2] / part[1][..., None]).transpose(2, 0, 1, 3).reshape(BLOCK_SLOTS, QUERY_HEADS * HEAD_SIZE)
        return jnp.where((row_ids < own_len)[:, None], result, 0.0).astype(jnp.bfloat16)

    block_ids = jnp.arange(N_CTX, dtype=jnp.int32)
    context_output = lax.map(one_block, (every_query, every_key, every_value, block_lengths, block_ids)).reshape(N_CTX * BLOCK_SLOTS, QUERY_HEADS * HEAD_SIZE)

    owner_id = query_owner[0].astype(jnp.int32)
    start_offset = (owner_id * REQUEST_ROWS).astype(jnp.int32)
    asked_rows = lax.dynamic_slice_in_dim(pending_request_queries, start_offset, REQUEST_ROWS, 0).reshape(REQUEST_ROWS, KEY_VALUE_HEADS, group_index, HEAD_SIZE)
    local_block_keys = lax.dynamic_slice_in_dim(pending_request_keys, start_offset, REQUEST_ROWS, 0).reshape(REQUEST_ROWS, KEY_VALUE_HEADS, HEAD_SIZE)
    local_block_values = lax.dynamic_slice_in_dim(pending_request_values, start_offset, REQUEST_ROWS, 0).reshape(REQUEST_ROWS, KEY_VALUE_HEADS, HEAD_SIZE)
    query_ids = jnp.arange(REQUEST_ROWS, dtype=jnp.int32)
    self_part = softmax_part(asked_rows, local_block_keys, local_block_values, query_ids[None, :] <= query_ids[:, None])

    def add_block(carry, items):
        key_rows, value_rows, own_len = items
        usable = jnp.broadcast_to(row_ids[None, :] < own_len, (REQUEST_ROWS, BLOCK_SLOTS))
        return combine(carry, softmax_part(asked_rows, key_rows, value_rows, usable)), None

    merged, _ = lax.scan(add_block, self_part, (every_key, every_value, block_lengths))
    answer = (merged[2] / merged[1][..., None]).transpose(2, 0, 1, 3).reshape(REQUEST_ROWS, QUERY_HEADS * HEAD_SIZE).astype(jnp.bfloat16)
    chosen = (block_ids == owner_id)[:, None, None]
    request_output = jnp.where(chosen, answer[None], jnp.zeros((1, REQUEST_ROWS, QUERY_HEADS * HEAD_SIZE), jnp.bfloat16)).astype(jnp.bfloat16)
    return context_output, request_output.reshape(N_CTX * REQUEST_ROWS, QUERY_HEADS * HEAD_SIZE)
```

```python
import functools

import jax
import jax.numpy as jnp
from jax import lax
from jax.experimental import pallas as pl
from jax.experimental.pallas import tpu as pltpu
from jax.sharding import PartitionSpec as P

HEAD_SIZE = 128
GROUP = 8
SCALE = HEAD_SIZE**-0.5
LOG2E = 1.4426950408889634
LN2 = 0.6931471805599453
MARK = 1024.0
VMEM_LIMIT = 32 * 1024 * 1024


def dot_nt(a, b):
    return lax.dot_general(a, b, (((1,), (1,)), ((), ())), preferred_element_type=jnp.float32)


def dot_nn(a, b):
    return lax.dot_general(a, b, (((1,), (0,)), ((), ())), preferred_element_type=jnp.float32)


def context_kernel(count, len_ref, root_ref, q_ref, k_ref, v_ref, *refs):
    ak_refs, av_refs = refs[:count], refs[count : 2 * count]
    o_ref, va_ref, vo_ref = refs[-3:]
    rows = k_ref.shape[0]
    half = rows // 2
    own_len = len_ref[0]
    root = root_ref[0] > 0
    ak = jnp.concatenate([ref[...] for ref in ak_refs], axis=0)
    ak = jnp.where(root, jnp.broadcast_to(k_ref[0:1, :], ak.shape), ak)
    av = jnp.concatenate([ref[...] for ref in av_refs], axis=0)
    hidden = (av > 100.0) | root
    va_ref[:, :HEAD_SIZE] = jnp.where(hidden, jnp.zeros_like(av), av)
    va_ref[:, HEAD_SIZE:] = jnp.where(hidden, jnp.zeros_like(av), jnp.ones_like(av))
    vo_ref[:, :HEAD_SIZE] = v_ref[...]
    vo_ref[:, HEAD_SIZE:] = jnp.ones((rows, HEAD_SIZE), jnp.bfloat16)
    c = SCALE * LOG2E
    for top in (0, half):
        keys = top + half
        row = top + lax.broadcasted_iota(jnp.int32, (half, keys), 0)
        col = lax.broadcasted_iota(jnp.int32, (half, keys), 1)
        causal = jnp.where(col <= row, 0.0, -jnp.inf).astype(jnp.float32)
        live = (top + lax.broadcasted_iota(jnp.int32, (half, HEAD_SIZE), 0)) < own_len
        for g in range(GROUP):
            lanes = slice(g * HEAD_SIZE, (g + 1) * HEAD_SIZE)
            q = q_ref[top : top + half, lanes]
            sa = dot_nt(q, ak)
            so = dot_nt(q, k_ref[0:keys, :]) + causal
            peak = jnp.maximum(
                jnp.max(sa, axis=1, keepdims=True), jnp.max(so, axis=1, keepdims=True)
            )
            wa = jnp.exp2((sa - peak) * c).astype(jnp.bfloat16)
            wo = jnp.exp2((so - peak) * c).astype(jnp.bfloat16)
            acc = dot_nn(wa, va_ref[...]) + dot_nn(wo, vo_ref[0:keys, :])
            out = acc[:, :HEAD_SIZE] / acc[:, HEAD_SIZE:]
            o_ref[top : top + half, lanes] = jnp.where(live, out, 0.0).astype(jnp.bfloat16)


def context_attention(own_len, is_root, q, k, v, anchor, head, done):
    rows, width = q.shape
    heads = k.shape[1] // HEAD_SIZE
    wide = GROUP * HEAD_SIZE
    smem = pl.BlockSpec(memory_space=pltpu.SMEM)
    kv_spec = pl.BlockSpec((rows, HEAD_SIZE), lambda i: (0, head))
    wide_spec = pl.BlockSpec((rows, wide), lambda i: (0, head))
    count = len(anchor)
    slab = anchor[0].shape[0]
    operands = [own_len, is_root, q, k, v] + anchor + anchor
    specs = [smem, smem, wide_spec, kv_spec, kv_spec]
    specs += [pl.BlockSpec((slab, HEAD_SIZE), lambda i: (0, head))] * count
    specs += [pl.BlockSpec((slab, HEAD_SIZE), lambda i: (0, heads + head))] * count
    alias = {}
    if done is not None:
        alias = {len(operands): 0}
        operands, specs = operands + [done], specs + [pl.BlockSpec(memory_space=pl.ANY)]
    return pl.pallas_call(
        functools.partial(context_kernel, count),
        grid=(1,),
        out_shape=jax.ShapeDtypeStruct((rows, width), jnp.bfloat16),
        in_specs=specs,
        out_specs=wide_spec,
        input_output_aliases=alias,
        scratch_shapes=[
            pltpu.VMEM((rows, 2 * HEAD_SIZE), jnp.bfloat16),
            pltpu.VMEM((rows, 2 * HEAD_SIZE), jnp.bfloat16),
        ],
        compiler_params=pltpu.CompilerParams(vmem_limit_bytes=VMEM_LIMIT),
        cost_estimate=pl.CostEstimate(
            flops=8 * rows * wide * rows, bytes_accessed=5 * 2**18, transcendentals=2 * rows * rows * GROUP
        ),
        name="context_attention",
    )(*operands)


def mark_kernel(len_ref, k_ref, v_ref, *o_refs):
    rows, width = k_ref.shape
    slab = rows // len(o_refs)
    first = jnp.broadcast_to(k_ref[0:1, :], (slab, width))
    for i, o_ref in enumerate(o_refs):
        span = slice(i * slab, (i + 1) * slab)
        valid = (i * slab + lax.broadcasted_iota(jnp.int32, first.shape, 0)) < len_ref[0]
        o_ref[:, :width] = jnp.where(valid, k_ref[span, :], first)
        o_ref[:, width:] = jnp.where(valid, v_ref[span, :], jnp.full_like(first, MARK))


def mark(own_len, k, v, pieces):
    rows, width = k.shape
    vmem = pl.BlockSpec(memory_space=pltpu.VMEM)
    shape = jax.ShapeDtypeStruct((rows // pieces, 2 * width), k.dtype)
    return pl.pallas_call(
        mark_kernel,
        out_shape=[shape] * pieces,
        in_specs=[pl.BlockSpec(memory_space=pltpu.SMEM), vmem, vmem],
        out_specs=[vmem] * pieces,
        compiler_params=pltpu.CompilerParams(vmem_limit_bytes=VMEM_LIMIT),
        cost_estimate=pl.CostEstimate(flops=2**18, bytes_accessed=2**20, transcendentals=0),
        name="mark",
    )(own_len, k, v)


def pack_kernel(rq_ref, o_ref):
    own, width = rq_ref.shape
    slabs = o_ref.shape[0] // 2
    some = o_ref.shape[1] // own
    for j in range(slabs):
        for c in range(2):
            for i in range(some):
                lane = c * (width // 2) + (some * j + i) * HEAD_SIZE
                o_ref[2 * j + c, i * own : (i + 1) * own, :] = rq_ref[:, lane : lane + HEAD_SIZE]


def pack(rq, slabs):
    vmem = pl.BlockSpec(memory_space=pltpu.VMEM)
    height = rq.size // (2 * slabs * HEAD_SIZE)
    return pl.pallas_call(
        pack_kernel,
        out_shape=jax.ShapeDtypeStruct((2 * slabs, height, HEAD_SIZE), jnp.bfloat16),
        in_specs=[vmem],
        out_specs=vmem,
        compiler_params=pltpu.CompilerParams(vmem_limit_bytes=56 * 1024 * 1024),
        cost_estimate=pl.CostEstimate(flops=2**18, bytes_accessed=2**19, transcendentals=0),
        name="pack",
    )(rq)


def plane_kernel(slab_ref, x_ref, o_ref):
    own = 16
    source = 2 * slab_ref[0]
    parts = []
    for i in range(x_ref.shape[1] // own):
        pick = slice(i * own, (i + 1) * own)
        parts += [x_ref[source, pick, :], x_ref[source + 1, pick, :]]
    part = jnp.concatenate(parts, axis=0)
    for z in range(o_ref.shape[0]):
        o_ref[z] = part


def slab_kernel(plane_ref, x_ref, o_ref):
    part = x_ref[plane_ref[0]]
    for j in range(o_ref.shape[0]):
        o_ref[j] = part


def choose(kernel, index, x, shape):
    vmem = pl.BlockSpec(memory_space=pltpu.VMEM)
    return pl.pallas_call(
        kernel,
        out_shape=jax.ShapeDtypeStruct(shape, x.dtype),
        in_specs=[pl.BlockSpec(memory_space=pltpu.SMEM), vmem],
        out_specs=vmem,
        compiler_params=pltpu.CompilerParams(vmem_limit_bytes=VMEM_LIMIT),
        cost_estimate=pl.CostEstimate(flops=2**18, bytes_accessed=3 * 2**19, transcendentals=0),
        name="choose",
    )(index, x)


def split3(x):
    high = x.astype(jnp.bfloat16).astype(jnp.float32)
    rest = x - high
    mid = rest.astype(jnp.bfloat16).astype(jnp.float32)
    low = (rest - mid).astype(jnp.bfloat16).astype(jnp.float32)
    return high, mid, low


def code_rows(pair, last, height):
    row = lax.broadcasted_iota(jnp.int32, (height, HEAD_SIZE), 0)
    return jnp.where(row == 0, pair, jnp.where(row == 1, last, 0.0)).astype(jnp.bfloat16)


def request_kernel(len_ref, own_ref, q_ref, k_ref, v_ref, rk_ref, rv_ref, o_ref, vb_ref, vr_ref):
    count, height, _ = o_ref.shape
    piece = height - 16
    n = count * piece
    keys = k_ref.shape[0]
    own = rk_ref.shape[0]
    c = SCALE * LOG2E
    vb_ref[:, :HEAD_SIZE] = v_ref[...]
    vb_ref[:, HEAD_SIZE:] = jnp.ones((keys, HEAD_SIZE), jnp.bfloat16)
    vr_ref[:, :HEAD_SIZE] = rv_ref[...]
    vr_ref[:, HEAD_SIZE:] = jnp.ones((own, HEAD_SIZE), jnp.bfloat16)
    q = q_ref[:, 0:piece, :].reshape(n, HEAD_SIZE)
    seen = lax.broadcasted_iota(jnp.int32, (n, keys), 1) < len_ref[0]
    sb = jnp.where(seen, dot_nt(q, k_ref[...]), -jnp.inf)
    row = lax.rem(lax.broadcasted_iota(jnp.int32, (n, own), 0), own)
    col = lax.broadcasted_iota(jnp.int32, (n, own), 1)
    seen_own = (col <= row) & (own_ref[0] > 0)
    sr = jnp.where(seen_own, dot_nt(q, rk_ref[...]), -jnp.inf)
    peak = jnp.maximum(jnp.max(sb, axis=1, keepdims=True), jnp.max(sr, axis=1, keepdims=True))
    wb = jnp.exp2((sb - peak) * c).astype(jnp.bfloat16)
    wr = jnp.exp2((sr - peak) * c).astype(jnp.bfloat16)
    acc = dot_nn(wb, vb_ref[...]) + dot_nn(wr, vr_ref[...])
    total = acc[:, HEAD_SIZE:]
    out = (acc[:, :HEAD_SIZE] / total).astype(jnp.bfloat16)
    lse = peak * SCALE + jnp.log(total)
    high, mid, low = split3(lse)
    row = lax.broadcasted_iota(jnp.int32, (piece, HEAD_SIZE), 0)
    lane = lax.broadcasted_iota(jnp.int32, (piece, HEAD_SIZE), 1)
    for p in range(count):
        part = slice(p * piece, (p + 1) * piece)
        pair = jnp.where(row == lane, high[part], jnp.where(row + piece == lane, mid[part], 0.0))
        last = jnp.where(row == lane, low[part], 0.0)
        o_ref[p, 0:piece, :] = out[part]
        o_ref[p, piece:height, :] = code_rows(
            jnp.sum(pair, axis=0, keepdims=True), jnp.sum(last, axis=0, keepdims=True), height - piece
        )


def request_partials(own_len, is_owner, moved, k, v, rk, rv):
    pieces = moved.shape[0]
    heads = k.shape[1] // HEAD_SIZE
    keys, own = k.shape[0], rk.shape[0]
    rows = heads * GROUP * own
    height = rows // pieces + 16
    smem = pl.BlockSpec(memory_space=pltpu.SMEM)
    kv_spec = pl.BlockSpec((keys, HEAD_SIZE), lambda h: (0, h))
    own_spec = pl.BlockSpec((own, HEAD_SIZE), lambda h: (0, h))
    return pl.pallas_call(
        request_kernel,
        grid=(heads,),
        out_shape=jax.ShapeDtypeStruct((pieces, height, HEAD_SIZE), jnp.bfloat16),
        in_specs=[
            smem,
            smem,
            pl.BlockSpec((pieces // heads,) + moved.shape[1:], lambda h: (h, 0, 0)),
            kv_spec,
            kv_spec,
            own_spec,
            own_spec,
        ],
        out_specs=pl.BlockSpec((pieces // heads, height, HEAD_SIZE), lambda h: (h, 0, 0)),
        scratch_shapes=[
            pltpu.VMEM((keys, 2 * HEAD_SIZE), jnp.bfloat16),
            pltpu.VMEM((own, 2 * HEAD_SIZE), jnp.bfloat16),
        ],
        compiler_params=pltpu.CompilerParams(vmem_limit_bytes=VMEM_LIMIT),
        cost_estimate=pl.CostEstimate(
            flops=4 * rows * HEAD_SIZE * (keys + own), bytes_accessed=3 * 2**20, transcendentals=rows * (keys + own)
        ),
        name="request_partials",
    )(own_len, is_owner, moved, k, v, rk, rv)


def join_kernel(keep_code, x_ref, o_ref):
    height = x_ref.shape[1]
    piece = height - 16
    code = x_ref[:, piece:height, :].astype(jnp.float32)
    pair, last = code[:, 0, :], code[:, 1, :]
    lse = pair + pltpu.roll(pair, piece, 1) + last
    lse = jnp.where(lax.broadcasted_iota(jnp.int32, lse.shape, 1) < piece, lse, 0.0)
    peak = jnp.max(lse, axis=0, keepdims=True)
    weight = jnp.exp(lse - peak)
    total = jnp.sum(weight, axis=0, keepdims=True)
    column = jnp.transpose(weight / total)
    out = jnp.zeros((piece, HEAD_SIZE), jnp.float32)
    for i in range(x_ref.shape[0]):
        out = out + column[0:piece, i : i + 1] * x_ref[i, 0:piece, :].astype(jnp.float32)
    copies = o_ref.shape[0]
    o_ref[:, 0:piece, :] = jnp.broadcast_to(out.astype(jnp.bfloat16)[None], (copies, piece, HEAD_SIZE))
    if keep_code:
        high, mid, low = split3(peak + jnp.log(total))
        lane = lax.broadcasted_iota(jnp.int32, high.shape, 1)
        pair = jnp.where(lane < piece, high, pltpu.roll(mid, piece, 1))
        rows = code_rows(pair, low, 16)
        o_ref[:, piece:height, :] = jnp.broadcast_to(rows[None], (copies, 16, HEAD_SIZE))


def join(x, copies, keep_code):
    height = x.shape[1] if keep_code else x.shape[1] - 16
    return pl.pallas_call(
        functools.partial(join_kernel, keep_code),
        out_shape=jax.ShapeDtypeStruct((copies, height, HEAD_SIZE), jnp.bfloat16),
        compiler_params=pltpu.CompilerParams(vmem_limit_bytes=VMEM_LIMIT),
        cost_estimate=pl.CostEstimate(flops=2**20, bytes_accessed=2**19, transcendentals=1024),
        name="join_pieces",
    )(x)


def exchange(x, axis):
    return lax.all_to_all(x, axis, split_axis=0, concat_axis=0, tiled=True)


def local(n_z, n_xy, q, k, v, block_lengths, rq, rk, rv, query_owner):
    z, xy = lax.axis_index("z"), lax.axis_index("xy")
    owner = query_owner[0]
    owner_z, owner_xy = owner // n_xy, owner % n_xy
    own_len = block_lengths
    mine = (z == owner_z) & (xy == owner_xy)
    is_owner = mine.astype(jnp.int32).reshape(1)
    is_root = ((z == 0) & (xy == 0)).astype(jnp.int32).reshape(1)
    heads = q.shape[1] // HEAD_SIZE
    own_rows = rk.shape[0]

    moved = exchange(pack(rq, n_xy), ("xy", "head"))
    moved = choose(plane_kernel, owner_xy.reshape(1), moved, (n_z, 2 * moved.shape[1], HEAD_SIZE))
    moved = exchange(moved, "z")
    moved = choose(slab_kernel, owner_z.reshape(1), moved, (n_xy,) + moved.shape[1:])
    moved = exchange(moved, "xy")

    def move(x, pairs):
        return lax.ppermute(x, ("z", "xy"), pairs)

    n_x = 4
    n_y = n_xy // n_x
    x, y = xy // n_y, xy % n_y
    pieces = mark(own_len, k, v, n_x)
    held = [move(pieces[i], [(0, i * n_y)]) for i in range(1, n_x)]
    held = jnp.where(x == 0, pieces[0], held[0] + held[1] + held[2])
    rows_x = [i * n_y for i in range(n_x)]
    got = [move(held, [(p, p + i) for p in rows_x]) for i in range(1, n_y)]
    held = jnp.where(y == 0, held, got[0] + got[1] + got[2])
    plane = range(n_xy)
    got = [move(held, [(p, to * n_xy + p) for p in plane]) for to in (3, 5)]
    held = jnp.where(z == 0, held, got[0] + got[1])
    steps = (((0, 1), (3, 4), (5, 6)), ((0, 7), (3, 2)))
    got = [move(held, [(a * n_xy + p, b * n_xy + p) for a, b in step for p in plane]) for step in steps]
    held = jnp.where((z == 0) | (z == 3) | (z == 5), held, got[0] + got[1])
    anchor = [held]
    for i in range(1, n_x):
        pairs = []
        for a in range(n_z * n_x):
            there = a // n_x * n_x + (a + i) % n_x
            pairs += [(a * n_y + p, there * n_y + p) for p in range(n_y)]
        anchor.append(move(held, pairs))

    partials = request_partials(own_len, is_owner, moved, k, v, rk, rv)
    planes = join(exchange(partials, "xy"), n_z, True)
    joined = exchange(planes, "z")
    context_output = context_attention(own_len, is_root, q, k, v, anchor, 0, None)
    context_output = context_attention(own_len, is_root, q, k, v, anchor, 1, context_output)
    answer = exchange(join(joined, n_xy, False), "xy")
    for head in range(2, k.shape[1] // HEAD_SIZE):
        context_output = context_attention(own_len, is_root, q, k, v, anchor, head, context_output)
    answer = answer.reshape(heads, own_rows, HEAD_SIZE).transpose(1, 0, 2).reshape(own_rows, heads * HEAD_SIZE)
    request_output = jnp.where(mine, answer, jnp.zeros_like(answer))
    return context_output, request_output


def solution(mesh):
    n_z, n_xy = 8, 16
    grid = jax.sharding.Mesh(mesh.devices.reshape(n_z, n_xy, 2), ("z", "xy", "head"))
    ctx = ("z", "xy")
    in_specs = (
        P(ctx, "head"),
        P(ctx, "head"),
        P(ctx, "head"),
        P(ctx),
        P(("z", "xy", "head"), None),
        P(ctx, "head"),
        P(ctx, "head"),
        P(),
    )
    out_specs = (P(ctx, "head"), P(ctx, "head"))
    return jax.shard_map(
        functools.partial(local, n_z, n_xy),
        mesh=grid,
        in_specs=in_specs,
        out_specs=out_specs,
        check_vma=False,
    )
```

```python
import functools

import jax
import jax.numpy as jnp
from jax import lax
from jax.experimental import pallas as pl
from jax.experimental.pallas import tpu as pltpu
from jax.sharding import PartitionSpec as P

HEAD_SIZE = 128
GROUP = 8
SCALE = HEAD_SIZE**-0.5
LOG2E = 1.4426950408889634
LN2 = 0.6931471805599453
MARK = 1024.0
VMEM_LIMIT = 32 * 1024 * 1024


def dot_nt(a, b):
    return lax.dot_general(a, b, (((1,), (1,)), ((), ())), preferred_element_type=jnp.float32)


def dot_nn(a, b):
    return lax.dot_general(a, b, (((1,), (0,)), ((), ())), preferred_element_type=jnp.float32)


def context_kernel(count, len_ref, root_ref, q_ref, k_ref, v_ref, *refs):
    ak_refs, av_refs = refs[:count], refs[count : 2 * count]
    o_ref, vs_ref = refs[-2:]
    rows = k_ref.shape[0]
    half = rows // 2
    own_len = len_ref[0]
    root = root_ref[0] > 0
    ak = jnp.concatenate([ref[...] for ref in ak_refs], axis=0)
    ak = jnp.where(root, jnp.broadcast_to(k_ref[0:1, :], ak.shape), ak)
    av = jnp.concatenate([ref[...] for ref in av_refs], axis=0)
    hidden = (av > 100.0) | root
    vs_ref[0:rows, :HEAD_SIZE] = jnp.where(hidden, jnp.zeros_like(av), av)
    vs_ref[0:rows, HEAD_SIZE:] = jnp.where(hidden, jnp.zeros_like(av), jnp.ones_like(av))
    vs_ref[rows:, :HEAD_SIZE] = v_ref[...]
    vs_ref[rows:, HEAD_SIZE:] = jnp.ones((rows, HEAD_SIZE), jnp.bfloat16)
    c = SCALE * LOG2E
    row = lax.broadcasted_iota(jnp.int32, (2 * half, half), 0)
    col = lax.broadcasted_iota(jnp.int32, (2 * half, half), 1)
    causal = jnp.where(col <= lax.rem(row, half), 0.0, -jnp.inf).astype(jnp.float32)

    def lanes(g):
        return slice(g * HEAD_SIZE, (g + 1) * HEAD_SIZE)

    def scores(top, g):
        keys = top + half
        q = jnp.concatenate([q_ref[top:keys, lanes(g)], q_ref[top:keys, lanes(g + 1)]], axis=0)
        sa = dot_nt(q, ak)
        so = dot_nt(q, k_ref[0:keys, :])
        tiles = [sa[:, i : i + half] for i in range(0, rows, half)]
        tiles += [so[:, i : i + half] for i in range(0, top, half)]
        return tiles + [so[:, top:keys] + causal]

    def finish(top, g, tiles):
        keys = top + half
        live = (top + lax.broadcasted_iota(jnp.int32, (half, HEAD_SIZE), 0)) < own_len
        peak = jnp.max(functools.reduce(jnp.maximum, tiles), axis=1, keepdims=True)
        weights = [jnp.exp2((tile - peak) * c).astype(jnp.bfloat16) for tile in tiles]
        acc = dot_nn(jnp.concatenate(weights, axis=1), vs_ref[0 : rows + keys, :])
        total = acc[:, HEAD_SIZE:]
        inverse = pl.reciprocal(total, approx=True)
        inverse = inverse * (2.0 - total * inverse)
        out = acc[:, :HEAD_SIZE] * inverse
        for i in range(2):
            part = jnp.where(live, out[i * half : (i + 1) * half], 0.0)
            o_ref[top:keys, lanes(g + i)] = part.astype(jnp.bfloat16)

    work = [(top, g) for top in (0, half) for g in range(0, GROUP, 2)]
    tiles = scores(*work[0])
    for i, item in enumerate(work):
        later = scores(*work[i + 1]) if i + 1 < len(work) else None
        finish(*item, tiles)
        tiles = later


def context_attention(own_len, is_root, q, k, v, anchor):
    rows, width = q.shape
    heads = k.shape[1] // HEAD_SIZE
    wide = GROUP * HEAD_SIZE
    count = len(anchor)
    slab = anchor[0].shape[0]
    smem = pl.BlockSpec(memory_space=pltpu.SMEM)
    kv_spec = pl.BlockSpec((rows, HEAD_SIZE), lambda h: (0, h))
    wide_spec = pl.BlockSpec((rows, wide), lambda h: (0, h))
    specs = [smem, smem, wide_spec, kv_spec, kv_spec]
    specs += [pl.BlockSpec((slab, HEAD_SIZE), lambda h: (0, h))] * count
    specs += [pl.BlockSpec((slab, HEAD_SIZE), lambda h: (0, heads + h))] * count
    return pl.pallas_call(
        functools.partial(context_kernel, count),
        grid=(heads,),
        out_shape=jax.ShapeDtypeStruct((rows, width), jnp.bfloat16),
        in_specs=specs,
        out_specs=wide_spec,
        scratch_shapes=[pltpu.VMEM((2 * rows, 2 * HEAD_SIZE), jnp.bfloat16)],
        compiler_params=pltpu.CompilerParams(vmem_limit_bytes=VMEM_LIMIT),
        cost_estimate=pl.CostEstimate(
            flops=8 * rows * width * rows, bytes_accessed=5 * 2**20, transcendentals=2 * rows * rows * heads * GROUP
        ),
        name="context_attention",
    )(own_len, is_root, q, k, v, *anchor, *anchor)


def mark_kernel(n_x, len_ref, own_ref, y_ref, k_ref, v_ref, rk_ref, rv_ref, *o_refs):
    rows, width = k_ref.shape
    own = rk_ref.shape[0]
    slab = rows // n_x
    first = jnp.broadcast_to(k_ref[0:1, :], (slab, width))
    for i, o_ref in enumerate(o_refs[:n_x]):
        span = slice(i * slab, (i + 1) * slab)
        valid = (i * slab + lax.broadcasted_iota(jnp.int32, first.shape, 0)) < len_ref[0]
        o_ref[:, :width] = jnp.where(valid, k_ref[span, :], first)
        o_ref[:, width:] = jnp.where(valid, v_ref[span, :], jnp.full_like(first, MARK))
    lines = o_refs[n_x:]
    valid = lax.broadcasted_iota(jnp.int32, (rows, HEAD_SIZE), 0) < len_ref[0]
    is_owner = own_ref[0] > 0
    for i, o_ref in enumerate(lines):
        head = lax.rem(y_ref[0] + i, len(lines))
        lanes = pl.ds(pl.multiple_of(head * HEAD_SIZE, HEAD_SIZE), HEAD_SIZE)
        first = k_ref[0:1, lanes]
        o_ref[0:rows, :] = jnp.where(valid, k_ref[:, lanes], jnp.broadcast_to(first, valid.shape))
        o_ref[rows : rows + own, :] = jnp.where(
            is_owner, rk_ref[:, lanes], jnp.broadcast_to(first, (own, HEAD_SIZE))
        )
        mark = jnp.full((rows, HEAD_SIZE), MARK, jnp.bfloat16)
        o_ref[rows + own : 2 * rows + own, :] = jnp.where(valid, v_ref[:, lanes], mark)
        o_ref[2 * rows + own :, :] = jnp.where(is_owner, rv_ref[:, lanes], mark[0:own])


def mark(own_len, is_owner, y, k, v, rk, rv, n_x, n_y):
    rows, width = k.shape
    vmem = pl.BlockSpec(memory_space=pltpu.VMEM)
    smem = pl.BlockSpec(memory_space=pltpu.SMEM)
    shapes = [jax.ShapeDtypeStruct((rows // n_x, 2 * width), k.dtype)] * n_x
    shapes += [jax.ShapeDtypeStruct((2 * (rows + rk.shape[0]), HEAD_SIZE), k.dtype)] * n_y
    return pl.pallas_call(
        functools.partial(mark_kernel, n_x),
        out_shape=shapes,
        in_specs=[smem] * 3 + [vmem] * 4,
        out_specs=[vmem] * len(shapes),
        compiler_params=pltpu.CompilerParams(vmem_limit_bytes=56 * 1024 * 1024),
        cost_estimate=pl.CostEstimate(flops=2**18, bytes_accessed=2**21, transcendentals=0),
        name="mark",
    )(own_len, is_owner, y, k, v, rk, rv)


def pack_kernel(n_y, rq_ref, o_ref):
    own, width = rq_ref.shape
    targets = o_ref.shape[0] // 2
    some = o_ref.shape[1] // own
    for j in range(targets):
        x, y = j // n_y, j % n_y
        for c in range(2):
            for i in range(some):
                lane = c * (width // 2) + (GROUP * y + some * x + i) * HEAD_SIZE
                o_ref[2 * j + c, i * own : (i + 1) * own, :] = rq_ref[:, lane : lane + HEAD_SIZE]


def pack(rq, targets, n_y):
    vmem = pl.BlockSpec(memory_space=pltpu.VMEM)
    height = rq.size // (2 * targets * HEAD_SIZE)
    return pl.pallas_call(
        functools.partial(pack_kernel, n_y),
        out_shape=jax.ShapeDtypeStruct((2 * targets, height, HEAD_SIZE), jnp.bfloat16),
        in_specs=[vmem],
        out_specs=vmem,
        compiler_params=pltpu.CompilerParams(vmem_limit_bytes=56 * 1024 * 1024),
        cost_estimate=pl.CostEstimate(flops=2**18, bytes_accessed=2**19, transcendentals=0),
        name="pack",
    )(rq)


def plane_kernel(source_ref, x_ref, o_ref):
    own = 16
    source = 2 * source_ref[0]
    parts = []
    for i in range(x_ref.shape[1] // own):
        pick = slice(i * own, (i + 1) * own)
        parts += [x_ref[source, pick, :], x_ref[source + 1, pick, :]]
    part = jnp.concatenate(parts, axis=0)
    for z in range(o_ref.shape[0]):
        o_ref[z] = part


def line_kernel(plane_ref, x_ref, o_ref):
    part = x_ref[plane_ref[0]]
    piece = part.shape[0]
    for j in range(o_ref.shape[0]):
        o_ref[j, 0:piece, :] = part
        o_ref[j, piece : 2 * piece, :] = part


def choose(kernel, index, x, shape):
    vmem = pl.BlockSpec(memory_space=pltpu.VMEM)
    return pl.pallas_call(
        kernel,
        out_shape=jax.ShapeDtypeStruct(shape, x.dtype),
        in_specs=[pl.BlockSpec(memory_space=pltpu.SMEM), vmem],
        out_specs=vmem,
        compiler_params=pltpu.CompilerParams(vmem_limit_bytes=VMEM_LIMIT),
        cost_estimate=pl.CostEstimate(flops=8 * 10**8, bytes_accessed=2**19, transcendentals=0),
        name="choose",
    )(index, x)


def split3(x):
    high = x.astype(jnp.bfloat16).astype(jnp.float32)
    rest = x - high
    mid = rest.astype(jnp.bfloat16).astype(jnp.float32)
    low = (rest - mid).astype(jnp.bfloat16).astype(jnp.float32)
    return high, mid, low


def code_rows(pair, last, height):
    row = lax.broadcasted_iota(jnp.int32, (height, HEAD_SIZE), 0)
    return jnp.where(row == 0, pair, jnp.where(row == 1, last, 0.0)).astype(jnp.bfloat16)


def request_kernel(own, q_ref, *refs):
    lines, o_ref, v_ref = refs[:-2], refs[-2], refs[-1]
    count = q_ref.shape[0]
    height = o_ref.shape[1]
    piece = (height - 16) // 2
    n = count * piece
    both = lines[0].shape[0] // 2
    rows = both - own
    c = SCALE * LOG2E
    q = q_ref[:, 0:piece, :].reshape(n, HEAD_SIZE)
    for i, ref in enumerate(lines):
        for part, (top, at) in (
            (ref[both : both + rows, :], (i * rows, rows)),
            (ref[both + rows :, :], (len(lines) * rows + i * own, own)),
        ):
            hidden = part > 100.0
            v_ref[top : top + at, :HEAD_SIZE] = jnp.where(hidden, jnp.zeros_like(part), part)
            v_ref[top : top + at, HEAD_SIZE:] = jnp.where(hidden, jnp.zeros_like(part), jnp.ones_like(part))
    own_keys = jnp.concatenate([ref[rows:both, :] for ref in lines], axis=0)
    row = lax.rem(lax.broadcasted_iota(jnp.int32, (n, own_keys.shape[0]), 0), own)
    col = lax.rem(lax.broadcasted_iota(jnp.int32, (n, own_keys.shape[0]), 1), own)
    scores = [dot_nt(q, ref[0:rows, :]) for ref in lines]
    scores.append(jnp.where(col <= row, dot_nt(q, own_keys), -jnp.inf))
    tiles = [s[:, i : i + HEAD_SIZE] for s in scores for i in range(0, s.shape[1], HEAD_SIZE)]
    peak = jnp.max(functools.reduce(jnp.maximum, tiles), axis=1, keepdims=True)
    weights = [jnp.exp2((tile - peak) * c).astype(jnp.bfloat16) for tile in tiles]
    acc = dot_nn(jnp.concatenate(weights, axis=1), v_ref[...])
    total = acc[:, HEAD_SIZE:]
    out = acc[:, :HEAD_SIZE] / total
    out_high = out.astype(jnp.bfloat16)
    out_low = (out - out_high.astype(jnp.float32)).astype(jnp.bfloat16)
    lse = peak * SCALE + jnp.log(total)
    high, mid, low = split3(lse)
    row = lax.broadcasted_iota(jnp.int32, (piece, HEAD_SIZE), 0)
    lane = lax.broadcasted_iota(jnp.int32, (piece, HEAD_SIZE), 1)
    for p in range(count):
        part = slice(p * piece, (p + 1) * piece)
        pair = jnp.where(row == lane, high[part], jnp.where(row + piece == lane, mid[part], 0.0))
        last = jnp.where(row == lane, low[part], 0.0)
        o_ref[p, 0:piece, :] = out_high[part]
        o_ref[p, piece : 2 * piece, :] = out_low[part]
        o_ref[p, 2 * piece : height, :] = code_rows(
            jnp.sum(pair, axis=0, keepdims=True), jnp.sum(last, axis=0, keepdims=True), 16
        )


def request_partials(moved, lines, own):
    count, piece = moved.shape[0], moved.shape[1] // 2
    keys = len(lines) * lines[0].shape[0] // 2
    vmem = pl.BlockSpec(memory_space=pltpu.VMEM)
    return pl.pallas_call(
        functools.partial(request_kernel, own),
        out_shape=jax.ShapeDtypeStruct((count, 2 * piece + 16, HEAD_SIZE), jnp.bfloat16),
        in_specs=[vmem] * (1 + len(lines)),
        out_specs=vmem,
        scratch_shapes=[pltpu.VMEM((keys, 2 * HEAD_SIZE), jnp.bfloat16)],
        compiler_params=pltpu.CompilerParams(vmem_limit_bytes=VMEM_LIMIT),
        cost_estimate=pl.CostEstimate(
            flops=2 * 10**9, bytes_accessed=2**20, transcendentals=count * piece * keys
        ),
        name="request_partials",
    )(moved, *lines)


def join_kernel(parts_in, keep_code, *refs):
    x_refs, o_ref = refs[:-1], refs[-1]
    if len(x_refs) == 1:
        x_refs = [x_refs[0].at[i] for i in range(x_refs[0].shape[0])]
    height = x_refs[0].shape[0]
    top = height - 16
    piece = top // parts_in
    count = max(len(x_refs), 8)
    row = lax.broadcasted_iota(jnp.int32, (count, HEAD_SIZE), 0)
    lane = lax.broadcasted_iota(jnp.int32, (count, HEAD_SIZE), 1)
    pair = jnp.zeros((count, HEAD_SIZE), jnp.float32)
    last = jnp.zeros((count, HEAD_SIZE), jnp.float32)
    for i, ref in enumerate(x_refs):
        code = ref[top:height, :].astype(jnp.float32)
        pair = jnp.where(row == i, code[0:1, :], pair)
        last = jnp.where(row == i, code[1:2, :], last)
    lse = jnp.where(lane < piece, pair + pltpu.roll(pair, piece, 1) + last, 0.0)
    lse = jnp.where(row < len(x_refs), lse, -jnp.inf)
    peak = jnp.max(lse, axis=0, keepdims=True)
    weight = jnp.exp(lse - peak)
    total = jnp.sum(weight, axis=0, keepdims=True)
    column = jnp.transpose(weight / total)
    out = jnp.zeros((piece, HEAD_SIZE), jnp.float32)
    for i, ref in enumerate(x_refs):
        part = ref[0:piece, :].astype(jnp.float32)
        if parts_in > 1:
            part = part + ref[piece:top, :].astype(jnp.float32)
        out = out + column[0:piece, i : i + 1] * part
    parts = [out.astype(jnp.bfloat16)]
    if keep_code:
        high, mid, low = split3(peak + jnp.log(total))
        pair = jnp.where(lane[0:1] < piece, high, pltpu.roll(mid, piece, 1))
        parts.append(code_rows(pair, low, 16))
    part = jnp.concatenate(parts, axis=0)
    if len(o_ref.shape) == 2:
        o_ref[...] = part
    else:
        for i in range(o_ref.shape[0]):
            o_ref[i] = part


def join(arrays, copies, parts_in, keep_code):
    height = (arrays[0].shape[-2] - 16) // parts_in + (16 if keep_code else 0)
    shape = (copies, height, HEAD_SIZE) if copies else (height, HEAD_SIZE)
    return pl.pallas_call(
        functools.partial(join_kernel, parts_in, keep_code),
        out_shape=jax.ShapeDtypeStruct(shape, jnp.bfloat16),
        compiler_params=pltpu.CompilerParams(vmem_limit_bytes=VMEM_LIMIT),
        cost_estimate=pl.CostEstimate(flops=2 * 10**9, bytes_accessed=2**19, transcendentals=1024),
        name="join_pieces",
    )(*arrays)


def exchange(x, axis):
    return lax.all_to_all(x, axis, split_axis=0, concat_axis=0, tiled=True)


def local(n_z, n_x, n_y, q, k, v, block_lengths, rq, rk, rv, query_owner):
    n_xy = n_x * n_y
    z, x, y = (lax.axis_index(name) for name in ("z", "x", "y"))
    owner = query_owner[0]
    owner_z, owner_xy = owner // n_xy, owner % n_xy
    own_len = block_lengths
    mine = (z == owner_z) & (x * n_y + y == owner_xy)
    is_owner = mine.astype(jnp.int32).reshape(1)
    is_root = ((z == 0) & (x == 0) & (y == 0)).astype(jnp.int32).reshape(1)
    own_rows = rk.shape[0]

    def move(value, pairs):
        return lax.ppermute(value, ("z", "x", "y"), pairs)

    moved = exchange(pack(rq, n_xy, n_y), ("x", "y", "head"))
    marked = mark(own_len, is_owner, y.reshape(1), k, v, rk, rv, n_x, n_y)
    pieces, lines = marked[:n_x], marked[n_x:]
    got = [move(pieces[i], [(0, i * n_y)]) for i in range(1, n_x)]
    lines = [lines[0]] + [
        lax.ppermute(lines[i], "y", [(a, (a + i) % n_y) for a in range(n_y)]) for i in range(1, n_y)
    ]

    moved = choose(plane_kernel, owner_xy.reshape(1), moved, (n_z, 2 * moved.shape[1], HEAD_SIZE))
    moved, got = lax.optimization_barrier((moved, got))
    anchor = jnp.where(x == 0, pieces[0], got[0] + got[1] + got[2])
    got = [move(anchor, [(i * n_y, i * n_y + j) for i in range(n_x)]) for j in range(1, n_y)]
    moved = exchange(moved, "z")

    moved = choose(line_kernel, owner_z.reshape(1), moved, (n_x, 2 * moved.shape[1], HEAD_SIZE))
    moved, got, lines = lax.optimization_barrier((moved, got, lines))
    anchor = jnp.where(y == 0, anchor, got[0] + got[1] + got[2])
    plane = range(n_xy)
    got = [move(anchor, [(p, to * n_xy + p) for p in plane]) for to in (3, 5)]
    moved = exchange(moved, "x")

    partials = request_partials(moved, lines, own_rows)
    partials, got = lax.optimization_barrier((partials, got))
    anchor = jnp.where(z == 0, anchor, got[0] + got[1])
    steps = (((0, 1), (3, 4), (5, 6)), ((0, 7), (3, 2)))
    got = [move(anchor, [(a * n_xy + p, b * n_xy + p) for a, b in step for p in plane]) for step in steps]
    partials = exchange(partials, "x")

    planes = join([partials], n_z, 2, True)
    planes, got = lax.optimization_barrier((planes, got))
    anchor = jnp.where((z == 0) | (z == 3) | (z == 5), anchor, got[0] + got[1])
    anchors = [anchor]
    for i in range(1, n_x):
        anchors.append(lax.ppermute(anchor, "x", [(a, (a + i) % n_x) for a in range(n_x)]))
    planes = exchange(planes, "z")

    answer = exchange(join([planes], n_xy, 1, False), ("x", "y"))
    context_output = context_attention(own_len, is_root, q, k, v, anchors)
    answer = answer.reshape(n_x, n_y, -1, own_rows, HEAD_SIZE).transpose(3, 1, 0, 2, 4).reshape(own_rows, q.shape[1])
    request_output = jnp.where(mine, answer, jnp.zeros_like(answer))
    return context_output, request_output


def solution(mesh):
    n_z, n_x, n_y = 8, 4, 4
    grid = jax.sharding.Mesh(mesh.devices.reshape(n_z, n_x, n_y, 2), ("z", "x", "y", "head"))
    ctx = ("z", "x", "y")
    in_specs = (
        P(ctx, "head"),
        P(ctx, "head"),
        P(ctx, "head"),
        P(ctx),
        P(ctx + ("head",), None),
        P(ctx, "head"),
        P(ctx, "head"),
        P(),
    )
    out_specs = (P(ctx, "head"), P(ctx, "head"))
    return jax.shard_map(
        functools.partial(local, n_z, n_x, n_y),
        mesh=grid,
        in_specs=in_specs,
        out_specs=out_specs,
        check_vma=False,
    )
```

```python
import functools

import jax
import jax.numpy as jnp
from jax import lax
from jax.experimental import pallas as pl
from jax.experimental.pallas import tpu as pltpu
from jax.sharding import PartitionSpec as P

HEAD_SIZE = 128
GROUP = 8
SCALE = HEAD_SIZE**-0.5
LOG2E = 1.4426950408889634
LN2 = 0.6931471805599453
MARK = 1024.0
VMEM_LIMIT = 32 * 1024 * 1024


def dot_nt(a, b):
    return lax.dot_general(a, b, (((1,), (1,)), ((), ())), preferred_element_type=jnp.float32)


def dot_nn(a, b):
    return lax.dot_general(a, b, (((1,), (0,)), ((), ())), preferred_element_type=jnp.float32)


def context_kernel(count, len_ref, root_ref, q_ref, k_ref, v_ref, *refs):
    ak_refs, av_refs = refs[:count], refs[count : 2 * count]
    o_ref, vs_ref = refs[-2:]
    rows = k_ref.shape[0]
    half = rows // 2
    own_len = len_ref[0]
    root = root_ref[0] > 0
    ak = jnp.concatenate([ref[...] for ref in ak_refs], axis=0)
    ak = jnp.where(root, jnp.broadcast_to(k_ref[0:1, :], ak.shape), ak)
    av = jnp.concatenate([ref[...] for ref in av_refs], axis=0)
    hidden = (av > 100.0) | root
    vs_ref[0:rows, :HEAD_SIZE] = jnp.where(hidden, jnp.zeros_like(av), av)
    vs_ref[0:rows, HEAD_SIZE:] = jnp.where(hidden, jnp.zeros_like(av), jnp.ones_like(av))
    vs_ref[rows:, :HEAD_SIZE] = v_ref[...]
    vs_ref[rows:, HEAD_SIZE:] = jnp.ones((rows, HEAD_SIZE), jnp.bfloat16)
    c = SCALE * LOG2E
    row = lax.broadcasted_iota(jnp.int32, (2 * half, half), 0)
    col = lax.broadcasted_iota(jnp.int32, (2 * half, half), 1)
    causal = jnp.where(col <= lax.rem(row, half), 0.0, -jnp.inf).astype(jnp.float32)

    def lanes(g):
        return slice(g * HEAD_SIZE, (g + 1) * HEAD_SIZE)

    def scores(top, g):
        keys = top + half
        q = jnp.concatenate([q_ref[top:keys, lanes(g)], q_ref[top:keys, lanes(g + 1)]], axis=0)
        sa = dot_nt(q, ak)
        so = dot_nt(q, k_ref[0:keys, :])
        tiles = [sa[:, i : i + half] for i in range(0, rows, half)]
        tiles += [so[:, i : i + half] for i in range(0, top, half)]
        return tiles + [so[:, top:keys] + causal]

    def finish(top, g, tiles):
        keys = top + half
        live = (top + lax.broadcasted_iota(jnp.int32, (half, HEAD_SIZE), 0)) < own_len
        peak = jnp.max(functools.reduce(jnp.maximum, tiles), axis=1, keepdims=True)
        weights = [jnp.exp2((tile - peak) * c).astype(jnp.bfloat16) for tile in tiles]
        acc = dot_nn(jnp.concatenate(weights, axis=1), vs_ref[0 : rows + keys, :])
        total = acc[:, HEAD_SIZE:]
        inverse = pl.reciprocal(total, approx=True)
        inverse = inverse * (2.0 - total * inverse)
        out = acc[:, :HEAD_SIZE] * inverse
        for i in range(2):
            part = jnp.where(live, out[i * half : (i + 1) * half], 0.0)
            o_ref[top:keys, lanes(g + i)] = part.astype(jnp.bfloat16)

    work = [(top, g) for top in (0, half) for g in range(0, GROUP, 2)]
    tiles = scores(*work[0])
    for i, item in enumerate(work):
        later = scores(*work[i + 1]) if i + 1 < len(work) else None
        finish(*item, tiles)
        tiles = later


def context_attention(own_len, is_root, q, k, v, anchor):
    rows, width = q.shape
    heads = k.shape[1] // HEAD_SIZE
    wide = GROUP * HEAD_SIZE
    count = len(anchor)
    slab = anchor[0].shape[0]
    smem = pl.BlockSpec(memory_space=pltpu.SMEM)
    kv_spec = pl.BlockSpec((rows, HEAD_SIZE), lambda h: (0, h))
    wide_spec = pl.BlockSpec((rows, wide), lambda h: (0, h))
    specs = [smem, smem, wide_spec, kv_spec, kv_spec]
    specs += [pl.BlockSpec((slab, HEAD_SIZE), lambda h: (0, h))] * count
    specs += [pl.BlockSpec((slab, HEAD_SIZE), lambda h: (0, heads + h))] * count
    return pl.pallas_call(
        functools.partial(context_kernel, count),
        grid=(heads,),
        out_shape=jax.ShapeDtypeStruct((rows, width), jnp.bfloat16),
        in_specs=specs,
        out_specs=wide_spec,
        scratch_shapes=[pltpu.VMEM((2 * rows, 2 * HEAD_SIZE), jnp.bfloat16)],
        compiler_params=pltpu.CompilerParams(vmem_limit_bytes=VMEM_LIMIT),
        cost_estimate=pl.CostEstimate(
            flops=8 * rows * width * rows, bytes_accessed=5 * 2**20, transcendentals=2 * rows * rows * heads * GROUP
        ),
        name="context_attention",
    )(own_len, is_root, q, k, v, *anchor, *anchor)


def mark_kernel(n_x, len_ref, own_ref, y_ref, k_ref, v_ref, rk_ref, rv_ref, *o_refs):
    rows, width = k_ref.shape
    own = rk_ref.shape[0]
    slab = rows // n_x
    first = jnp.broadcast_to(k_ref[0:1, :], (slab, width))
    for i, o_ref in enumerate(o_refs[:n_x]):
        span = slice(i * slab, (i + 1) * slab)
        valid = (i * slab + lax.broadcasted_iota(jnp.int32, first.shape, 0)) < len_ref[0]
        o_ref[:, :width] = jnp.where(valid, k_ref[span, :], first)
        o_ref[:, width:] = jnp.where(valid, v_ref[span, :], jnp.full_like(first, MARK))
    lines = o_refs[n_x:]
    valid = lax.broadcasted_iota(jnp.int32, (rows, HEAD_SIZE), 0) < len_ref[0]
    is_owner = own_ref[0] > 0
    for i, o_ref in enumerate(lines):
        head = lax.rem(y_ref[0] + i, len(lines))
        lanes = pl.ds(pl.multiple_of(head * HEAD_SIZE, HEAD_SIZE), HEAD_SIZE)
        first = k_ref[0:1, lanes]
        o_ref[0:rows, :] = jnp.where(valid, k_ref[:, lanes], jnp.broadcast_to(first, valid.shape))
        o_ref[rows : rows + own, :] = jnp.where(
            is_owner, rk_ref[:, lanes], jnp.broadcast_to(first, (own, HEAD_SIZE))
        )
        mark = jnp.full((rows, HEAD_SIZE), MARK, jnp.bfloat16)
        o_ref[rows + own : 2 * rows + own, :] = jnp.where(valid, v_ref[:, lanes], mark)
        o_ref[2 * rows + own :, :] = jnp.where(is_owner, rv_ref[:, lanes], mark[0:own])


def mark(own_len, is_owner, y, k, v, rk, rv, n_x, n_y):
    rows, width = k.shape
    vmem = pl.BlockSpec(memory_space=pltpu.VMEM)
    smem = pl.BlockSpec(memory_space=pltpu.SMEM)
    shapes = [jax.ShapeDtypeStruct((rows // n_x, 2 * width), k.dtype)] * n_x
    shapes += [jax.ShapeDtypeStruct((2 * (rows + rk.shape[0]), HEAD_SIZE), k.dtype)] * n_y
    return pl.pallas_call(
        functools.partial(mark_kernel, n_x),
        out_shape=shapes,
        in_specs=[smem] * 3 + [vmem] * 4,
        out_specs=[vmem] * len(shapes),
        compiler_params=pltpu.CompilerParams(vmem_limit_bytes=56 * 1024 * 1024),
        cost_estimate=pl.CostEstimate(flops=2**18, bytes_accessed=2**21, transcendentals=0),
        name="mark",
    )(own_len, is_owner, y, k, v, rk, rv)


def pack_kernel(n_y, rq_ref, o_ref):
    own, width = rq_ref.shape
    targets = o_ref.shape[0] // 2
    some = o_ref.shape[1] // own
    for j in range(targets):
        x, y = j // n_y, j % n_y
        for c in range(2):
            for i in range(some):
                lane = c * (width // 2) + (GROUP * y + some * x + i) * HEAD_SIZE
                o_ref[2 * j + c, i * own : (i + 1) * own, :] = rq_ref[:, lane : lane + HEAD_SIZE]


def pack(rq, targets, n_y):
    vmem = pl.BlockSpec(memory_space=pltpu.VMEM)
    height = rq.size // (2 * targets * HEAD_SIZE)
    return pl.pallas_call(
        functools.partial(pack_kernel, n_y),
        out_shape=jax.ShapeDtypeStruct((2 * targets, height, HEAD_SIZE), jnp.bfloat16),
        in_specs=[vmem],
        out_specs=vmem,
        compiler_params=pltpu.CompilerParams(vmem_limit_bytes=56 * 1024 * 1024),
        cost_estimate=pl.CostEstimate(flops=2**18, bytes_accessed=2**19, transcendentals=0),
        name="pack",
    )(rq)


def plane_kernel(source_ref, x_ref, o_ref):
    own = 16
    source = 2 * source_ref[0]
    parts = []
    for i in range(x_ref.shape[1] // own):
        pick = slice(i * own, (i + 1) * own)
        parts += [x_ref[source, pick, :], x_ref[source + 1, pick, :]]
    part = jnp.concatenate(parts, axis=0)
    for z in range(o_ref.shape[0]):
        o_ref[z] = part


def line_kernel(plane_ref, x_ref, o_ref):
    o_ref[...] = x_ref[plane_ref[0]]


def choose(kernel, index, x, shape, flops):
    vmem = pl.BlockSpec(memory_space=pltpu.VMEM)
    return pl.pallas_call(
        kernel,
        out_shape=jax.ShapeDtypeStruct(shape, x.dtype),
        in_specs=[pl.BlockSpec(memory_space=pltpu.SMEM), vmem],
        out_specs=vmem,
        compiler_params=pltpu.CompilerParams(vmem_limit_bytes=VMEM_LIMIT),
        cost_estimate=pl.CostEstimate(flops=flops, bytes_accessed=2**19, transcendentals=0),
        name="choose",
    )(index, x)


def split3(x):
    high = x.astype(jnp.bfloat16).astype(jnp.float32)
    rest = x - high
    mid = rest.astype(jnp.bfloat16).astype(jnp.float32)
    low = (rest - mid).astype(jnp.bfloat16).astype(jnp.float32)
    return high, mid, low


def code_rows(pair, last, height):
    row = lax.broadcasted_iota(jnp.int32, (height, HEAD_SIZE), 0)
    return jnp.where(row == 0, pair, jnp.where(row == 1, last, 0.0)).astype(jnp.bfloat16)


def request_kernel(own, count, *refs):
    q_refs, lines = refs[:count], refs[count : -count - 1]
    o_refs, v_ref = refs[-count - 1 : -1], refs[-1]
    piece = q_refs[0].shape[0]
    n = count * piece
    both = lines[0].shape[0] // 2
    rows = both - own
    c = SCALE * LOG2E
    q = jnp.concatenate([ref[...] for ref in q_refs], axis=0)
    for i, ref in enumerate(lines):
        for part, (top, at) in (
            (ref[both : both + rows, :], (i * rows, rows)),
            (ref[both + rows :, :], (len(lines) * rows + i * own, own)),
        ):
            hidden = part > 100.0
            v_ref[top : top + at, :HEAD_SIZE] = jnp.where(hidden, jnp.zeros_like(part), part)
            v_ref[top : top + at, HEAD_SIZE:] = jnp.where(hidden, jnp.zeros_like(part), jnp.ones_like(part))
    own_keys = jnp.concatenate([ref[rows:both, :] for ref in lines], axis=0)
    row = lax.rem(lax.broadcasted_iota(jnp.int32, (n, own_keys.shape[0]), 0), own)
    col = lax.rem(lax.broadcasted_iota(jnp.int32, (n, own_keys.shape[0]), 1), own)
    scores = [dot_nt(q, ref[0:rows, :]) for ref in lines]
    scores.append(jnp.where(col <= row, dot_nt(q, own_keys), -jnp.inf))
    tiles = [s[:, i : i + HEAD_SIZE] for s in scores for i in range(0, s.shape[1], HEAD_SIZE)]
    peak = jnp.max(functools.reduce(jnp.maximum, tiles), axis=1, keepdims=True)
    weights = [jnp.exp2((tile - peak) * c).astype(jnp.bfloat16) for tile in tiles]
    acc = dot_nn(jnp.concatenate(weights, axis=1), v_ref[...])
    total = acc[:, HEAD_SIZE:]
    out = acc[:, :HEAD_SIZE] / total
    out_high = out.astype(jnp.bfloat16)
    out_low = (out - out_high.astype(jnp.float32)).astype(jnp.bfloat16)
    lse = peak * SCALE + jnp.log(total)
    high, mid, low = split3(lse)
    row = lax.broadcasted_iota(jnp.int32, (piece, HEAD_SIZE), 0)
    lane = lax.broadcasted_iota(jnp.int32, (piece, HEAD_SIZE), 1)
    for p, o_ref in enumerate(o_refs):
        part = slice(p * piece, (p + 1) * piece)
        pair = jnp.where(row == lane, high[part], jnp.where(row + piece == lane, mid[part], 0.0))
        last = jnp.where(row == lane, low[part], 0.0)
        o_ref[0:piece, :] = out_high[part]
        o_ref[piece : 2 * piece, :] = out_low[part]
        o_ref[2 * piece :, :] = code_rows(
            jnp.sum(pair, axis=0, keepdims=True), jnp.sum(last, axis=0, keepdims=True), 16
        )


def request_partials(queries, lines, own):
    count, piece = len(queries), queries[0].shape[0]
    keys = len(lines) * lines[0].shape[0] // 2
    vmem = pl.BlockSpec(memory_space=pltpu.VMEM)
    return pl.pallas_call(
        functools.partial(request_kernel, own, count),
        out_shape=[jax.ShapeDtypeStruct((2 * piece + 16, HEAD_SIZE), jnp.bfloat16)] * count,
        in_specs=[vmem] * (count + len(lines)),
        out_specs=[vmem] * count,
        scratch_shapes=[pltpu.VMEM((keys, 2 * HEAD_SIZE), jnp.bfloat16)],
        compiler_params=pltpu.CompilerParams(vmem_limit_bytes=VMEM_LIMIT),
        cost_estimate=pl.CostEstimate(
            flops=3 * 10**9, bytes_accessed=2**20, transcendentals=count * piece * keys
        ),
        name="request_partials",
    )(*queries, *lines)


def join_kernel(parts_in, keep_code, *refs):
    x_refs, o_ref = refs[:-1], refs[-1]
    if len(x_refs) == 1:
        x_refs = [x_refs[0].at[i] for i in range(x_refs[0].shape[0])]
    height = x_refs[0].shape[0]
    top = height - 16
    piece = top // parts_in
    count = max(len(x_refs), 8)
    row = lax.broadcasted_iota(jnp.int32, (count, HEAD_SIZE), 0)
    lane = lax.broadcasted_iota(jnp.int32, (count, HEAD_SIZE), 1)
    pair = jnp.zeros((count, HEAD_SIZE), jnp.float32)
    last = jnp.zeros((count, HEAD_SIZE), jnp.float32)
    for i, ref in enumerate(x_refs):
        code = ref[top:height, :].astype(jnp.float32)
        pair = jnp.where(row == i, code[0:1, :], pair)
        last = jnp.where(row == i, code[1:2, :], last)
    lse = jnp.where(lane < piece, pair + pltpu.roll(pair, piece, 1) + last, 0.0)
    lse = jnp.where(row < len(x_refs), lse, -jnp.inf)
    peak = jnp.max(lse, axis=0, keepdims=True)
    weight = jnp.exp(lse - peak)
    total = jnp.sum(weight, axis=0, keepdims=True)
    column = jnp.transpose(weight / total)
    out = jnp.zeros((piece, HEAD_SIZE), jnp.float32)
    for i, ref in enumerate(x_refs):
        part = ref[0:piece, :].astype(jnp.float32)
        if parts_in > 1:
            part = part + ref[piece:top, :].astype(jnp.float32)
        out = out + column[0:piece, i : i + 1] * part
    parts = [out.astype(jnp.bfloat16)]
    if keep_code:
        high, mid, low = split3(peak + jnp.log(total))
        pair = jnp.where(lane[0:1] < piece, high, pltpu.roll(mid, piece, 1))
        parts.append(code_rows(pair, low, 16))
    part = jnp.concatenate(parts, axis=0)
    if len(o_ref.shape) == 2:
        o_ref[...] = part
    else:
        for i in range(o_ref.shape[0]):
            o_ref[i] = part


def join(arrays, copies, parts_in, keep_code):
    height = (arrays[0].shape[-2] - 16) // parts_in + (16 if keep_code else 0)
    shape = (copies, height, HEAD_SIZE) if copies else (height, HEAD_SIZE)
    return pl.pallas_call(
        functools.partial(join_kernel, parts_in, keep_code),
        out_shape=jax.ShapeDtypeStruct(shape, jnp.bfloat16),
        compiler_params=pltpu.CompilerParams(vmem_limit_bytes=VMEM_LIMIT),
        cost_estimate=pl.CostEstimate(flops=3 * 10**9, bytes_accessed=2**19, transcendentals=1024),
        name="join_pieces",
    )(*arrays)


def exchange(x, axis):
    return lax.all_to_all(x, axis, split_axis=0, concat_axis=0, tiled=True)


def local(n_z, n_x, n_y, q, k, v, block_lengths, rq, rk, rv, query_owner):
    n_xy = n_x * n_y
    z, x, y = (lax.axis_index(name) for name in ("z", "x", "y"))
    owner = query_owner[0]
    owner_z, owner_xy = owner // n_xy, owner % n_xy
    own_len = block_lengths
    mine = (z == owner_z) & (x * n_y + y == owner_xy)
    is_owner = mine.astype(jnp.int32).reshape(1)
    is_root = ((z == 0) & (x == 0) & (y == 0)).astype(jnp.int32).reshape(1)
    own_rows = rk.shape[0]

    def move(value, pairs):
        return lax.ppermute(value, ("z", "x", "y"), pairs)

    def shift_x(value, count):
        return lax.ppermute(value, "x", [(a, (a + count) % n_x) for a in range(n_x)])

    moved = exchange(pack(rq, n_xy, n_y), ("x", "y", "head"))
    marked = mark(own_len, is_owner, y.reshape(1), k, v, rk, rv, n_x, n_y)
    pieces, lines = marked[:n_x], marked[n_x:]
    got = [move(pieces[i], [(0, i * n_y)]) for i in range(1, n_x)]
    lines = [lines[0]] + [
        lax.ppermute(lines[i], "y", [(a, (a + i) % n_y) for a in range(n_y)]) for i in range(1, n_y)
    ]

    moved = choose(plane_kernel, owner_xy.reshape(1), moved, (n_z, 2 * moved.shape[1], HEAD_SIZE), 8 * 10**8)
    moved, got = lax.optimization_barrier((moved, got))
    anchor = jnp.where(x == 0, pieces[0], got[0] + got[1] + got[2])
    got = [move(anchor, [(i * n_y, i * n_y + j) for i in range(n_x)]) for j in range(1, n_y)]
    moved = exchange(moved, "z")

    moved = choose(line_kernel, owner_z.reshape(1), moved, moved.shape[1:], 3 * 10**9)
    moved, got, lines = lax.optimization_barrier((moved, got, lines))
    anchor = jnp.where(y == 0, anchor, got[0] + got[1] + got[2])
    plane = range(n_xy)
    got = [move(anchor, [(p, to * n_xy + p) for p in plane]) for to in (3, 5)]
    queries = [moved] + [shift_x(moved, i) for i in range(1, n_x)]

    partials = request_partials(queries, lines, own_rows)
    anchor = jnp.where(z == 0, anchor, got[0] + got[1])
    steps = (((0, 1), (3, 4), (5, 6)), ((0, 7), (3, 2)))
    got = [move(anchor, [(a * n_xy + p, b * n_xy + p) for a, b in step for p in plane]) for step in steps]
    partials = [partials[0]] + [shift_x(partials[i], n_x - i) for i in range(1, n_x)]

    planes = join(partials, n_z, 2, True)
    anchor = jnp.where((z == 0) | (z == 3) | (z == 5), anchor, got[0] + got[1])
    anchors = [anchor]
    for i in range(1, n_x):
        anchors.append(shift_x(anchor, i))
    planes = exchange(planes, "z")

    answer = exchange(join([planes], n_xy, 1, False), ("x", "y"))
    context_output = context_attention(own_len, is_root, q, k, v, anchors)
    answer = answer.reshape(n_x, n_y, -1, own_rows, HEAD_SIZE).transpose(3, 1, 0, 2, 4).reshape(own_rows, q.shape[1])
    request_output = jnp.where(mine, answer, jnp.zeros_like(answer))
    return context_output, request_output


def solution(mesh):
    n_z, n_x, n_y = 8, 4, 4
    grid = jax.sharding.Mesh(mesh.devices.reshape(n_z, n_x, n_y, 2), ("z", "x", "y", "head"))
    ctx = ("z", "x", "y")
    in_specs = (
        P(ctx, "head"),
        P(ctx, "head"),
        P(ctx, "head"),
        P(ctx),
        P(ctx + ("head",), None),
        P(ctx, "head"),
        P(ctx, "head"),
        P(),
    )
    out_specs = (P(ctx, "head"), P(ctx, "head"))
    return jax.shard_map(
        functools.partial(local, n_z, n_x, n_y),
        mesh=grid,
        in_specs=in_specs,
        out_specs=out_specs,
        check_vma=False,
    )
```

```python
import functools

import jax
import jax.numpy as jnp
from jax import lax
from jax.experimental import pallas as pl
from jax.experimental.pallas import tpu as pltpu
from jax.sharding import PartitionSpec as P

HEAD_SIZE = 128
GROUP = 8
SCALE = HEAD_SIZE**-0.5
LOG2E = 1.4426950408889634
LN2 = 0.6931471805599453
MARK = 1024.0
VMEM_LIMIT = 32 * 1024 * 1024


def dot_nt(a, b):
    return lax.dot_general(a, b, (((1,), (1,)), ((), ())), preferred_element_type=jnp.float32)


def dot_nn(a, b):
    return lax.dot_general(a, b, (((1,), (0,)), ((), ())), preferred_element_type=jnp.float32)


def context_kernel(count, len_ref, root_ref, q_ref, k_ref, v_ref, *refs):
    ak_refs, av_refs = refs[:count], refs[count : 2 * count]
    o_ref, vs_ref = refs[-2:]
    rows = k_ref.shape[0]
    half = rows // 2
    own_len = len_ref[0]
    root = root_ref[0] > 0
    ak = jnp.concatenate([ref[...] for ref in ak_refs], axis=0)
    ak = jnp.where(root, jnp.broadcast_to(k_ref[0:1, :], ak.shape), ak)
    av = jnp.concatenate([ref[...] for ref in av_refs], axis=0)
    hidden = (av > 100.0) | root
    vs_ref[0:rows, :HEAD_SIZE] = jnp.where(hidden, jnp.zeros_like(av), av)
    vs_ref[0:rows, HEAD_SIZE:] = jnp.where(hidden, jnp.zeros_like(av), jnp.ones_like(av))
    vs_ref[rows:, :HEAD_SIZE] = v_ref[...]
    vs_ref[rows:, HEAD_SIZE:] = jnp.ones((rows, HEAD_SIZE), jnp.bfloat16)
    c = SCALE * LOG2E
    row = lax.broadcasted_iota(jnp.int32, (2 * half, half), 0)
    col = lax.broadcasted_iota(jnp.int32, (2 * half, half), 1)
    causal = jnp.where(col <= lax.rem(row, half), 0.0, -jnp.inf).astype(jnp.float32)

    def lanes(g):
        return slice(g * HEAD_SIZE, (g + 1) * HEAD_SIZE)

    def scores(top, g):
        keys = top + half
        q = jnp.concatenate([q_ref[top:keys, lanes(g)], q_ref[top:keys, lanes(g + 1)]], axis=0)
        sa = dot_nt(q, ak)
        so = dot_nt(q, k_ref[0:keys, :])
        tiles = [sa[:, i : i + half] for i in range(0, rows, half)]
        tiles += [so[:, i : i + half] for i in range(0, top, half)]
        return tiles + [so[:, top:keys] + causal]

    def finish(top, g, tiles):
        keys = top + half
        live = (top + lax.broadcasted_iota(jnp.int32, (half, HEAD_SIZE), 0)) < own_len
        peak = jnp.max(functools.reduce(jnp.maximum, tiles), axis=1, keepdims=True)
        weights = [jnp.exp2((tile - peak) * c).astype(jnp.bfloat16) for tile in tiles]
        acc = dot_nn(jnp.concatenate(weights, axis=1), vs_ref[0 : rows + keys, :])
        total = acc[:, HEAD_SIZE:]
        inverse = pl.reciprocal(total, approx=True)
        inverse = inverse * (2.0 - total * inverse)
        out = acc[:, :HEAD_SIZE] * inverse
        for i in range(2):
            part = jnp.where(live, out[i * half : (i + 1) * half], 0.0)
            o_ref[top:keys, lanes(g + i)] = part.astype(jnp.bfloat16)

    work = [(top, g) for top in (0, half) for g in range(0, GROUP, 2)]
    tiles = scores(*work[0])
    for i, item in enumerate(work):
        later = scores(*work[i + 1]) if i + 1 < len(work) else None
        finish(*item, tiles)
        tiles = later


def context_attention(own_len, is_root, q, k, v, anchor):
    rows, width = q.shape
    heads = k.shape[1] // HEAD_SIZE
    wide = GROUP * HEAD_SIZE
    count = len(anchor)
    slab = anchor[0].shape[0]
    smem = pl.BlockSpec(memory_space=pltpu.SMEM)
    kv_spec = pl.BlockSpec((rows, HEAD_SIZE), lambda h: (0, h))
    wide_spec = pl.BlockSpec((rows, wide), lambda h: (0, h))
    specs = [smem, smem, wide_spec, kv_spec, kv_spec]
    specs += [pl.BlockSpec((slab, HEAD_SIZE), lambda h: (0, h))] * count
    specs += [pl.BlockSpec((slab, HEAD_SIZE), lambda h: (0, heads + h))] * count
    return pl.pallas_call(
        functools.partial(context_kernel, count),
        grid=(heads,),
        out_shape=jax.ShapeDtypeStruct((rows, width), jnp.bfloat16),
        in_specs=specs,
        out_specs=wide_spec,
        scratch_shapes=[pltpu.VMEM((2 * rows, 2 * HEAD_SIZE), jnp.bfloat16)],
        compiler_params=pltpu.CompilerParams(vmem_limit_bytes=VMEM_LIMIT),
        cost_estimate=pl.CostEstimate(
            flops=8 * rows * width * rows, bytes_accessed=5 * 2**20, transcendentals=2 * rows * rows * heads * GROUP
        ),
        name="context_attention",
    )(own_len, is_root, q, k, v, *anchor, *anchor)


def mark_kernel(n_x, len_ref, own_ref, y_ref, k_ref, v_ref, rk_ref, rv_ref, *o_refs):
    rows, width = k_ref.shape
    own = rk_ref.shape[0]
    slab = rows // n_x
    first = jnp.broadcast_to(k_ref[0:1, :], (slab, width))
    for i, o_ref in enumerate(o_refs[:n_x]):
        span = slice(i * slab, (i + 1) * slab)
        valid = (i * slab + lax.broadcasted_iota(jnp.int32, first.shape, 0)) < len_ref[0]
        o_ref[:, :width] = jnp.where(valid, k_ref[span, :], first)
        o_ref[:, width:] = jnp.where(valid, v_ref[span, :], jnp.full_like(first, MARK))
    lines = o_refs[n_x:]
    valid = lax.broadcasted_iota(jnp.int32, (rows, HEAD_SIZE), 0) < len_ref[0]
    is_owner = own_ref[0] > 0
    for i, o_ref in enumerate(lines):
        head = lax.rem(y_ref[0] + i, len(lines))
        lanes = pl.ds(pl.multiple_of(head * HEAD_SIZE, HEAD_SIZE), HEAD_SIZE)
        first = k_ref[0:1, lanes]
        o_ref[0:rows, :] = jnp.where(valid, k_ref[:, lanes], jnp.broadcast_to(first, valid.shape))
        o_ref[rows : rows + own, :] = jnp.where(
            is_owner, rk_ref[:, lanes], jnp.broadcast_to(first, (own, HEAD_SIZE))
        )
        mark = jnp.full((rows, HEAD_SIZE), MARK, jnp.bfloat16)
        o_ref[rows + own : 2 * rows + own, :] = jnp.where(valid, v_ref[:, lanes], mark)
        o_ref[2 * rows + own :, :] = jnp.where(is_owner, rv_ref[:, lanes], mark[0:own])


def pack_kernel(n_y, rq_ref, o_ref):
    own, width = rq_ref.shape
    targets = o_ref.shape[0] // 2
    some = o_ref.shape[1] // own
    for j in range(targets):
        x, y = j // n_y, j % n_y
        for c in range(2):
            for i in range(some):
                lane = c * (width // 2) + (GROUP * y + some * x + i) * HEAD_SIZE
                o_ref[2 * j + c, i * own : (i + 1) * own, :] = rq_ref[:, lane : lane + HEAD_SIZE]


def prepare_kernel(n_x, n_y, len_ref, own_ref, y_ref, rq_ref, k_ref, v_ref, rk_ref, rv_ref, sent_ref, *o_refs):
    pack_kernel(n_y, rq_ref, sent_ref)
    mark_kernel(n_x, len_ref, own_ref, y_ref, k_ref, v_ref, rk_ref, rv_ref, *o_refs)


def prepare(own_len, is_owner, y, rq, k, v, rk, rv, n_x, n_y):
    rows, width = k.shape
    vmem = pl.BlockSpec(memory_space=pltpu.VMEM)
    smem = pl.BlockSpec(memory_space=pltpu.SMEM)
    targets = 2 * n_x * n_y
    shapes = [jax.ShapeDtypeStruct((targets, rq.size // (targets * HEAD_SIZE), HEAD_SIZE), k.dtype)]
    shapes += [jax.ShapeDtypeStruct((rows // n_x, 2 * width), k.dtype)] * n_x
    shapes += [jax.ShapeDtypeStruct((2 * (rows + rk.shape[0]), HEAD_SIZE), k.dtype)] * n_y
    out = pl.pallas_call(
        functools.partial(prepare_kernel, n_x, n_y),
        out_shape=shapes,
        in_specs=[smem] * 3 + [vmem] * 5,
        out_specs=[vmem] * len(shapes),
        compiler_params=pltpu.CompilerParams(vmem_limit_bytes=56 * 1024 * 1024),
        cost_estimate=pl.CostEstimate(flops=2**18, bytes_accessed=5 * 2**19, transcendentals=0),
        name="prepare",
    )(own_len, is_owner, y, rq, k, v, rk, rv)
    return out[0], out[1 : 1 + n_x], out[1 + n_x :]


def plane_kernel(source_ref, x_ref, o_ref):
    own = 16
    source = 2 * source_ref[0]
    parts = []
    for i in range(x_ref.shape[1] // own):
        pick = slice(i * own, (i + 1) * own)
        parts += [x_ref[source, pick, :], x_ref[source + 1, pick, :]]
    part = jnp.concatenate(parts, axis=0)
    for z in range(o_ref.shape[0]):
        o_ref[z] = part


def line_kernel(plane_ref, x_ref, o_ref):
    o_ref[...] = x_ref[plane_ref[0], 0 : o_ref.shape[0], :]


def choose(kernel, index, x, shape, flops):
    vmem = pl.BlockSpec(memory_space=pltpu.VMEM)
    return pl.pallas_call(
        kernel,
        out_shape=jax.ShapeDtypeStruct(shape, x.dtype),
        in_specs=[pl.BlockSpec(memory_space=pltpu.SMEM), vmem],
        out_specs=vmem,
        compiler_params=pltpu.CompilerParams(vmem_limit_bytes=VMEM_LIMIT),
        cost_estimate=pl.CostEstimate(flops=flops, bytes_accessed=2**19, transcendentals=0),
        name="choose",
    )(index, x)


def split3(x):
    high = x.astype(jnp.bfloat16).astype(jnp.float32)
    rest = x - high
    mid = rest.astype(jnp.bfloat16).astype(jnp.float32)
    low = (rest - mid).astype(jnp.bfloat16).astype(jnp.float32)
    return high, mid, low


def code_rows(pair, last, height):
    row = lax.broadcasted_iota(jnp.int32, (height, HEAD_SIZE), 0)
    return jnp.where(row == 0, pair, jnp.where(row == 1, last, 0.0)).astype(jnp.bfloat16)


def request_kernel(own, count, *refs):
    q_refs, lines = refs[:count], refs[count : -count - 1]
    o_refs, v_ref = refs[-count - 1 : -1], refs[-1]
    piece = q_refs[0].shape[0]
    n = count * piece
    both = lines[0].shape[0] // 2
    rows = both - own
    c = SCALE * LOG2E
    q = jnp.concatenate([ref[...] for ref in q_refs], axis=0)
    for i, ref in enumerate(lines):
        for part, (top, at) in (
            (ref[both : both + rows, :], (i * rows, rows)),
            (ref[both + rows :, :], (len(lines) * rows + i * own, own)),
        ):
            hidden = part > 100.0
            v_ref[top : top + at, :HEAD_SIZE] = jnp.where(hidden, jnp.zeros_like(part), part)
            v_ref[top : top + at, HEAD_SIZE:] = jnp.where(hidden, jnp.zeros_like(part), jnp.ones_like(part))
    own_keys = jnp.concatenate([ref[rows:both, :] for ref in lines], axis=0)
    row = lax.rem(lax.broadcasted_iota(jnp.int32, (n, own_keys.shape[0]), 0), own)
    col = lax.rem(lax.broadcasted_iota(jnp.int32, (n, own_keys.shape[0]), 1), own)
    scores = [dot_nt(q, ref[0:rows, :]) for ref in lines]
    scores.append(jnp.where(col <= row, dot_nt(q, own_keys), -jnp.inf))
    tiles = [s[:, i : i + HEAD_SIZE] for s in scores for i in range(0, s.shape[1], HEAD_SIZE)]
    peak = jnp.max(functools.reduce(jnp.maximum, tiles), axis=1, keepdims=True)
    weights = [jnp.exp2((tile - peak) * c).astype(jnp.bfloat16) for tile in tiles]
    acc = dot_nn(jnp.concatenate(weights, axis=1), v_ref[...])
    total = acc[:, HEAD_SIZE:]
    out = acc[:, :HEAD_SIZE] / total
    out_high = out.astype(jnp.bfloat16)
    out_low = (out - out_high.astype(jnp.float32)).astype(jnp.bfloat16)
    lse = peak * SCALE + jnp.log(total)
    high, mid, low = split3(lse)
    row = lax.broadcasted_iota(jnp.int32, (piece, HEAD_SIZE), 0)
    lane = lax.broadcasted_iota(jnp.int32, (piece, HEAD_SIZE), 1)
    for p, o_ref in enumerate(o_refs):
        part = slice(p * piece, (p + 1) * piece)
        pair = jnp.where(row == lane, high[part], jnp.where(row + piece == lane, mid[part], 0.0))
        last = jnp.where(row == lane, low[part], 0.0)
        o_ref[0:piece, :] = out_high[part]
        o_ref[piece : 2 * piece, :] = out_low[part]
        o_ref[2 * piece :, :] = code_rows(
            jnp.sum(pair, axis=0, keepdims=True), jnp.sum(last, axis=0, keepdims=True), 16
        )


def request_partials(queries, lines, own):
    count, piece = len(queries), queries[0].shape[0]
    keys = len(lines) * lines[0].shape[0] // 2
    vmem = pl.BlockSpec(memory_space=pltpu.VMEM)
    return pl.pallas_call(
        functools.partial(request_kernel, own, count),
        out_shape=[jax.ShapeDtypeStruct((2 * piece + 16, HEAD_SIZE), jnp.bfloat16)] * count,
        in_specs=[vmem] * (count + len(lines)),
        out_specs=[vmem] * count,
        scratch_shapes=[pltpu.VMEM((keys, 2 * HEAD_SIZE), jnp.bfloat16)],
        compiler_params=pltpu.CompilerParams(vmem_limit_bytes=VMEM_LIMIT),
        cost_estimate=pl.CostEstimate(
            flops=3 * 10**9, bytes_accessed=2**20, transcendentals=count * piece * keys
        ),
        name="request_partials",
    )(*queries, *lines)


def join_kernel(parts_in, keep_code, *refs):
    x_refs, o_ref = refs[:-1], refs[-1]
    if len(x_refs) == 1:
        x_refs = [x_refs[0].at[i] for i in range(x_refs[0].shape[0])]
    height = x_refs[0].shape[0]
    top = height - 16
    piece = top // parts_in
    count = max(len(x_refs), 8)
    row = lax.broadcasted_iota(jnp.int32, (count, HEAD_SIZE), 0)
    lane = lax.broadcasted_iota(jnp.int32, (count, HEAD_SIZE), 1)
    pair = jnp.zeros((count, HEAD_SIZE), jnp.float32)
    last = jnp.zeros((count, HEAD_SIZE), jnp.float32)
    for i, ref in enumerate(x_refs):
        code = ref[top:height, :].astype(jnp.float32)
        pair = jnp.where(row == i, code[0:1, :], pair)
        last = jnp.where(row == i, code[1:2, :], last)
    lse = jnp.where(lane < piece, pair + pltpu.roll(pair, piece, 1) + last, 0.0)
    lse = jnp.where(row < len(x_refs), lse, -jnp.inf)
    peak = jnp.max(lse, axis=0, keepdims=True)
    weight = jnp.exp(lse - peak)
    total = jnp.sum(weight, axis=0, keepdims=True)
    column = jnp.transpose(weight / total)
    out = jnp.zeros((piece, HEAD_SIZE), jnp.float32)
    for i, ref in enumerate(x_refs):
        part = ref[0:piece, :].astype(jnp.float32)
        if parts_in > 1:
            part = part + ref[piece:top, :].astype(jnp.float32)
        out = out + column[0:piece, i : i + 1] * part
    parts = [out.astype(jnp.bfloat16)]
    if keep_code:
        high, mid, low = split3(peak + jnp.log(total))
        pair = jnp.where(lane[0:1] < piece, high, pltpu.roll(mid, piece, 1))
        parts.append(code_rows(pair, low, 16))
    part = jnp.concatenate(parts, axis=0)
    if len(o_ref.shape) == 2:
        o_ref[...] = part
    else:
        for i in range(o_ref.shape[0]):
            o_ref[i] = part


def join(arrays, copies, parts_in, keep_code):
    height = (arrays[0].shape[-2] - 16) // parts_in + (16 if keep_code else 0)
    shape = (copies, height, HEAD_SIZE) if copies else (height, HEAD_SIZE)
    return pl.pallas_call(
        functools.partial(join_kernel, parts_in, keep_code),
        out_shape=jax.ShapeDtypeStruct(shape, jnp.bfloat16),
        compiler_params=pltpu.CompilerParams(vmem_limit_bytes=VMEM_LIMIT),
        cost_estimate=pl.CostEstimate(flops=3 * 10**9, bytes_accessed=2**19, transcendentals=1024),
        name="join_pieces",
    )(*arrays)


def exchange(x, axis, groups=None):
    return lax.all_to_all(x, axis, split_axis=0, concat_axis=0, axis_index_groups=groups, tiled=True)


def local(n_z, n_x, n_y, q, k, v, block_lengths, rq, rk, rv, query_owner):
    n_xy = n_x * n_y
    z, x, y = (lax.axis_index(name) for name in ("z", "x", "y"))
    owner = query_owner[0]
    owner_z, owner_xy = owner // n_xy, owner % n_xy
    own_len = block_lengths
    mine = (z == owner_z) & (x * n_y + y == owner_xy)
    is_owner = mine.astype(jnp.int32).reshape(1)
    is_root = ((z == 0) & (x == 0) & (y == 0)).astype(jnp.int32).reshape(1)
    own_rows = rk.shape[0]
    down = [list(range(n_z))[::-1]]

    def move(value, pairs):
        return lax.ppermute(value, ("z", "x", "y"), pairs)

    def shift_x(value, count):
        return lax.ppermute(value, "x", [(a, (a + count) % n_x) for a in range(n_x)])

    sent, pieces, lines = prepare(own_len, is_owner, y.reshape(1), rq, k, v, rk, rv, n_x, n_y)
    moved = exchange(sent, ("x", "y", "head"))
    got = [move(pieces[i], [(0, i * n_y)]) for i in range(1, n_x)]
    lines = [lines[0]] + [
        lax.ppermute(lines[i], "y", [(a, (a + i) % n_y) for a in range(n_y)]) for i in range(1, n_y)
    ]

    piece = (2 * moved.shape[1], HEAD_SIZE)
    moved = choose(plane_kernel, owner_xy.reshape(1), moved, (n_z,) + piece, 8 * 10**8)
    moved, got = lax.optimization_barrier((moved, got))
    anchor = jnp.where(x == 0, pieces[0], got[0] + got[1] + got[2])
    got = [move(anchor, [(i * n_y, i * n_y + j) for i in range(n_x)]) for j in range(1, n_y)]
    moved = exchange(moved, "z", down)

    moved = choose(line_kernel, (n_z - 1 - owner_z).reshape(1), moved, piece, 3 * 10**9)
    moved, got, lines = lax.optimization_barrier((moved, got, lines))
    anchor = jnp.where(y == 0, anchor, got[0] + got[1] + got[2])
    plane = range(n_xy)
    got = [move(anchor, [(p, to * n_xy + p) for p in plane]) for to in (3, 5)]
    queries = [moved] + [shift_x(moved, i) for i in range(1, n_x)]

    partials = request_partials(queries, lines, own_rows)
    anchor = jnp.where(z == 0, anchor, got[0] + got[1])
    steps = (((0, 1), (3, 4), (5, 6)), ((0, 7), (3, 2)))
    got = [move(anchor, [(a * n_xy + p, b * n_xy + p) for a, b in step for p in plane]) for step in steps]
    partials = [partials[0]] + [shift_x(partials[i], n_x - i) for i in range(1, n_x)]

    planes = join(partials, n_z, 2, True)
    anchor = jnp.where((z == 0) | (z == 3) | (z == 5), anchor, got[0] + got[1])
    anchors = [anchor]
    for i in range(1, n_x):
        anchors.append(shift_x(anchor, i))
    planes = exchange(planes, "z", down)

    answer = exchange(join([planes], n_xy, 1, False), ("x", "y"))
    context_output = context_attention(own_len, is_root, q, k, v, anchors)
    answer = answer.reshape(n_x, n_y, -1, own_rows, HEAD_SIZE).transpose(3, 1, 0, 2, 4).reshape(own_rows, q.shape[1])
    request_output = jnp.where(mine, answer, jnp.zeros_like(answer))
    return context_output, request_output


def solution(mesh):
    n_z, n_x, n_y = 8, 4, 4
    grid = jax.sharding.Mesh(mesh.devices.reshape(n_z, n_x, n_y, 2), ("z", "x", "y", "head"))
    ctx = ("z", "x", "y")
    in_specs = (
        P(ctx, "head"),
        P(ctx, "head"),
        P(ctx, "head"),
        P(ctx),
        P(ctx + ("head",), None),
        P(ctx, "head"),
        P(ctx, "head"),
        P(),
    )
    out_specs = (P(ctx, "head"), P(ctx, "head"))
    return jax.shard_map(
        functools.partial(local, n_z, n_x, n_y),
        mesh=grid,
        in_specs=in_specs,
        out_specs=out_specs,
        check_vma=False,
    )
```

```python
import functools

import jax
import jax.numpy as jnp
from jax import lax
from jax.experimental import pallas as pl
from jax.experimental.pallas import tpu as pltpu
from jax.sharding import PartitionSpec as P

HEAD_SIZE = 128
GROUP = 8
SCALE = HEAD_SIZE**-0.5
LOG2E = 1.4426950408889634
LN2 = 0.6931471805599453
MARK = 1024.0
VMEM_LIMIT = 32 * 1024 * 1024
STACK = 8
N_X, N_Y = 4, 4


def place():
    return (lax.axis_index("z") * N_X + lax.axis_index("x")) * N_Y + lax.axis_index("y")


def dot_nt(a, b):
    return lax.dot_general(a, b, (((1,), (1,)), ((), ())), preferred_element_type=jnp.float32)


def dot_nn(a, b):
    return lax.dot_general(a, b, (((1,), (0,)), ((), ())), preferred_element_type=jnp.float32)


def context_kernel(count, len_ref, q_ref, k_ref, v_ref, *refs):
    ak_refs, av_refs = refs[:count], refs[count : 2 * count]
    o_ref, zero_ref, vs_ref = refs[-3:]
    zero_ref[...] = jnp.zeros_like(zero_ref)
    rows = k_ref.shape[0]
    half = rows // 2
    own_len = len_ref[0]
    root = place() == 0
    ak = jnp.concatenate([ref[...] for ref in ak_refs], axis=0)
    ak = jnp.where(root, jnp.broadcast_to(k_ref[0:1, :], ak.shape), ak)
    av = jnp.concatenate([ref[...] for ref in av_refs], axis=0)
    hidden = (av > 100.0) | root
    vs_ref[0:rows, :HEAD_SIZE] = jnp.where(hidden, jnp.zeros_like(av), av)
    vs_ref[0:rows, HEAD_SIZE:] = jnp.where(hidden, jnp.zeros_like(av), jnp.ones_like(av))
    vs_ref[rows:, :HEAD_SIZE] = v_ref[...]
    vs_ref[rows:, HEAD_SIZE:] = jnp.ones((rows, HEAD_SIZE), jnp.bfloat16)
    c = SCALE * LOG2E
    row = lax.broadcasted_iota(jnp.int32, (STACK * half, half), 0)
    col = lax.broadcasted_iota(jnp.int32, (STACK * half, half), 1)
    causal = jnp.where(col <= lax.rem(row, half), 0.0, -jnp.inf).astype(jnp.float32)

    def lanes(g):
        return slice(g * HEAD_SIZE, (g + 1) * HEAD_SIZE)

    def scores(top, g):
        keys = top + half
        q = jnp.concatenate([q_ref[top:keys, lanes(g + i)] for i in range(STACK)], axis=0)
        sa = dot_nt(q, ak)
        so = dot_nt(q, k_ref[0:keys, :])
        tiles = [sa[:, i : i + half] for i in range(0, rows, half)]
        tiles += [so[:, i : i + half] for i in range(0, top, half)]
        return tiles + [so[:, top:keys] + causal]

    def finish(top, g, tiles):
        keys = top + half
        live = (top + lax.broadcasted_iota(jnp.int32, (half, HEAD_SIZE), 0)) < own_len
        peak = jnp.max(functools.reduce(jnp.maximum, tiles), axis=1, keepdims=True)
        weights = [jnp.exp2((tile - peak) * c).astype(jnp.bfloat16) for tile in tiles]
        acc = dot_nn(jnp.concatenate(weights, axis=1), vs_ref[0 : rows + keys, :])
        total = acc[:, HEAD_SIZE:]
        inverse = pl.reciprocal(total, approx=True)
        inverse = inverse * (2.0 - total * inverse)
        out = acc[:, :HEAD_SIZE] * inverse
        for i in range(STACK):
            part = jnp.where(live, out[i * half : (i + 1) * half], 0.0)
            o_ref[top:keys, lanes(g + i)] = part.astype(jnp.bfloat16)

    work = [(top, g) for top in (0, half) for g in range(0, GROUP, STACK)]
    tiles = scores(*work[0])
    for i, item in enumerate(work):
        later = scores(*work[i + 1]) if i + 1 < len(work) else None
        finish(*item, tiles)
        tiles = later


def context_attention(own_len, q, k, v, anchor, own_rows):
    rows, width = q.shape
    heads = k.shape[1] // HEAD_SIZE
    wide = GROUP * HEAD_SIZE
    count = len(anchor)
    slab = anchor[0].shape[0]
    smem = pl.BlockSpec(memory_space=pltpu.SMEM)
    kv_spec = pl.BlockSpec((rows, HEAD_SIZE), lambda h: (0, h))
    wide_spec = pl.BlockSpec((rows, wide), lambda h: (0, h))
    specs = [smem, wide_spec, kv_spec, kv_spec]
    specs += [pl.BlockSpec((slab, HEAD_SIZE), lambda h: (0, h))] * count
    specs += [pl.BlockSpec((slab, HEAD_SIZE), lambda h: (0, heads + h))] * count
    return pl.pallas_call(
        functools.partial(context_kernel, count),
        grid=(heads,),
        out_shape=[
            jax.ShapeDtypeStruct((rows, width), jnp.bfloat16),
            jax.ShapeDtypeStruct((own_rows, width), jnp.bfloat16),
        ],
        in_specs=specs,
        out_specs=[wide_spec, pl.BlockSpec((own_rows, wide), lambda h: (0, h))],
        scratch_shapes=[pltpu.VMEM((2 * rows, 2 * HEAD_SIZE), jnp.bfloat16)],
        compiler_params=pltpu.CompilerParams(vmem_limit_bytes=VMEM_LIMIT),
        cost_estimate=pl.CostEstimate(
            flops=8 * rows * width * rows, bytes_accessed=5 * 2**20, transcendentals=2 * rows * rows * heads * GROUP
        ),
        name="context_attention",
    )(own_len, q, k, v, *anchor, *anchor)


def mark_kernel(n_x, len_ref, k_ref, v_ref, rk_ref, rv_ref, *o_refs):
    rows, width = k_ref.shape
    own = rk_ref.shape[0]
    slab = rows // n_x
    first = jnp.broadcast_to(k_ref[0:1, :], (slab, width))
    for i, o_ref in enumerate(o_refs[:n_x]):
        span = slice(i * slab, (i + 1) * slab)
        valid = (i * slab + lax.broadcasted_iota(jnp.int32, first.shape, 0)) < len_ref[0]
        o_ref[:, :width] = jnp.where(valid, k_ref[span, :], first)
        o_ref[:, width:] = jnp.where(valid, v_ref[span, :], jnp.full_like(first, MARK))
    lines = o_refs[n_x:]
    valid = lax.broadcasted_iota(jnp.int32, (rows, HEAD_SIZE), 0) < len_ref[0]
    y = lax.axis_index("y")
    for i, o_ref in enumerate(lines):
        head = lax.rem(y + i, len(lines))
        lanes = pl.ds(pl.multiple_of(head * HEAD_SIZE, HEAD_SIZE), HEAD_SIZE)
        first = k_ref[0:1, lanes]
        o_ref[0:rows, :] = jnp.where(valid, k_ref[:, lanes], jnp.broadcast_to(first, valid.shape))
        o_ref[rows : rows + own, :] = rk_ref[:, lanes]
        mark = jnp.full((rows, HEAD_SIZE), MARK, jnp.bfloat16)
        o_ref[rows + own : 2 * rows + own, :] = jnp.where(valid, v_ref[:, lanes], mark)
        o_ref[2 * rows + own :, :] = rv_ref[:, lanes]


def pack_kernel(n_y, rq_ref, o_ref):
    own, width = rq_ref.shape
    targets = o_ref.shape[0] // 2
    some = o_ref.shape[1] // own
    for j in range(targets):
        x, y = j // n_y, j % n_y
        for c in range(2):
            for i in range(some):
                lane = c * (width // 2) + (GROUP * y + some * x + i) * HEAD_SIZE
                o_ref[2 * j + c, i * own : (i + 1) * own, :] = rq_ref[:, lane : lane + HEAD_SIZE]


def prepare_kernel(n_x, n_y, len_ref, rq_ref, k_ref, v_ref, rk_ref, rv_ref, sent_ref, *o_refs):
    pack_kernel(n_y, rq_ref, sent_ref)
    mark_kernel(n_x, len_ref, k_ref, v_ref, rk_ref, rv_ref, *o_refs)


def prepare(own_len, rq, k, v, rk, rv, n_x, n_y):
    rows, width = k.shape
    vmem = pl.BlockSpec(memory_space=pltpu.VMEM)
    targets = 2 * n_x * n_y
    shapes = [jax.ShapeDtypeStruct((targets, rq.size // (targets * HEAD_SIZE), HEAD_SIZE), k.dtype)]
    shapes += [jax.ShapeDtypeStruct((rows // n_x, 2 * width), k.dtype)] * n_x
    shapes += [jax.ShapeDtypeStruct((2 * (rows + rk.shape[0]), HEAD_SIZE), k.dtype)] * n_y
    out = pl.pallas_call(
        functools.partial(prepare_kernel, n_x, n_y),
        out_shape=shapes,
        in_specs=[pl.BlockSpec(memory_space=pltpu.SMEM)] + [vmem] * 5,
        out_specs=[vmem] * len(shapes),
        compiler_params=pltpu.CompilerParams(vmem_limit_bytes=56 * 1024 * 1024),
        cost_estimate=pl.CostEstimate(flops=2**18, bytes_accessed=5 * 2**19, transcendentals=0),
        name="prepare",
    )(own_len, rq, k, v, rk, rv)
    return out[0], out[1 : 1 + n_x], out[1 + n_x :]


def plane_kernel(owner_ref, x_ref, o_ref):
    own = 16
    source = 2 * lax.rem(owner_ref[0], N_X * N_Y)
    parts = []
    for i in range(x_ref.shape[1] // own):
        pick = slice(i * own, (i + 1) * own)
        parts += [x_ref[source, pick, :], x_ref[source + 1, pick, :]]
    part = jnp.concatenate(parts, axis=0)
    for z in range(o_ref.shape[0]):
        o_ref[z] = part


def line_kernel(owner_ref, x_ref, o_ref):
    o_ref[...] = x_ref[x_ref.shape[0] - 1 - lax.div(owner_ref[0], N_X * N_Y)]


def choose(kernel, owner, x, shape, flops):
    vmem = pl.BlockSpec(memory_space=pltpu.VMEM)
    return pl.pallas_call(
        kernel,
        out_shape=jax.ShapeDtypeStruct(shape, x.dtype),
        in_specs=[pl.BlockSpec(memory_space=pltpu.SMEM), vmem],
        out_specs=vmem,
        compiler_params=pltpu.CompilerParams(vmem_limit_bytes=VMEM_LIMIT),
        cost_estimate=pl.CostEstimate(flops=flops, bytes_accessed=2**19, transcendentals=0),
        name="choose",
    )(owner, x)


def split3(x):
    high = x.astype(jnp.bfloat16).astype(jnp.float32)
    rest = x - high
    mid = rest.astype(jnp.bfloat16).astype(jnp.float32)
    low = (rest - mid).astype(jnp.bfloat16).astype(jnp.float32)
    return high, mid, low


def code_rows(pair, last, height):
    row = lax.broadcasted_iota(jnp.int32, (height, HEAD_SIZE), 0)
    return jnp.where(row == 0, pair, jnp.where(row == 1, last, 0.0)).astype(jnp.bfloat16)


def request_kernel(own, count, owner_ref, *refs):
    q_refs, lines = refs[:count], refs[count : -count - 1]
    o_refs, v_ref = refs[-count - 1 : -1], refs[-1]
    piece = q_refs[0].shape[0]
    n = count * piece
    both = lines[0].shape[0] // 2
    rows = both - own
    c = SCALE * LOG2E
    q = jnp.concatenate([ref[...] for ref in q_refs], axis=0)
    for i, ref in enumerate(lines):
        part = ref[both : both + rows, :]
        hidden = part > 100.0
        top = i * rows
        v_ref[top : top + rows, :HEAD_SIZE] = jnp.where(hidden, jnp.zeros_like(part), part)
        v_ref[top : top + rows, HEAD_SIZE:] = jnp.where(hidden, jnp.zeros_like(part), jnp.ones_like(part))
        top = len(lines) * rows + i * own
        v_ref[top : top + own, :HEAD_SIZE] = ref[both + rows :, :]
        v_ref[top : top + own, HEAD_SIZE:] = jnp.ones((own, HEAD_SIZE), jnp.bfloat16)
    owner = owner_ref[0]
    same = lax.div(owner, N_Y) == lax.div(place(), N_Y)
    asked = jnp.where(same, lax.rem(lax.axis_index("y") - lax.rem(owner, N_Y) + N_Y, N_Y), -1)
    own_keys = jnp.concatenate([ref[rows:both, :] for ref in lines], axis=0)
    row = lax.rem(lax.broadcasted_iota(jnp.int32, (n, own_keys.shape[0]), 0), own)
    col = lax.broadcasted_iota(jnp.int32, (n, own_keys.shape[0]), 1) - asked * own
    scores = [dot_nt(q, ref[0:rows, :]) for ref in lines]
    scores.append(jnp.where((asked >= 0) & (col >= 0) & (col <= row), dot_nt(q, own_keys), -jnp.inf))
    tiles = [s[:, i : i + HEAD_SIZE] for s in scores for i in range(0, s.shape[1], HEAD_SIZE)]
    peak = jnp.max(functools.reduce(jnp.maximum, tiles), axis=1, keepdims=True)
    weights = [jnp.exp2((tile - peak) * c).astype(jnp.bfloat16) for tile in tiles]
    acc = dot_nn(jnp.concatenate(weights, axis=1), v_ref[...])
    total = acc[:, HEAD_SIZE:]
    out = acc[:, :HEAD_SIZE] / total
    out_high = out.astype(jnp.bfloat16)
    out_low = (out - out_high.astype(jnp.float32)).astype(jnp.bfloat16)
    lse = peak * SCALE + jnp.log(total)
    high, mid, low = split3(lse)
    row = lax.broadcasted_iota(jnp.int32, (piece, HEAD_SIZE), 0)
    lane = lax.broadcasted_iota(jnp.int32, (piece, HEAD_SIZE), 1)
    for p, o_ref in enumerate(o_refs):
        part = slice(p * piece, (p + 1) * piece)
        pair = jnp.where(row == lane, high[part], jnp.where(row + piece == lane, mid[part], 0.0))
        last = jnp.where(row == lane, low[part], 0.0)
        o_ref[0:piece, :] = out_high[part]
        o_ref[piece : 2 * piece, :] = out_low[part]
        o_ref[2 * piece :, :] = code_rows(
            jnp.sum(pair, axis=0, keepdims=True), jnp.sum(last, axis=0, keepdims=True), 16
        )


def request_partials(owner, queries, lines, own):
    count, piece = len(queries), queries[0].shape[0]
    keys = len(lines) * lines[0].shape[0] // 2
    vmem = pl.BlockSpec(memory_space=pltpu.VMEM)
    return pl.pallas_call(
        functools.partial(request_kernel, own, count),
        out_shape=[jax.ShapeDtypeStruct((2 * piece + 16, HEAD_SIZE), jnp.bfloat16)] * count,
        in_specs=[pl.BlockSpec(memory_space=pltpu.SMEM)] + [vmem] * (count + len(lines)),
        out_specs=[vmem] * count,
        scratch_shapes=[pltpu.VMEM((keys, 2 * HEAD_SIZE), jnp.bfloat16)],
        compiler_params=pltpu.CompilerParams(vmem_limit_bytes=VMEM_LIMIT),
        cost_estimate=pl.CostEstimate(
            flops=3 * 10**9, bytes_accessed=2**20, transcendentals=count * piece * keys
        ),
        name="request_partials",
    )(owner, *queries, *lines)


def join_kernel(parts_in, keep_code, *refs):
    x_refs, o_ref = refs[:-1], refs[-1]
    if len(x_refs) == 1:
        x_refs = [x_refs[0].at[i] for i in range(x_refs[0].shape[0])]
    height = x_refs[0].shape[0]
    top = height - 16
    piece = top // parts_in
    count = max(len(x_refs), 8)
    row = lax.broadcasted_iota(jnp.int32, (count, HEAD_SIZE), 0)
    lane = lax.broadcasted_iota(jnp.int32, (count, HEAD_SIZE), 1)
    pair = jnp.zeros((count, HEAD_SIZE), jnp.float32)
    last = jnp.zeros((count, HEAD_SIZE), jnp.float32)
    for i, ref in enumerate(x_refs):
        code = ref[top:height, :].astype(jnp.float32)
        pair = jnp.where(row == i, code[0:1, :], pair)
        last = jnp.where(row == i, code[1:2, :], last)
    lse = jnp.where(lane < piece, pair + pltpu.roll(pair, piece, 1) + last, 0.0)
    lse = jnp.where(row < len(x_refs), lse, -jnp.inf)
    peak = jnp.max(lse, axis=0, keepdims=True)
    weight = jnp.exp(lse - peak)
    total = jnp.sum(weight, axis=0, keepdims=True)
    column = jnp.transpose(weight / total)
    out = jnp.zeros((piece, HEAD_SIZE), jnp.float32)
    for i, ref in enumerate(x_refs):
        part = ref[0:piece, :].astype(jnp.float32)
        if parts_in > 1:
            part = part + ref[piece:top, :].astype(jnp.float32)
        out = out + column[0:piece, i : i + 1] * part
    parts = [out.astype(jnp.bfloat16)]
    if keep_code:
        high, mid, low = split3(peak + jnp.log(total))
        pair = jnp.where(lane[0:1] < piece, high, pltpu.roll(mid, piece, 1))
        parts.append(code_rows(pair, low, 16))
    part = jnp.concatenate(parts, axis=0)
    if len(o_ref.shape) == 2:
        o_ref[...] = part
    else:
        for i in range(o_ref.shape[0]):
            o_ref[i] = part


def join(arrays, copies, parts_in, keep_code):
    height = (arrays[0].shape[-2] - 16) // parts_in + (16 if keep_code else 0)
    shape = (copies, height, HEAD_SIZE) if copies else (height, HEAD_SIZE)
    return pl.pallas_call(
        functools.partial(join_kernel, parts_in, keep_code),
        out_shape=jax.ShapeDtypeStruct(shape, jnp.bfloat16),
        compiler_params=pltpu.CompilerParams(vmem_limit_bytes=VMEM_LIMIT),
        cost_estimate=pl.CostEstimate(flops=3 * 10**9, bytes_accessed=2**19, transcendentals=1024),
        name="join_pieces",
    )(*arrays)


def answer_kernel(owner_ref, x_ref, _, o_ref, rows_ref, sem):
    own = rows_ref.shape[0]
    some = x_ref.shape[1] // own

    @pl.when(place() == owner_ref[0])
    def _():
        for j in range(x_ref.shape[0]):
            x, y = j // N_Y, j % N_Y
            for i in range(some):
                lane = (GROUP * y + some * x + i) * HEAD_SIZE
                rows_ref[:, lane : lane + HEAD_SIZE] = x_ref[j, i * own : (i + 1) * own, :]
        copy = pltpu.make_async_copy(rows_ref, o_ref, sem)
        copy.start()
        copy.wait()


def answer_rows(owner, x, zeros):
    any_spec = pl.BlockSpec(memory_space=pl.ANY)
    return pl.pallas_call(
        answer_kernel,
        out_shape=jax.ShapeDtypeStruct(zeros.shape, zeros.dtype),
        in_specs=[pl.BlockSpec(memory_space=pltpu.SMEM), pl.BlockSpec(memory_space=pltpu.VMEM), any_spec],
        out_specs=any_spec,
        input_output_aliases={2: 0},
        scratch_shapes=[pltpu.VMEM(zeros.shape, zeros.dtype), pltpu.SemaphoreType.DMA],
        compiler_params=pltpu.CompilerParams(vmem_limit_bytes=VMEM_LIMIT),
        cost_estimate=pl.CostEstimate(flops=2**18, bytes_accessed=2**19, transcendentals=0),
        name="answer_rows",
    )(owner, x, zeros)


def exchange(x, axis, groups=None):
    return lax.all_to_all(x, axis, split_axis=0, concat_axis=0, axis_index_groups=groups, tiled=True)


def local(n_z, n_x, n_y, q, k, v, block_lengths, rq, rk, rv, query_owner):
    n_xy = n_x * n_y
    z, x, y = (lax.axis_index(name) for name in ("z", "x", "y"))
    own_len = block_lengths
    own_rows = rk.shape[0]
    down = [list(range(n_z))[::-1]]

    def move(value, pairs):
        return lax.ppermute(value, ("z", "x", "y"), pairs)

    def shift_x(value, count):
        return lax.ppermute(value, "x", [(a, (a + count) % n_x) for a in range(n_x)])

    sent, pieces, lines = prepare(own_len, rq, k, v, rk, rv, n_x, n_y)
    moved = exchange(sent, ("x", "y", "head"))
    got = [move(pieces[i], [(0, i * n_y)]) for i in range(1, n_x)]
    lines = [lines[0]] + [
        lax.ppermute(lines[i], "y", [(a, (a + i) % n_y) for a in range(n_y)]) for i in range(1, n_y)
    ]

    piece = (2 * moved.shape[1], HEAD_SIZE)
    moved, got = lax.optimization_barrier((moved, got))
    moved = choose(plane_kernel, query_owner, moved, (n_z,) + piece, 8 * 10**8)
    anchor = jnp.where(x == 0, pieces[0], got[0] + got[1] + got[2])
    got = [move(anchor, [(i * n_y, i * n_y + j) for i in range(n_x)]) for j in range(1, n_y)]
    moved = exchange(moved, "z", down)

    moved = choose(line_kernel, query_owner, moved, piece, 3 * 10**9)
    moved, lines = lax.optimization_barrier((moved, lines))
    anchor = jnp.where(y == 0, anchor, got[0] + got[1] + got[2])
    plane = range(n_xy)
    got = [move(anchor, [(p, to * n_xy + p) for p in plane]) for to in (2, 6)]
    queries = [moved] + [shift_x(moved, i) for i in range(1, n_x)]

    partials = request_partials(query_owner, queries, lines, own_rows)
    anchor = jnp.where(z == 0, anchor, got[0] + got[1])
    steps = (((0, 1), (2, 3), (6, 5)), ((0, 7), (2, 4)))
    got = [move(anchor, [(a * n_xy + p, b * n_xy + p) for a, b in step for p in plane]) for step in steps]
    partials = [partials[0]] + [shift_x(partials[i], n_x - i) for i in range(1, n_x)]

    planes = join(partials, n_z, 2, True)
    anchor = jnp.where((z == 0) | (z == 2) | (z == 6), anchor, got[0] + got[1])
    anchors = [anchor]
    for i in range(1, n_x):
        anchors.append(shift_x(anchor, i))
    planes = exchange(planes, "z", down)

    answer = exchange(join([planes], n_xy, 1, False), ("x", "y"))
    context_output, zeros = context_attention(own_len, q, k, v, anchors, own_rows)
    request_output = answer_rows(query_owner, answer, zeros)
    return context_output, request_output


def solution(mesh):
    n_z, n_x, n_y = 8, N_X, N_Y
    grid = jax.sharding.Mesh(mesh.devices.reshape(n_z, n_x, n_y, 2), ("z", "x", "y", "head"))
    ctx = ("z", "x", "y")
    in_specs = (
        P(ctx, "head"),
        P(ctx, "head"),
        P(ctx, "head"),
        P(ctx),
        P(ctx + ("head",), None),
        P(ctx, "head"),
        P(ctx, "head"),
        P(),
    )
    out_specs = (P(ctx, "head"), P(ctx, "head"))
    return jax.shard_map(
        functools.partial(local, n_z, n_x, n_y),
        mesh=grid,
        in_specs=in_specs,
        out_specs=out_specs,
        check_vma=False,
    )
```

```python
import functools

import jax
import jax.numpy as jnp
from jax import lax
from jax.experimental import pallas as pl
from jax.experimental.pallas import tpu as pltpu
from jax.sharding import PartitionSpec as P

HEAD_SIZE = 128
GROUP = 8
SCALE = HEAD_SIZE**-0.5
LOG2E = 1.4426950408889634
LN2 = 0.6931471805599453
MARK = 1024.0
VMEM_LIMIT = 32 * 1024 * 1024
STACK = 4
N_X, N_Y = 4, 4


def place():
    return (lax.axis_index("z") * N_X + lax.axis_index("x")) * N_Y + lax.axis_index("y")


def dot_nt(a, b):
    return lax.dot_general(a, b, (((1,), (1,)), ((), ())), preferred_element_type=jnp.float32)


def dot_nn(a, b):
    return lax.dot_general(a, b, (((1,), (0,)), ((), ())), preferred_element_type=jnp.float32)


def context_kernel(count, len_ref, q_ref, k_ref, v_ref, *refs):
    ak_refs, av_refs = refs[:count], refs[count : 2 * count]
    o_ref, zero_ref, vs_ref = refs[-3:]
    zero_ref[...] = jnp.zeros_like(zero_ref)
    rows = k_ref.shape[0]
    half = rows // 2
    own_len = len_ref[0]
    root = place() == 0
    ak = jnp.concatenate([ref[...] for ref in ak_refs], axis=0)
    ak = jnp.where(root, jnp.broadcast_to(k_ref[0:1, :], ak.shape), ak)
    av = jnp.concatenate([ref[...] for ref in av_refs], axis=0)
    hidden = (av > 100.0) | root
    vs_ref[0:rows, :HEAD_SIZE] = jnp.where(hidden, jnp.zeros_like(av), av)
    vs_ref[0:rows, HEAD_SIZE:] = jnp.where(hidden, jnp.zeros_like(av), jnp.ones_like(av))
    vs_ref[rows:, :HEAD_SIZE] = v_ref[...]
    vs_ref[rows:, HEAD_SIZE:] = jnp.ones((rows, HEAD_SIZE), jnp.bfloat16)
    c = SCALE * LOG2E
    row = lax.broadcasted_iota(jnp.int32, (STACK * half, half), 0)
    col = lax.broadcasted_iota(jnp.int32, (STACK * half, half), 1)
    causal = jnp.where(col <= lax.rem(row, half), 0.0, -jnp.inf).astype(jnp.float32)

    def lanes(g):
        return slice(g * HEAD_SIZE, (g + 1) * HEAD_SIZE)

    def scores(top, g):
        keys = top + half
        q = jnp.concatenate([q_ref[top:keys, lanes(g + i)] for i in range(STACK)], axis=0)
        sa = dot_nt(q, ak)
        so = dot_nt(q, k_ref[0:keys, :])
        tiles = [sa[:, i : i + half] for i in range(0, rows, half)]
        tiles += [so[:, i : i + half] for i in range(0, top, half)]
        return tiles + [so[:, top:keys] + causal]

    def finish(top, g, tiles):
        keys = top + half
        live = (top + lax.broadcasted_iota(jnp.int32, (half, HEAD_SIZE), 0)) < own_len
        peak = jnp.max(functools.reduce(jnp.maximum, tiles), axis=1, keepdims=True)
        weights = [jnp.exp2((tile - peak) * c).astype(jnp.bfloat16) for tile in tiles]
        acc = dot_nn(jnp.concatenate(weights, axis=1), vs_ref[0 : rows + keys, :])
        total = acc[:, HEAD_SIZE:]
        inverse = pl.reciprocal(total, approx=True)
        inverse = inverse * (2.0 - total * inverse)
        out = acc[:, :HEAD_SIZE] * inverse
        for i in range(STACK):
            part = jnp.where(live, out[i * half : (i + 1) * half], 0.0)
            o_ref[top:keys, lanes(g + i)] = part.astype(jnp.bfloat16)

    work = [(top, g) for top in (0, half) for g in range(0, GROUP, STACK)]
    tiles = scores(*work[0])
    for i, item in enumerate(work):
        later = scores(*work[i + 1]) if i + 1 < len(work) else None
        finish(*item, tiles)
        tiles = later


def context_attention(own_len, q, k, v, anchor, own_rows):
    rows, width = q.shape
    heads = k.shape[1] // HEAD_SIZE
    wide = GROUP * HEAD_SIZE
    count = len(anchor)
    slab = anchor[0].shape[0]
    smem = pl.BlockSpec(memory_space=pltpu.SMEM)
    kv_spec = pl.BlockSpec((rows, HEAD_SIZE), lambda h: (0, h))
    wide_spec = pl.BlockSpec((rows, wide), lambda h: (0, h))
    specs = [smem, wide_spec, kv_spec, kv_spec]
    specs += [pl.BlockSpec((slab, HEAD_SIZE), lambda h: (0, h))] * count
    specs += [pl.BlockSpec((slab, HEAD_SIZE), lambda h: (0, heads + h))] * count
    return pl.pallas_call(
        functools.partial(context_kernel, count),
        grid=(heads,),
        out_shape=[
            jax.ShapeDtypeStruct((rows, width), jnp.bfloat16),
            jax.ShapeDtypeStruct((own_rows, width), jnp.bfloat16),
        ],
        in_specs=specs,
        out_specs=[wide_spec, pl.BlockSpec((own_rows, wide), lambda h: (0, h))],
        scratch_shapes=[pltpu.VMEM((2 * rows, 2 * HEAD_SIZE), jnp.bfloat16)],
        compiler_params=pltpu.CompilerParams(vmem_limit_bytes=VMEM_LIMIT),
        cost_estimate=pl.CostEstimate(
            flops=8 * rows * width * rows, bytes_accessed=5 * 2**20, transcendentals=2 * rows * rows * heads * GROUP
        ),
        name="context_attention",
    )(own_len, q, k, v, *anchor, *anchor)


def mark_kernel(n_x, len_ref, k_ref, v_ref, rk_ref, rv_ref, *o_refs):
    rows, width = k_ref.shape
    own = rk_ref.shape[0]
    slab = rows // n_x
    first = jnp.broadcast_to(k_ref[0:1, :], (slab, width))
    for i, o_ref in enumerate(o_refs[:n_x]):
        span = slice(i * slab, (i + 1) * slab)
        valid = (i * slab + lax.broadcasted_iota(jnp.int32, first.shape, 0)) < len_ref[0]
        o_ref[:, :width] = jnp.where(valid, k_ref[span, :], first)
        o_ref[:, width:] = jnp.where(valid, v_ref[span, :], jnp.full_like(first, MARK))
    lines = o_refs[n_x:]
    valid = lax.broadcasted_iota(jnp.int32, (rows, HEAD_SIZE), 0) < len_ref[0]
    y = lax.axis_index("y")
    for i, o_ref in enumerate(lines):
        head = lax.rem(y + i, len(lines))
        lanes = pl.ds(pl.multiple_of(head * HEAD_SIZE, HEAD_SIZE), HEAD_SIZE)
        first = k_ref[0:1, lanes]
        o_ref[0:rows, :] = jnp.where(valid, k_ref[:, lanes], jnp.broadcast_to(first, valid.shape))
        o_ref[rows : rows + own, :] = rk_ref[:, lanes]
        mark = jnp.full((rows, HEAD_SIZE), MARK, jnp.bfloat16)
        o_ref[rows + own : 2 * rows + own, :] = jnp.where(valid, v_ref[:, lanes], mark)
        o_ref[2 * rows + own :, :] = rv_ref[:, lanes]


def pack_kernel(n_y, rq_ref, o_ref):
    own, width = rq_ref.shape
    targets = o_ref.shape[0] // 2
    some = o_ref.shape[1] // own
    for j in range(targets):
        x, y = j // n_y, j % n_y
        for c in range(2):
            for i in range(some):
                lane = c * (width // 2) + (GROUP * y + some * x + i) * HEAD_SIZE
                o_ref[2 * j + c, i * own : (i + 1) * own, :] = rq_ref[:, lane : lane + HEAD_SIZE]


def prepare_kernel(n_x, n_y, len_ref, rq_ref, k_ref, v_ref, rk_ref, rv_ref, sent_ref, *o_refs):
    pack_kernel(n_y, rq_ref, sent_ref)
    mark_kernel(n_x, len_ref, k_ref, v_ref, rk_ref, rv_ref, *o_refs)


def prepare(own_len, rq, k, v, rk, rv, n_x, n_y):
    rows, width = k.shape
    vmem = pl.BlockSpec(memory_space=pltpu.VMEM)
    targets = 2 * n_x * n_y
    shapes = [jax.ShapeDtypeStruct((targets, rq.size // (targets * HEAD_SIZE), HEAD_SIZE), k.dtype)]
    shapes += [jax.ShapeDtypeStruct((rows // n_x, 2 * width), k.dtype)] * n_x
    shapes += [jax.ShapeDtypeStruct((2 * (rows + rk.shape[0]), HEAD_SIZE), k.dtype)] * n_y
    out = pl.pallas_call(
        functools.partial(prepare_kernel, n_x, n_y),
        out_shape=shapes,
        in_specs=[pl.BlockSpec(memory_space=pltpu.SMEM)] + [vmem] * 5,
        out_specs=[vmem] * len(shapes),
        compiler_params=pltpu.CompilerParams(vmem_limit_bytes=56 * 1024 * 1024),
        cost_estimate=pl.CostEstimate(flops=2**18, bytes_accessed=5 * 2**19, transcendentals=0),
        name="prepare",
    )(own_len, rq, k, v, rk, rv)
    return out[0], out[1 : 1 + n_x], out[1 + n_x :]


def plane_kernel(owner_ref, x_ref, o_ref):
    own = 16
    source = 2 * lax.rem(owner_ref[0], N_X * N_Y)
    parts = []
    for i in range(x_ref.shape[1] // own):
        pick = slice(i * own, (i + 1) * own)
        parts += [x_ref[source, pick, :], x_ref[source + 1, pick, :]]
    part = jnp.concatenate(parts, axis=0)
    for z in range(o_ref.shape[0]):
        o_ref[z] = part


def line_kernel(owner_ref, x_ref, o_ref):
    o_ref[...] = x_ref[x_ref.shape[0] - 1 - lax.div(owner_ref[0], N_X * N_Y)]


def choose(kernel, owner, x, shape, flops):
    vmem = pl.BlockSpec(memory_space=pltpu.VMEM)
    return pl.pallas_call(
        kernel,
        out_shape=jax.ShapeDtypeStruct(shape, x.dtype),
        in_specs=[pl.BlockSpec(memory_space=pltpu.SMEM), vmem],
        out_specs=vmem,
        compiler_params=pltpu.CompilerParams(vmem_limit_bytes=VMEM_LIMIT),
        cost_estimate=pl.CostEstimate(flops=flops, bytes_accessed=2**19, transcendentals=0),
        name="choose",
    )(owner, x)


def split3(x):
    high = x.astype(jnp.bfloat16).astype(jnp.float32)
    rest = x - high
    mid = rest.astype(jnp.bfloat16).astype(jnp.float32)
    low = (rest - mid).astype(jnp.bfloat16).astype(jnp.float32)
    return high, mid, low


def code_rows(pair, last, height):
    row = lax.broadcasted_iota(jnp.int32, (height, HEAD_SIZE), 0)
    return jnp.where(row == 0, pair, jnp.where(row == 1, last, 0.0)).astype(jnp.bfloat16)


def request_kernel(own, count, owner_ref, *refs):
    q_refs, lines = refs[:count], refs[count : -count - 1]
    o_refs, v_ref = refs[-count - 1 : -1], refs[-1]
    piece = q_refs[0].shape[0]
    n = count * piece
    both = lines[0].shape[0] // 2
    rows = both - own
    c = SCALE * LOG2E
    q = jnp.concatenate([ref[...] for ref in q_refs], axis=0)
    for i, ref in enumerate(lines):
        part = ref[both : both + rows, :]
        hidden = part > 100.0
        top = i * rows
        v_ref[top : top + rows, :HEAD_SIZE] = jnp.where(hidden, jnp.zeros_like(part), part)
        v_ref[top : top + rows, HEAD_SIZE:] = jnp.where(hidden, jnp.zeros_like(part), jnp.ones_like(part))
        top = len(lines) * rows + i * own
        v_ref[top : top + own, :HEAD_SIZE] = ref[both + rows :, :]
        v_ref[top : top + own, HEAD_SIZE:] = jnp.ones((own, HEAD_SIZE), jnp.bfloat16)
    owner = owner_ref[0]
    same = lax.div(owner, N_Y) == lax.div(place(), N_Y)
    asked = jnp.where(same, lax.rem(lax.axis_index("y") - lax.rem(owner, N_Y) + N_Y, N_Y), -1)
    own_keys = jnp.concatenate([ref[rows:both, :] for ref in lines], axis=0)
    row = lax.rem(lax.broadcasted_iota(jnp.int32, (n, own_keys.shape[0]), 0), own)
    col = lax.broadcasted_iota(jnp.int32, (n, own_keys.shape[0]), 1) - asked * own
    scores = [dot_nt(q, ref[0:rows, :]) for ref in lines]
    scores.append(jnp.where((asked >= 0) & (col >= 0) & (col <= row), dot_nt(q, own_keys), -jnp.inf))
    tiles = [s[:, i : i + HEAD_SIZE] for s in scores for i in range(0, s.shape[1], HEAD_SIZE)]
    peak = jnp.max(functools.reduce(jnp.maximum, tiles), axis=1, keepdims=True)
    weights = [jnp.exp2((tile - peak) * c).astype(jnp.bfloat16) for tile in tiles]
    acc = dot_nn(jnp.concatenate(weights, axis=1), v_ref[...])
    total = acc[:, HEAD_SIZE:]
    out = acc[:, :HEAD_SIZE] / total
    out_high = out.astype(jnp.bfloat16)
    out_low = (out - out_high.astype(jnp.float32)).astype(jnp.bfloat16)
    lse = peak * SCALE + jnp.log(total)
    high, mid, low = split3(lse)
    row = lax.broadcasted_iota(jnp.int32, (piece, HEAD_SIZE), 0)
    lane = lax.broadcasted_iota(jnp.int32, (piece, HEAD_SIZE), 1)
    for p, o_ref in enumerate(o_refs):
        part = slice(p * piece, (p + 1) * piece)
        pair = jnp.where(row == lane, high[part], jnp.where(row + piece == lane, mid[part], 0.0))
        last = jnp.where(row == lane, low[part], 0.0)
        o_ref[0:piece, :] = out_high[part]
        o_ref[piece : 2 * piece, :] = out_low[part]
        o_ref[2 * piece :, :] = code_rows(
            jnp.sum(pair, axis=0, keepdims=True), jnp.sum(last, axis=0, keepdims=True), 16
        )


def request_partials(owner, queries, lines, own):
    count, piece = len(queries), queries[0].shape[0]
    keys = len(lines) * lines[0].shape[0] // 2
    vmem = pl.BlockSpec(memory_space=pltpu.VMEM)
    return pl.pallas_call(
        functools.partial(request_kernel, own, count),
        out_shape=[jax.ShapeDtypeStruct((2 * piece + 16, HEAD_SIZE), jnp.bfloat16)] * count,
        in_specs=[pl.BlockSpec(memory_space=pltpu.SMEM)] + [vmem] * (count + len(lines)),
        out_specs=[vmem] * count,
        scratch_shapes=[pltpu.VMEM((keys, 2 * HEAD_SIZE), jnp.bfloat16)],
        compiler_params=pltpu.CompilerParams(vmem_limit_bytes=VMEM_LIMIT),
        cost_estimate=pl.CostEstimate(
            flops=3 * 10**9, bytes_accessed=2**20, transcendentals=count * piece * keys
        ),
        name="request_partials",
    )(owner, *queries, *lines)


def join_kernel(parts_in, keep_code, *refs):
    x_refs, o_ref = refs[:-1], refs[-1]
    if len(x_refs) == 1:
        x_refs = [x_refs[0].at[i] for i in range(x_refs[0].shape[0])]
    height = x_refs[0].shape[0]
    top = height - 16
    piece = top // parts_in
    count = max(len(x_refs), 8)
    row = lax.broadcasted_iota(jnp.int32, (count, HEAD_SIZE), 0)
    lane = lax.broadcasted_iota(jnp.int32, (count, HEAD_SIZE), 1)
    pair = jnp.zeros((count, HEAD_SIZE), jnp.float32)
    last = jnp.zeros((count, HEAD_SIZE), jnp.float32)
    for i, ref in enumerate(x_refs):
        code = ref[top:height, :].astype(jnp.float32)
        pair = jnp.where(row == i, code[0:1, :], pair)
        last = jnp.where(row == i, code[1:2, :], last)
    lse = jnp.where(lane < piece, pair + pltpu.roll(pair, piece, 1) + last, 0.0)
    lse = jnp.where(row < len(x_refs), lse, -jnp.inf)
    peak = jnp.max(lse, axis=0, keepdims=True)
    weight = jnp.exp(lse - peak)
    total = jnp.sum(weight, axis=0, keepdims=True)
    column = jnp.transpose(weight / total)
    out = jnp.zeros((piece, HEAD_SIZE), jnp.float32)
    for i, ref in enumerate(x_refs):
        part = ref[0:piece, :].astype(jnp.float32)
        if parts_in > 1:
            part = part + ref[piece:top, :].astype(jnp.float32)
        out = out + column[0:piece, i : i + 1] * part
    parts = [out.astype(jnp.bfloat16)]
    if keep_code:
        high, mid, low = split3(peak + jnp.log(total))
        pair = jnp.where(lane[0:1] < piece, high, pltpu.roll(mid, piece, 1))
        parts.append(code_rows(pair, low, 16))
    part = jnp.concatenate(parts, axis=0)
    if len(o_ref.shape) == 2:
        o_ref[...] = part
    else:
        for i in range(o_ref.shape[0]):
            o_ref[i] = part


def join(arrays, copies, parts_in, keep_code):
    height = (arrays[0].shape[-2] - 16) // parts_in + (16 if keep_code else 0)
    shape = (copies, height, HEAD_SIZE) if copies else (height, HEAD_SIZE)
    return pl.pallas_call(
        functools.partial(join_kernel, parts_in, keep_code),
        out_shape=jax.ShapeDtypeStruct(shape, jnp.bfloat16),
        compiler_params=pltpu.CompilerParams(vmem_limit_bytes=VMEM_LIMIT),
        cost_estimate=pl.CostEstimate(flops=3 * 10**9, bytes_accessed=2**19, transcendentals=1024),
        name="join_pieces",
    )(*arrays)


def answer_kernel(owner_ref, x_ref, _, o_ref, rows_ref, sem):
    own = rows_ref.shape[0]
    some = x_ref.shape[1] // own

    @pl.when(place() == owner_ref[0])
    def _():
        for j in range(x_ref.shape[0]):
            x, y = j // N_Y, j % N_Y
            for i in range(some):
                lane = (GROUP * y + some * x + i) * HEAD_SIZE
                rows_ref[:, lane : lane + HEAD_SIZE] = x_ref[j, i * own : (i + 1) * own, :]
        copy = pltpu.make_async_copy(rows_ref, o_ref, sem)
        copy.start()
        copy.wait()


def answer_rows(owner, x, zeros):
    any_spec = pl.BlockSpec(memory_space=pl.ANY)
    return pl.pallas_call(
        answer_kernel,
        out_shape=jax.ShapeDtypeStruct(zeros.shape, zeros.dtype),
        in_specs=[pl.BlockSpec(memory_space=pltpu.SMEM), pl.BlockSpec(memory_space=pltpu.VMEM), any_spec],
        out_specs=any_spec,
        input_output_aliases={2: 0},
        scratch_shapes=[pltpu.VMEM(zeros.shape, zeros.dtype), pltpu.SemaphoreType.DMA],
        compiler_params=pltpu.CompilerParams(vmem_limit_bytes=VMEM_LIMIT),
        cost_estimate=pl.CostEstimate(flops=2**18, bytes_accessed=2**19, transcendentals=0),
        name="answer_rows",
    )(owner, x, zeros)


def exchange(x, axis, groups=None):
    return lax.all_to_all(x, axis, split_axis=0, concat_axis=0, axis_index_groups=groups, tiled=True)


def local(n_z, n_x, n_y, q, k, v, block_lengths, rq, rk, rv, query_owner):
    n_xy = n_x * n_y
    z, x, y = (lax.axis_index(name) for name in ("z", "x", "y"))
    own_len = block_lengths
    own_rows = rk.shape[0]
    down = [list(range(n_z))[::-1]]

    def move(value, pairs):
        return lax.ppermute(value, ("z", "x", "y"), pairs)

    def shift_x(value, count):
        return lax.ppermute(value, "x", [(a, (a + count) % n_x) for a in range(n_x)])

    sent, pieces, lines = prepare(own_len, rq, k, v, rk, rv, n_x, n_y)
    moved = exchange(sent, ("x", "y", "head"))
    got = [move(pieces[i], [(0, i * n_y)]) for i in range(1, n_x)]
    lines = [lines[0]] + [
        lax.ppermute(lines[i], "y", [(a, (a + i) % n_y) for a in range(n_y)]) for i in range(1, n_y)
    ]

    piece = (2 * moved.shape[1], HEAD_SIZE)
    moved, got = lax.optimization_barrier((moved, got))
    moved = choose(plane_kernel, query_owner, moved, (n_z,) + piece, 8 * 10**8)
    anchor = jnp.where(x == 0, pieces[0], got[0] + got[1] + got[2])
    got = [move(anchor, [(i * n_y, (to * n_x + i) * n_y) for i in range(n_x)]) for to in (2, 6)]
    moved = exchange(moved, "z", down)

    moved = choose(line_kernel, query_owner, moved, piece, 3 * 10**9)
    moved, lines = lax.optimization_barrier((moved, lines))
    anchor = jnp.where(z == 0, anchor, got[0] + got[1])
    rows = [(to * n_x + i) * n_y for to in (0, 2, 6) for i in range(n_x)]
    got = [move(anchor, [(p, p + j) for p in rows]) for j in range(1, n_y)]
    queries = [moved] + [shift_x(moved, i) for i in range(1, n_x)]

    partials = request_partials(query_owner, queries, lines, own_rows)
    anchor = jnp.where(y == 0, anchor, got[0] + got[1] + got[2])
    plane = range(n_xy)
    steps = (((0, 1), (2, 3), (6, 5)), ((0, 7), (2, 4)))
    got = [move(anchor, [(a * n_xy + p, b * n_xy + p) for a, b in step for p in plane]) for step in steps]
    partials = [partials[0]] + [shift_x(partials[i], n_x - i) for i in range(1, n_x)]

    planes = join(partials, n_z, 2, True)
    anchor = jnp.where((z == 0) | (z == 2) | (z == 6), anchor, got[0] + got[1])
    anchors = [anchor]
    for i in range(1, n_x):
        anchors.append(shift_x(anchor, i))
    planes = exchange(planes, "z", down)

    answer = exchange(join([planes], n_xy, 1, False), ("x", "y"))
    context_output, zeros = context_attention(own_len, q, k, v, anchors, own_rows)
    request_output = answer_rows(query_owner, answer, zeros)
    return context_output, request_output


def solution(mesh):
    n_z, n_x, n_y = 8, N_X, N_Y
    grid = jax.sharding.Mesh(mesh.devices.reshape(n_z, n_x, n_y, 2), ("z", "x", "y", "head"))
    ctx = ("z", "x", "y")
    in_specs = (
        P(ctx, "head"),
        P(ctx, "head"),
        P(ctx, "head"),
        P(ctx),
        P(ctx + ("head",), None),
        P(ctx, "head"),
        P(ctx, "head"),
        P(),
    )
    out_specs = (P(ctx, "head"), P(ctx, "head"))
    return jax.shard_map(
        functools.partial(local, n_z, n_x, n_y),
        mesh=grid,
        in_specs=in_specs,
        out_specs=out_specs,
        check_vma=False,
    )
```

```python
import functools

import jax
import jax.numpy as jnp
from jax import lax
from jax.experimental import pallas as pl
from jax.experimental.pallas import tpu as pltpu
from jax.sharding import PartitionSpec as P

HEAD_SIZE = 128
GROUP = 8
SCALE = HEAD_SIZE**-0.5
LOG2E = 1.4426950408889634
LN2 = 0.6931471805599453
MARK = 1024.0
VMEM_LIMIT = 32 * 1024 * 1024
STACK = 4
N_X, N_Y = 4, 4


def place():
    return (lax.axis_index("z") * N_X + lax.axis_index("x")) * N_Y + lax.axis_index("y")


def dot_nt(a, b):
    return lax.dot_general(a, b, (((1,), (1,)), ((), ())), preferred_element_type=jnp.float32)


def dot_nn(a, b):
    return lax.dot_general(a, b, (((1,), (0,)), ((), ())), preferred_element_type=jnp.float32)


def context_kernel(count, len_ref, q_ref, k_ref, v_ref, *refs):
    anchor_refs = refs[:count]
    o_ref, zero_ref, vs_ref, out_ref, sems = refs[-5:]
    zero_ref[...] = jnp.zeros_like(zero_ref)
    rows, width = k_ref.shape
    half = rows // 2
    heads = width // HEAD_SIZE
    own_len = len_ref[0]
    root = place() == 0
    c = SCALE * LOG2E
    row = lax.broadcasted_iota(jnp.int32, (STACK * half, half), 0)
    col = lax.broadcasted_iota(jnp.int32, (STACK * half, half), 1)
    causal = jnp.where(col <= lax.rem(row, half), 0.0, -jnp.inf).astype(jnp.float32)

    def lanes(g):
        return slice(g * HEAD_SIZE, (g + 1) * HEAD_SIZE)

    def load(h):
        ak = jnp.concatenate([ref[:, lanes(h)] for ref in anchor_refs], axis=0)
        ak = jnp.where(root, jnp.broadcast_to(k_ref[0:1, lanes(h)], ak.shape), ak)
        av = jnp.concatenate([ref[:, lanes(heads + h)] for ref in anchor_refs], axis=0)
        hidden = (av > 100.0) | root
        vs_ref[h, 0:rows, :HEAD_SIZE] = jnp.where(hidden, jnp.zeros_like(av), av)
        vs_ref[h, 0:rows, HEAD_SIZE:] = jnp.where(hidden, jnp.zeros_like(av), jnp.ones_like(av))
        vs_ref[h, rows:, :HEAD_SIZE] = v_ref[:, lanes(h)]
        vs_ref[h, rows:, HEAD_SIZE:] = jnp.ones((rows, HEAD_SIZE), jnp.bfloat16)
        return ak

    def scores(h, top, g, ak):
        keys = top + half
        q = jnp.concatenate([q_ref[top:keys, lanes(g + i)] for i in range(STACK)], axis=0)
        sa = dot_nt(q, ak)
        so = dot_nt(q, k_ref[0:keys, lanes(h)])
        tiles = [sa[:, i : i + half] for i in range(0, rows, half)]
        tiles += [so[:, i : i + half] for i in range(0, top, half)]
        return tiles + [so[:, top:keys] + causal]

    def finish(index, h, top, g, tiles):
        keys = top + half
        live = (top + lax.broadcasted_iota(jnp.int32, (half, HEAD_SIZE), 0)) < own_len
        peak = jnp.max(functools.reduce(jnp.maximum, tiles), axis=1, keepdims=True)
        weights = [jnp.exp2((tile - peak) * c).astype(jnp.bfloat16) for tile in tiles]
        acc = dot_nn(jnp.concatenate(weights, axis=1), vs_ref[h, 0 : rows + keys, :])
        total = acc[:, HEAD_SIZE:]
        inverse = pl.reciprocal(total, approx=True)
        inverse = inverse * (2.0 - total * inverse)
        out = acc[:, :HEAD_SIZE] * inverse
        for i in range(STACK):
            part = jnp.where(live, out[i * half : (i + 1) * half], 0.0)
            out_ref[top:keys, lanes(g + i)] = part.astype(jnp.bfloat16)
        where = (slice(top, keys), slice(g * HEAD_SIZE, (g + STACK) * HEAD_SIZE))
        copy = pltpu.make_async_copy(out_ref.at[where], o_ref.at[where], sems.at[index])
        copy.start()
        return copy

    work = [
        (h, top, h * GROUP + g) for h in range(heads) for top in (half, 0) for g in range(0, GROUP, STACK)
    ]
    ak = load(0)
    tiles = scores(*work[0], ak)
    copies = []
    for i, item in enumerate(work):
        later = None
        if i + 1 < len(work):
            if work[i + 1][0] != item[0]:
                ak = load(work[i + 1][0])
            later = scores(*work[i + 1], ak)
        copies.append(finish(i, *item, tiles))
        tiles = later
    for copy in copies:
        copy.wait()


def context_attention(own_len, q, k, v, anchor, own_rows):
    rows, width = q.shape
    heads = k.shape[1] // HEAD_SIZE
    vmem = pl.BlockSpec(memory_space=pltpu.VMEM)
    tiles = 2 * heads * GROUP // STACK
    return pl.pallas_call(
        functools.partial(context_kernel, len(anchor)),
        out_shape=[
            jax.ShapeDtypeStruct((rows, width), jnp.bfloat16),
            jax.ShapeDtypeStruct((own_rows, width), jnp.bfloat16),
        ],
        in_specs=[pl.BlockSpec(memory_space=pltpu.SMEM)] + [vmem] * (3 + len(anchor)),
        out_specs=[pl.BlockSpec(memory_space=pl.ANY), vmem],
        scratch_shapes=[
            pltpu.VMEM((heads, 2 * rows, 2 * HEAD_SIZE), jnp.bfloat16),
            pltpu.VMEM((rows, width), jnp.bfloat16),
            pltpu.SemaphoreType.DMA((tiles,)),
        ],
        compiler_params=pltpu.CompilerParams(vmem_limit_bytes=VMEM_LIMIT),
        cost_estimate=pl.CostEstimate(
            flops=8 * rows * width * rows, bytes_accessed=5 * 2**20, transcendentals=2 * rows * rows * heads * GROUP
        ),
        name="context_attention",
    )(own_len, q, k, v, *anchor)


def mark_kernel(n_x, len_ref, k_ref, v_ref, rk_ref, rv_ref, *o_refs):
    rows, width = k_ref.shape
    own = rk_ref.shape[0]
    slab = rows // n_x
    first = jnp.broadcast_to(k_ref[0:1, :], (slab, width))
    for i, o_ref in enumerate(o_refs[:n_x]):
        span = slice(i * slab, (i + 1) * slab)
        valid = (i * slab + lax.broadcasted_iota(jnp.int32, first.shape, 0)) < len_ref[0]
        o_ref[:, :width] = jnp.where(valid, k_ref[span, :], first)
        o_ref[:, width:] = jnp.where(valid, v_ref[span, :], jnp.full_like(first, MARK))
    lines = o_refs[n_x:]
    valid = lax.broadcasted_iota(jnp.int32, (rows, HEAD_SIZE), 0) < len_ref[0]
    y = lax.axis_index("y")
    for i, o_ref in enumerate(lines):
        head = lax.rem(y + i, len(lines))
        lanes = pl.ds(pl.multiple_of(head * HEAD_SIZE, HEAD_SIZE), HEAD_SIZE)
        first = k_ref[0:1, lanes]
        o_ref[0:rows, :] = jnp.where(valid, k_ref[:, lanes], jnp.broadcast_to(first, valid.shape))
        o_ref[rows : rows + own, :] = rk_ref[:, lanes]
        mark = jnp.full((rows, HEAD_SIZE), MARK, jnp.bfloat16)
        o_ref[rows + own : 2 * rows + own, :] = jnp.where(valid, v_ref[:, lanes], mark)
        o_ref[2 * rows + own :, :] = rv_ref[:, lanes]


def pack_kernel(n_y, rq_ref, o_ref):
    own, width = rq_ref.shape
    targets = o_ref.shape[0] // 2
    some = o_ref.shape[1] // own
    for j in range(targets):
        x, y = j // n_y, j % n_y
        for c in range(2):
            for i in range(some):
                lane = c * (width // 2) + (GROUP * y + some * x + i) * HEAD_SIZE
                o_ref[2 * j + c, i * own : (i + 1) * own, :] = rq_ref[:, lane : lane + HEAD_SIZE]


def prepare_kernel(n_x, n_y, len_ref, rq_ref, k_ref, v_ref, rk_ref, rv_ref, sent_ref, *o_refs):
    pack_kernel(n_y, rq_ref, sent_ref)
    mark_kernel(n_x, len_ref, k_ref, v_ref, rk_ref, rv_ref, *o_refs)


def prepare(own_len, rq, k, v, rk, rv, n_x, n_y):
    rows, width = k.shape
    vmem = pl.BlockSpec(memory_space=pltpu.VMEM)
    targets = 2 * n_x * n_y
    shapes = [jax.ShapeDtypeStruct((targets, rq.size // (targets * HEAD_SIZE), HEAD_SIZE), k.dtype)]
    shapes += [jax.ShapeDtypeStruct((rows // n_x, 2 * width), k.dtype)] * n_x
    shapes += [jax.ShapeDtypeStruct((2 * (rows + rk.shape[0]), HEAD_SIZE), k.dtype)] * n_y
    out = pl.pallas_call(
        functools.partial(prepare_kernel, n_x, n_y),
        out_shape=shapes,
        in_specs=[pl.BlockSpec(memory_space=pltpu.SMEM)] + [vmem] * 5,
        out_specs=[vmem] * len(shapes),
        compiler_params=pltpu.CompilerParams(vmem_limit_bytes=56 * 1024 * 1024),
        cost_estimate=pl.CostEstimate(flops=2**18, bytes_accessed=5 * 2**19, transcendentals=0),
        name="prepare",
    )(own_len, rq, k, v, rk, rv)
    return out[0], out[1 : 1 + n_x], out[1 + n_x :]


def plane_kernel(owner_ref, x_ref, o_ref):
    own = 16
    source = 2 * lax.rem(owner_ref[0], N_X * N_Y)
    parts = []
    for i in range(x_ref.shape[1] // own):
        pick = slice(i * own, (i + 1) * own)
        parts += [x_ref[source, pick, :], x_ref[source + 1, pick, :]]
    part = jnp.concatenate(parts, axis=0)
    for z in range(o_ref.shape[0]):
        o_ref[z] = part


def line_kernel(owner_ref, x_ref, o_ref):
    o_ref[...] = x_ref[x_ref.shape[0] - 1 - lax.div(owner_ref[0], N_X * N_Y)]


def choose(kernel, owner, x, shape, flops):
    vmem = pl.BlockSpec(memory_space=pltpu.VMEM)
    return pl.pallas_call(
        kernel,
        out_shape=jax.ShapeDtypeStruct(shape, x.dtype),
        in_specs=[pl.BlockSpec(memory_space=pltpu.SMEM), vmem],
        out_specs=vmem,
        compiler_params=pltpu.CompilerParams(vmem_limit_bytes=VMEM_LIMIT),
        cost_estimate=pl.CostEstimate(flops=flops, bytes_accessed=2**19, transcendentals=0),
        name="choose",
    )(owner, x)


def split3(x):
    high = x.astype(jnp.bfloat16).astype(jnp.float32)
    rest = x - high
    mid = rest.astype(jnp.bfloat16).astype(jnp.float32)
    low = (rest - mid).astype(jnp.bfloat16).astype(jnp.float32)
    return high, mid, low


def code_rows(pair, last, height):
    row = lax.broadcasted_iota(jnp.int32, (height, HEAD_SIZE), 0)
    return jnp.where(row == 0, pair, jnp.where(row == 1, last, 0.0)).astype(jnp.bfloat16)


def request_kernel(own, count, owner_ref, *refs):
    q_refs, lines = refs[:count], refs[count : -count - 1]
    o_refs, v_ref = refs[-count - 1 : -1], refs[-1]
    piece = q_refs[0].shape[0]
    n = count * piece
    both = lines[0].shape[0] // 2
    rows = both - own
    c = SCALE * LOG2E
    q = jnp.concatenate([ref[...] for ref in q_refs], axis=0)
    for i, ref in enumerate(lines):
        part = ref[both : both + rows, :]
        hidden = part > 100.0
        top = i * rows
        v_ref[top : top + rows, :HEAD_SIZE] = jnp.where(hidden, jnp.zeros_like(part), part)
        v_ref[top : top + rows, HEAD_SIZE:] = jnp.where(hidden, jnp.zeros_like(part), jnp.ones_like(part))
        top = len(lines) * rows + i * own
        v_ref[top : top + own, :HEAD_SIZE] = ref[both + rows :, :]
        v_ref[top : top + own, HEAD_SIZE:] = jnp.ones((own, HEAD_SIZE), jnp.bfloat16)
    owner = owner_ref[0]
    same = lax.div(owner, N_Y) == lax.div(place(), N_Y)
    asked = jnp.where(same, lax.rem(lax.axis_index("y") - lax.rem(owner, N_Y) + N_Y, N_Y), -1)
    own_keys = jnp.concatenate([ref[rows:both, :] for ref in lines], axis=0)
    row = lax.rem(lax.broadcasted_iota(jnp.int32, (n, own_keys.shape[0]), 0), own)
    col = lax.broadcasted_iota(jnp.int32, (n, own_keys.shape[0]), 1) - asked * own
    scores = [dot_nt(q, ref[0:rows, :]) for ref in lines]
    scores.append(jnp.where((asked >= 0) & (col >= 0) & (col <= row), dot_nt(q, own_keys), -jnp.inf))
    tiles = [s[:, i : i + HEAD_SIZE] for s in scores for i in range(0, s.shape[1], HEAD_SIZE)]
    peak = jnp.max(functools.reduce(jnp.maximum, tiles), axis=1, keepdims=True)
    weights = [jnp.exp2((tile - peak) * c).astype(jnp.bfloat16) for tile in tiles]
    acc = dot_nn(jnp.concatenate(weights, axis=1), v_ref[...])
    total = acc[:, HEAD_SIZE:]
    out = acc[:, :HEAD_SIZE] / total
    out_high = out.astype(jnp.bfloat16)
    out_low = (out - out_high.astype(jnp.float32)).astype(jnp.bfloat16)
    lse = peak * SCALE + jnp.log(total)
    high, mid, low = split3(lse)
    row = lax.broadcasted_iota(jnp.int32, (piece, HEAD_SIZE), 0)
    lane = lax.broadcasted_iota(jnp.int32, (piece, HEAD_SIZE), 1)
    for p, o_ref in enumerate(o_refs):
        part = slice(p * piece, (p + 1) * piece)
        pair = jnp.where(row == lane, high[part], jnp.where(row + piece == lane, mid[part], 0.0))
        last = jnp.where(row == lane, low[part], 0.0)
        o_ref[0:piece, :] = out_high[part]
        o_ref[piece : 2 * piece, :] = out_low[part]
        o_ref[2 * piece :, :] = code_rows(
            jnp.sum(pair, axis=0, keepdims=True), jnp.sum(last, axis=0, keepdims=True), 16
        )


def request_partials(owner, queries, lines, own):
    count, piece = len(queries), queries[0].shape[0]
    keys = len(lines) * lines[0].shape[0] // 2
    vmem = pl.BlockSpec(memory_space=pltpu.VMEM)
    return pl.pallas_call(
        functools.partial(request_kernel, own, count),
        out_shape=[jax.ShapeDtypeStruct((2 * piece + 16, HEAD_SIZE), jnp.bfloat16)] * count,
        in_specs=[pl.BlockSpec(memory_space=pltpu.SMEM)] + [vmem] * (count + len(lines)),
        out_specs=[vmem] * count,
        scratch_shapes=[pltpu.VMEM((keys, 2 * HEAD_SIZE), jnp.bfloat16)],
        compiler_params=pltpu.CompilerParams(vmem_limit_bytes=VMEM_LIMIT),
        cost_estimate=pl.CostEstimate(
            flops=3 * 10**9, bytes_accessed=2**20, transcendentals=count * piece * keys
        ),
        name="request_partials",
    )(owner, *queries, *lines)


def join_kernel(parts_in, keep_code, *refs):
    x_refs, o_ref = refs[:-1], refs[-1]
    if len(x_refs) == 1:
        x_refs = [x_refs[0].at[i] for i in range(x_refs[0].shape[0])]
    height = x_refs[0].shape[0]
    top = height - 16
    piece = top // parts_in
    count = max(len(x_refs), 8)
    row = lax.broadcasted_iota(jnp.int32, (count, HEAD_SIZE), 0)
    lane = lax.broadcasted_iota(jnp.int32, (count, HEAD_SIZE), 1)
    pair = jnp.zeros((count, HEAD_SIZE), jnp.float32)
    last = jnp.zeros((count, HEAD_SIZE), jnp.float32)
    for i, ref in enumerate(x_refs):
        code = ref[top:height, :].astype(jnp.float32)
        pair = jnp.where(row == i, code[0:1, :], pair)
        last = jnp.where(row == i, code[1:2, :], last)
    lse = jnp.where(lane < piece, pair + pltpu.roll(pair, piece, 1) + last, 0.0)
    lse = jnp.where(row < len(x_refs), lse, -jnp.inf)
    peak = jnp.max(lse, axis=0, keepdims=True)
    weight = jnp.exp(lse - peak)
    total = jnp.sum(weight, axis=0, keepdims=True)
    column = jnp.transpose(weight / total)
    out = jnp.zeros((piece, HEAD_SIZE), jnp.float32)
    for i, ref in enumerate(x_refs):
        part = ref[0:piece, :].astype(jnp.float32)
        if parts_in > 1:
            part = part + ref[piece:top, :].astype(jnp.float32)
        out = out + column[0:piece, i : i + 1] * part
    parts = [out.astype(jnp.bfloat16)]
    if keep_code:
        high, mid, low = split3(peak + jnp.log(total))
        pair = jnp.where(lane[0:1] < piece, high, pltpu.roll(mid, piece, 1))
        parts.append(code_rows(pair, low, 16))
    part = jnp.concatenate(parts, axis=0)
    if len(o_ref.shape) == 2:
        o_ref[...] = part
    else:
        for i in range(o_ref.shape[0]):
            o_ref[i] = part


def join(arrays, copies, parts_in, keep_code):
    height = (arrays[0].shape[-2] - 16) // parts_in + (16 if keep_code else 0)
    shape = (copies, height, HEAD_SIZE) if copies else (height, HEAD_SIZE)
    return pl.pallas_call(
        functools.partial(join_kernel, parts_in, keep_code),
        out_shape=jax.ShapeDtypeStruct(shape, jnp.bfloat16),
        compiler_params=pltpu.CompilerParams(vmem_limit_bytes=VMEM_LIMIT),
        cost_estimate=pl.CostEstimate(flops=3 * 10**9, bytes_accessed=2**19, transcendentals=1024),
        name="join_pieces",
    )(*arrays)


def answer_kernel(owner_ref, x_ref, _, o_ref, rows_ref, sem):
    own = rows_ref.shape[0]
    some = x_ref.shape[1] // own

    @pl.when(place() == owner_ref[0])
    def _():
        for j in range(x_ref.shape[0]):
            x, y = j // N_Y, j % N_Y
            for i in range(some):
                lane = (GROUP * y + some * x + i) * HEAD_SIZE
                rows_ref[:, lane : lane + HEAD_SIZE] = x_ref[j, i * own : (i + 1) * own, :]
        copy = pltpu.make_async_copy(rows_ref, o_ref, sem)
        copy.start()
        copy.wait()


def answer_rows(owner, x, zeros):
    any_spec = pl.BlockSpec(memory_space=pl.ANY)
    return pl.pallas_call(
        answer_kernel,
        out_shape=jax.ShapeDtypeStruct(zeros.shape, zeros.dtype),
        in_specs=[pl.BlockSpec(memory_space=pltpu.SMEM), pl.BlockSpec(memory_space=pltpu.VMEM), any_spec],
        out_specs=any_spec,
        input_output_aliases={2: 0},
        scratch_shapes=[pltpu.VMEM(zeros.shape, zeros.dtype), pltpu.SemaphoreType.DMA],
        compiler_params=pltpu.CompilerParams(vmem_limit_bytes=VMEM_LIMIT),
        cost_estimate=pl.CostEstimate(flops=2**18, bytes_accessed=2**19, transcendentals=0),
        name="answer_rows",
    )(owner, x, zeros)


def exchange(x, axis, groups=None):
    return lax.all_to_all(x, axis, split_axis=0, concat_axis=0, axis_index_groups=groups, tiled=True)


def local(n_z, n_x, n_y, q, k, v, block_lengths, rq, rk, rv, query_owner):
    n_xy = n_x * n_y
    z, x, y = (lax.axis_index(name) for name in ("z", "x", "y"))
    own_len = block_lengths
    own_rows = rk.shape[0]
    down = [list(range(n_z))[::-1]]

    def move(value, pairs):
        return lax.ppermute(value, ("z", "x", "y"), pairs)

    def shift_x(value, count):
        return lax.ppermute(value, "x", [(a, (a + count) % n_x) for a in range(n_x)])

    sent, pieces, lines = prepare(own_len, rq, k, v, rk, rv, n_x, n_y)
    moved = exchange(sent, ("x", "y", "head"))
    got = [move(pieces[i], [(0, i * n_y)]) for i in range(1, n_x)]
    lines = [lines[0]] + [
        lax.ppermute(lines[i], "y", [(a, (a + i) % n_y) for a in range(n_y)]) for i in range(1, n_y)
    ]

    piece = (2 * moved.shape[1], HEAD_SIZE)
    moved, got = lax.optimization_barrier((moved, got))
    moved = choose(plane_kernel, query_owner, moved, (n_z,) + piece, 8 * 10**8)
    anchor = jnp.where(x == 0, pieces[0], got[0] + got[1] + got[2])
    got = [move(anchor, [(i * n_y, (to * n_x + i) * n_y) for i in range(n_x)]) for to in (3, 5)]
    moved = exchange(moved, "z", down)

    moved = choose(line_kernel, query_owner, moved, piece, 3 * 10**9)
    moved, lines = lax.optimization_barrier((moved, lines))
    anchor = jnp.where(z == 0, anchor, got[0] + got[1])
    rows = [(to * n_x + i) * n_y for to in (0, 3, 5) for i in range(n_x)]
    got = [move(anchor, [(p, p + j) for p in rows]) for j in range(1, n_y)]
    queries = [moved] + [shift_x(moved, i) for i in range(1, n_x)]

    partials = request_partials(query_owner, queries, lines, own_rows)
    anchor = jnp.where(y == 0, anchor, got[0] + got[1] + got[2])
    plane = range(n_xy)
    steps = (((0, 1), (3, 4), (5, 6)), ((3, 2), (5, 7)))
    got = [move(anchor, [(a * n_xy + p, b * n_xy + p) for a, b in step for p in plane]) for step in steps]
    partials = [partials[0]] + [shift_x(partials[i], n_x - i) for i in range(1, n_x)]

    planes = join(partials, n_z, 2, True)
    anchor = jnp.where((z == 0) | (z == 3) | (z == 5), anchor, got[0] + got[1])
    anchors = [anchor]
    for i in range(1, n_x):
        anchors.append(shift_x(anchor, i))
    planes = exchange(planes, "z", down)

    answer = exchange(join([planes], n_xy, 1, False), ("x", "y"))
    context_output, zeros = context_attention(own_len, q, k, v, anchors, own_rows)
    request_output = answer_rows(query_owner, answer, zeros)
    return context_output, request_output


def solution(mesh):
    n_z, n_x, n_y = 8, N_X, N_Y
    grid = jax.sharding.Mesh(mesh.devices.reshape(n_z, n_x, n_y, 2), ("z", "x", "y", "head"))
    ctx = ("z", "x", "y")
    in_specs = (
        P(ctx, "head"),
        P(ctx, "head"),
        P(ctx, "head"),
        P(ctx),
        P(ctx + ("head",), None),
        P(ctx, "head"),
        P(ctx, "head"),
        P(),
    )
    out_specs = (P(ctx, "head"), P(ctx, "head"))
    return jax.shard_map(
        functools.partial(local, n_z, n_x, n_y),
        mesh=grid,
        in_specs=in_specs,
        out_specs=out_specs,
        check_vma=False,
    )
```

```python
import functools

import jax
import jax.numpy as jnp
from jax import lax
from jax.experimental import pallas as pl
from jax.experimental.pallas import tpu as pltpu
from jax.sharding import PartitionSpec as P

HEAD_SIZE = 128
GROUP = 8
SCALE = HEAD_SIZE**-0.5
LOG2E = 1.4426950408889634
LN2 = 0.6931471805599453
MARK = 1024.0
VMEM_LIMIT = 32 * 1024 * 1024
STACK = 4
N_X, N_Y = 4, 4
PLANES = (4, 2, 1, 7, 6, 5, 3, 0)
SWAPS = (0, 3, 2, 1)


def place():
    return (lax.axis_index("z") * N_X + lax.axis_index("x")) * N_Y + lax.axis_index("y")


def dot_nt(a, b):
    return lax.dot_general(a, b, (((1,), (1,)), ((), ())), preferred_element_type=jnp.float32)


def dot_nn(a, b):
    return lax.dot_general(a, b, (((1,), (0,)), ((), ())), preferred_element_type=jnp.float32)


def context_kernel(count, len_ref, q_ref, k_ref, v_ref, *refs):
    anchor_refs = refs[:count]
    o_ref, zero_ref, vs_ref, out_ref, sems = refs[-5:]
    zero_ref[...] = jnp.zeros_like(zero_ref)
    rows, width = k_ref.shape
    half = rows // 2
    heads = width // HEAD_SIZE
    own_len = len_ref[0]
    root = place() == 0
    c = SCALE * LOG2E
    row = lax.broadcasted_iota(jnp.int32, (STACK * half, half), 0)
    col = lax.broadcasted_iota(jnp.int32, (STACK * half, half), 1)
    causal = jnp.where(col <= lax.rem(row, half), 0.0, -jnp.inf).astype(jnp.float32)

    def lanes(g):
        return slice(g * HEAD_SIZE, (g + 1) * HEAD_SIZE)

    def load(h):
        ak = jnp.concatenate([ref[:, lanes(h)] for ref in anchor_refs], axis=0)
        ak = jnp.where(root, jnp.broadcast_to(k_ref[0:1, lanes(h)], ak.shape), ak)
        av = jnp.concatenate([ref[:, lanes(heads + h)] for ref in anchor_refs], axis=0)
        hidden = (av > 100.0) | root
        vs_ref[h, 0:rows, :HEAD_SIZE] = jnp.where(hidden, jnp.zeros_like(av), av)
        vs_ref[h, 0:rows, HEAD_SIZE:] = jnp.where(hidden, jnp.zeros_like(av), jnp.ones_like(av))
        vs_ref[h, rows:, :HEAD_SIZE] = v_ref[:, lanes(h)]
        vs_ref[h, rows:, HEAD_SIZE:] = jnp.ones((rows, HEAD_SIZE), jnp.bfloat16)
        return ak

    def scores(h, top, g, ak):
        keys = top + half
        q = jnp.concatenate([q_ref[top:keys, lanes(g + i)] for i in range(STACK)], axis=0)
        sa = dot_nt(q, ak)
        so = dot_nt(q, k_ref[0:keys, lanes(h)])
        tiles = [sa[:, i : i + half] for i in range(0, rows, half)]
        tiles += [so[:, i : i + half] for i in range(0, top, half)]
        return tiles + [so[:, top:keys] + causal]

    def finish(index, h, top, g, tiles):
        keys = top + half
        live = (top + lax.broadcasted_iota(jnp.int32, (half, HEAD_SIZE), 0)) < own_len
        peak = jnp.max(functools.reduce(jnp.maximum, tiles), axis=1, keepdims=True)
        weights = [jnp.exp2((tile - peak) * c).astype(jnp.bfloat16) for tile in tiles]
        acc = dot_nn(jnp.concatenate(weights, axis=1), vs_ref[h, 0 : rows + keys, :])
        total = acc[:, HEAD_SIZE:]
        inverse = pl.reciprocal(total, approx=True)
        inverse = inverse * (2.0 - total * inverse)
        out = acc[:, :HEAD_SIZE] * inverse
        for i in range(STACK):
            part = jnp.where(live, out[i * half : (i + 1) * half], 0.0)
            out_ref[top:keys, lanes(g + i)] = part.astype(jnp.bfloat16)
        where = (slice(top, keys), slice(g * HEAD_SIZE, (g + STACK) * HEAD_SIZE))
        copy = pltpu.make_async_copy(out_ref.at[where], o_ref.at[where], sems.at[index])
        copy.start()
        return copy

    work = [
        (h, top, h * GROUP + g) for h in range(heads) for top in (half, 0) for g in range(0, GROUP, STACK)
    ]
    ak = load(0)
    tiles = scores(*work[0], ak)
    copies = []
    for i, item in enumerate(work):
        later = None
        if i + 1 < len(work):
            if work[i + 1][0] != item[0]:
                ak = load(work[i + 1][0])
            later = scores(*work[i + 1], ak)
        copies.append(finish(i, *item, tiles))
        tiles = later
    for copy in copies:
        copy.wait()


def context_attention(own_len, q, k, v, anchor, own_rows):
    rows, width = q.shape
    heads = k.shape[1] // HEAD_SIZE
    vmem = pl.BlockSpec(memory_space=pltpu.VMEM)
    tiles = 2 * heads * GROUP // STACK
    return pl.pallas_call(
        functools.partial(context_kernel, len(anchor)),
        out_shape=[
            jax.ShapeDtypeStruct((rows, width), jnp.bfloat16),
            jax.ShapeDtypeStruct((own_rows, width), jnp.bfloat16),
        ],
        in_specs=[pl.BlockSpec(memory_space=pltpu.SMEM)] + [vmem] * (3 + len(anchor)),
        out_specs=[pl.BlockSpec(memory_space=pl.ANY), vmem],
        scratch_shapes=[
            pltpu.VMEM((heads, 2 * rows, 2 * HEAD_SIZE), jnp.bfloat16),
            pltpu.VMEM((rows, width), jnp.bfloat16),
            pltpu.SemaphoreType.DMA((tiles,)),
        ],
        compiler_params=pltpu.CompilerParams(vmem_limit_bytes=VMEM_LIMIT),
        cost_estimate=pl.CostEstimate(
            flops=8 * rows * width * rows, bytes_accessed=5 * 2**20, transcendentals=2 * rows * rows * heads * GROUP
        ),
        name="context_attention",
    )(own_len, q, k, v, *anchor)


def mark_kernel(n_x, len_ref, k_ref, v_ref, rk_ref, rv_ref, *o_refs):
    rows, width = k_ref.shape
    own = rk_ref.shape[0]
    slab = rows // n_x
    first = jnp.broadcast_to(k_ref[0:1, :], (slab, width))
    for i, o_ref in enumerate(o_refs[:n_x]):
        span = slice(i * slab, (i + 1) * slab)
        valid = (i * slab + lax.broadcasted_iota(jnp.int32, first.shape, 0)) < len_ref[0]
        o_ref[:, :width] = jnp.where(valid, k_ref[span, :], first)
        o_ref[:, width:] = jnp.where(valid, v_ref[span, :], jnp.full_like(first, MARK))
    lines = o_refs[n_x:]
    valid = lax.broadcasted_iota(jnp.int32, (rows, HEAD_SIZE), 0) < len_ref[0]
    y = lax.axis_index("y")
    for i, o_ref in enumerate(lines):
        head = y ^ SWAPS[i]
        lanes = pl.ds(pl.multiple_of(head * HEAD_SIZE, HEAD_SIZE), HEAD_SIZE)
        first = k_ref[0:1, lanes]
        o_ref[0:rows, :] = jnp.where(valid, k_ref[:, lanes], jnp.broadcast_to(first, valid.shape))
        o_ref[rows : rows + own, :] = rk_ref[:, lanes]
        mark = jnp.full((rows, HEAD_SIZE), MARK, jnp.bfloat16)
        o_ref[rows + own : 2 * rows + own, :] = jnp.where(valid, v_ref[:, lanes], mark)
        o_ref[2 * rows + own :, :] = rv_ref[:, lanes]


def pack_kernel(n_y, rq_ref, o_ref):
    own, width = rq_ref.shape
    targets = o_ref.shape[0] // 2
    some = o_ref.shape[1] // own
    for j in range(targets):
        x, y = j // n_y, j % n_y
        for c in range(2):
            for i in range(some):
                lane = c * (width // 2) + (GROUP * y + some * x + i) * HEAD_SIZE
                o_ref[2 * j + c, i * own : (i + 1) * own, :] = rq_ref[:, lane : lane + HEAD_SIZE]


def prepare_kernel(n_x, n_y, len_ref, rq_ref, k_ref, v_ref, rk_ref, rv_ref, sent_ref, *o_refs):
    pack_kernel(n_y, rq_ref, sent_ref)
    mark_kernel(n_x, len_ref, k_ref, v_ref, rk_ref, rv_ref, *o_refs)


def prepare(own_len, rq, k, v, rk, rv, n_x, n_y):
    rows, width = k.shape
    vmem = pl.BlockSpec(memory_space=pltpu.VMEM)
    targets = 2 * n_x * n_y
    shapes = [jax.ShapeDtypeStruct((targets, rq.size // (targets * HEAD_SIZE), HEAD_SIZE), k.dtype)]
    shapes += [jax.ShapeDtypeStruct((rows // n_x, 2 * width), k.dtype)] * n_x
    shapes += [jax.ShapeDtypeStruct((2 * (rows + rk.shape[0]), HEAD_SIZE), k.dtype)] * n_y
    out = pl.pallas_call(
        functools.partial(prepare_kernel, n_x, n_y),
        out_shape=shapes,
        in_specs=[pl.BlockSpec(memory_space=pltpu.SMEM)] + [vmem] * 5,
        out_specs=[vmem] * len(shapes),
        compiler_params=pltpu.CompilerParams(vmem_limit_bytes=56 * 1024 * 1024),
        cost_estimate=pl.CostEstimate(flops=2**18, bytes_accessed=5 * 2**19, transcendentals=0),
        name="prepare",
    )(own_len, rq, k, v, rk, rv)
    return out[0], out[1 : 1 + n_x], out[1 + n_x :]


def plane_kernel(owner_ref, x_ref, o_ref):
    own = 16
    source = 2 * lax.rem(owner_ref[0], N_X * N_Y)
    parts = []
    for i in range(x_ref.shape[1] // own):
        pick = slice(i * own, (i + 1) * own)
        parts += [x_ref[source, pick, :], x_ref[source + 1, pick, :]]
    part = jnp.concatenate(parts, axis=0)
    for z in range(o_ref.shape[0]):
        o_ref[z] = part


def line_kernel(owner_ref, x_ref, o_ref):
    owner_z = lax.div(owner_ref[0], N_X * N_Y)
    spot = 0
    for i, z in enumerate(PLANES):
        spot = jnp.where(owner_z == z, i, spot)
    o_ref[...] = x_ref[spot]


def choose(kernel, owner, x, shape, flops):
    vmem = pl.BlockSpec(memory_space=pltpu.VMEM)
    return pl.pallas_call(
        kernel,
        out_shape=jax.ShapeDtypeStruct(shape, x.dtype),
        in_specs=[pl.BlockSpec(memory_space=pltpu.SMEM), vmem],
        out_specs=vmem,
        compiler_params=pltpu.CompilerParams(vmem_limit_bytes=VMEM_LIMIT),
        cost_estimate=pl.CostEstimate(flops=flops, bytes_accessed=2**19, transcendentals=0),
        name="choose",
    )(owner, x)


def split3(x):
    high = x.astype(jnp.bfloat16).astype(jnp.float32)
    rest = x - high
    mid = rest.astype(jnp.bfloat16).astype(jnp.float32)
    low = (rest - mid).astype(jnp.bfloat16).astype(jnp.float32)
    return high, mid, low


def code_rows(pair, last, height):
    row = lax.broadcasted_iota(jnp.int32, (height, HEAD_SIZE), 0)
    return jnp.where(row == 0, pair, jnp.where(row == 1, last, 0.0)).astype(jnp.bfloat16)


def request_kernel(own, count, owner_ref, *refs):
    q_refs, lines = refs[:count], refs[count : -count - 1]
    o_refs, v_ref = refs[-count - 1 : -1], refs[-1]
    piece = q_refs[0].shape[0]
    n = count * piece
    both = lines[0].shape[0] // 2
    rows = both - own
    c = SCALE * LOG2E
    q = jnp.concatenate([ref[...] for ref in q_refs], axis=0)
    for i, ref in enumerate(lines):
        part = ref[both : both + rows, :]
        hidden = part > 100.0
        top = i * rows
        v_ref[top : top + rows, :HEAD_SIZE] = jnp.where(hidden, jnp.zeros_like(part), part)
        v_ref[top : top + rows, HEAD_SIZE:] = jnp.where(hidden, jnp.zeros_like(part), jnp.ones_like(part))
        top = len(lines) * rows + i * own
        v_ref[top : top + own, :HEAD_SIZE] = ref[both + rows :, :]
        v_ref[top : top + own, HEAD_SIZE:] = jnp.ones((own, HEAD_SIZE), jnp.bfloat16)
    owner = owner_ref[0]
    same = lax.div(owner, N_Y) == lax.div(place(), N_Y)
    apart = lax.axis_index("y") ^ lax.rem(owner, N_Y)
    asked = jnp.where(same, jnp.where(apart == 0, 0, N_Y - apart), -1)
    own_keys = jnp.concatenate([ref[rows:both, :] for ref in lines], axis=0)
    row = lax.rem(lax.broadcasted_iota(jnp.int32, (n, own_keys.shape[0]), 0), own)
    col = lax.broadcasted_iota(jnp.int32, (n, own_keys.shape[0]), 1) - asked * own
    scores = [dot_nt(q, ref[0:rows, :]) for ref in lines]
    scores.append(jnp.where((asked >= 0) & (col >= 0) & (col <= row), dot_nt(q, own_keys), -jnp.inf))
    tiles = [s[:, i : i + HEAD_SIZE] for s in scores for i in range(0, s.shape[1], HEAD_SIZE)]
    peak = jnp.max(functools.reduce(jnp.maximum, tiles), axis=1, keepdims=True)
    weights = [jnp.exp2((tile - peak) * c).astype(jnp.bfloat16) for tile in tiles]
    acc = dot_nn(jnp.concatenate(weights, axis=1), v_ref[...])
    total = acc[:, HEAD_SIZE:]
    out = acc[:, :HEAD_SIZE] / total
    out_high = out.astype(jnp.bfloat16)
    out_low = (out - out_high.astype(jnp.float32)).astype(jnp.bfloat16)
    lse = peak * SCALE + jnp.log(total)
    high, mid, low = split3(lse)
    row = lax.broadcasted_iota(jnp.int32, (piece, HEAD_SIZE), 0)
    lane = lax.broadcasted_iota(jnp.int32, (piece, HEAD_SIZE), 1)
    for p, o_ref in enumerate(o_refs):
        part = slice(p * piece, (p + 1) * piece)
        pair = jnp.where(row == lane, high[part], jnp.where(row + piece == lane, mid[part], 0.0))
        last = jnp.where(row == lane, low[part], 0.0)
        o_ref[0:piece, :] = out_high[part]
        o_ref[piece : 2 * piece, :] = out_low[part]
        o_ref[2 * piece :, :] = code_rows(
            jnp.sum(pair, axis=0, keepdims=True), jnp.sum(last, axis=0, keepdims=True), 16
        )


def request_partials(owner, queries, lines, own):
    count, piece = len(queries), queries[0].shape[0]
    keys = len(lines) * lines[0].shape[0] // 2
    vmem = pl.BlockSpec(memory_space=pltpu.VMEM)
    return pl.pallas_call(
        functools.partial(request_kernel, own, count),
        out_shape=[jax.ShapeDtypeStruct((2 * piece + 16, HEAD_SIZE), jnp.bfloat16)] * count,
        in_specs=[pl.BlockSpec(memory_space=pltpu.SMEM)] + [vmem] * (count + len(lines)),
        out_specs=[vmem] * count,
        scratch_shapes=[pltpu.VMEM((keys, 2 * HEAD_SIZE), jnp.bfloat16)],
        compiler_params=pltpu.CompilerParams(vmem_limit_bytes=VMEM_LIMIT),
        cost_estimate=pl.CostEstimate(
            flops=3 * 10**9, bytes_accessed=2**20, transcendentals=count * piece * keys
        ),
        name="request_partials",
    )(owner, *queries, *lines)


def join_kernel(parts_in, keep_code, *refs):
    x_refs, o_ref = refs[:-1], refs[-1]
    if len(x_refs) == 1:
        x_refs = [x_refs[0].at[i] for i in range(x_refs[0].shape[0])]
    height = x_refs[0].shape[0]
    top = height - 16
    piece = top // parts_in
    count = max(len(x_refs), 8)
    row = lax.broadcasted_iota(jnp.int32, (count, HEAD_SIZE), 0)
    lane = lax.broadcasted_iota(jnp.int32, (count, HEAD_SIZE), 1)
    pair = jnp.zeros((count, HEAD_SIZE), jnp.float32)
    last = jnp.zeros((count, HEAD_SIZE), jnp.float32)
    for i, ref in enumerate(x_refs):
        code = ref[top:height, :].astype(jnp.float32)
        pair = jnp.where(row == i, code[0:1, :], pair)
        last = jnp.where(row == i, code[1:2, :], last)
    lse = jnp.where(lane < piece, pair + pltpu.roll(pair, piece, 1) + last, 0.0)
    lse = jnp.where(row < len(x_refs), lse, -jnp.inf)
    peak = jnp.max(lse, axis=0, keepdims=True)
    weight = jnp.exp(lse - peak)
    total = jnp.sum(weight, axis=0, keepdims=True)
    column = jnp.transpose(weight / total)
    out = jnp.zeros((piece, HEAD_SIZE), jnp.float32)
    for i, ref in enumerate(x_refs):
        part = ref[0:piece, :].astype(jnp.float32)
        if parts_in > 1:
            part = part + ref[piece:top, :].astype(jnp.float32)
        out = out + column[0:piece, i : i + 1] * part
    parts = [out.astype(jnp.bfloat16)]
    if keep_code:
        high, mid, low = split3(peak + jnp.log(total))
        pair = jnp.where(lane[0:1] < piece, high, pltpu.roll(mid, piece, 1))
        parts.append(code_rows(pair, low, 16))
    part = jnp.concatenate(parts, axis=0)
    if len(o_ref.shape) == 2:
        o_ref[...] = part
    else:
        for i in range(o_ref.shape[0]):
            o_ref[i] = part


def join(arrays, copies, parts_in, keep_code):
    height = (arrays[0].shape[-2] - 16) // parts_in + (16 if keep_code else 0)
    shape = (copies, height, HEAD_SIZE) if copies else (height, HEAD_SIZE)
    return pl.pallas_call(
        functools.partial(join_kernel, parts_in, keep_code),
        out_shape=jax.ShapeDtypeStruct(shape, jnp.bfloat16),
        compiler_params=pltpu.CompilerParams(vmem_limit_bytes=VMEM_LIMIT),
        cost_estimate=pl.CostEstimate(flops=3 * 10**9, bytes_accessed=2**19, transcendentals=1024),
        name="join_pieces",
    )(*arrays)


def answer_kernel(owner_ref, x_ref, _, o_ref, rows_ref, sem):
    own = rows_ref.shape[0]
    some = x_ref.shape[1] // own

    @pl.when(place() == owner_ref[0])
    def _():
        for j in range(x_ref.shape[0]):
            x, y = j // N_Y, j % N_Y
            for i in range(some):
                lane = (GROUP * y + some * x + i) * HEAD_SIZE
                rows_ref[:, lane : lane + HEAD_SIZE] = x_ref[j, i * own : (i + 1) * own, :]
        copy = pltpu.make_async_copy(rows_ref, o_ref, sem)
        copy.start()
        copy.wait()


def answer_rows(owner, x, zeros):
    any_spec = pl.BlockSpec(memory_space=pl.ANY)
    return pl.pallas_call(
        answer_kernel,
        out_shape=jax.ShapeDtypeStruct(zeros.shape, zeros.dtype),
        in_specs=[pl.BlockSpec(memory_space=pltpu.SMEM), pl.BlockSpec(memory_space=pltpu.VMEM), any_spec],
        out_specs=any_spec,
        input_output_aliases={2: 0},
        scratch_shapes=[pltpu.VMEM(zeros.shape, zeros.dtype), pltpu.SemaphoreType.DMA],
        compiler_params=pltpu.CompilerParams(vmem_limit_bytes=VMEM_LIMIT),
        cost_estimate=pl.CostEstimate(flops=2**18, bytes_accessed=2**19, transcendentals=0),
        name="answer_rows",
    )(owner, x, zeros)


def exchange(x, axis, groups=None):
    return lax.all_to_all(x, axis, split_axis=0, concat_axis=0, axis_index_groups=groups, tiled=True)


def local(n_z, n_x, n_y, q, k, v, block_lengths, rq, rk, rv, query_owner):
    n_xy = n_x * n_y
    z, x, y = (lax.axis_index(name) for name in ("z", "x", "y"))
    own_len = block_lengths
    own_rows = rk.shape[0]
    down = [list(range(n_z))[::-1]]

    def move(value, pairs):
        return lax.ppermute(value, ("z", "x", "y"), pairs)

    def swap(value, axis, apart):
        return lax.ppermute(value, axis, [(a, a ^ apart) for a in range(4)])

    sent, pieces, lines = prepare(own_len, rq, k, v, rk, rv, n_x, n_y)
    moved = exchange(sent, ("x", "y", "head"))
    got = [move(pieces[i], [(0, i * n_y)]) for i in range(1, n_x)]
    lines = [lines[0]] + [swap(lines[i], "y", SWAPS[i]) for i in range(1, n_y)]

    piece = (2 * moved.shape[1], HEAD_SIZE)
    moved, got = lax.optimization_barrier((moved, got))
    moved = choose(plane_kernel, query_owner, moved, (n_z,) + piece, 8 * 10**8)
    anchor = jnp.where(x == 0, pieces[0], got[0] + got[1] + got[2])
    got = [move(anchor, [(i * n_y, (to * n_x + i) * n_y) for i in range(n_x)]) for to in (3, 5)]
    moved = exchange(moved, "z", [list(PLANES)])

    moved = choose(line_kernel, query_owner, moved, piece, 3 * 10**9)
    moved, lines = lax.optimization_barrier((moved, lines))
    anchor = jnp.where(z == 0, anchor, got[0] + got[1])
    rows = [(to * n_x + i) * n_y for to in (0, 3, 5) for i in range(n_x)]
    got = [move(anchor, [(p, p + j) for p in rows]) for j in range(1, n_y)]
    queries = [moved] + [swap(moved, "x", i) for i in range(1, n_x)]

    partials = request_partials(query_owner, queries, lines, own_rows)
    anchor = jnp.where(y == 0, anchor, got[0] + got[1] + got[2])
    plane = range(n_xy)
    steps = (((0, 1), (3, 4), (5, 6)), ((3, 2), (5, 7)))
    got = [move(anchor, [(a * n_xy + p, b * n_xy + p) for a, b in step for p in plane]) for step in steps]
    partials = [partials[0]] + [swap(partials[i], "x", i) for i in SWAPS[1:]]

    planes = join(partials, n_z, 2, True)
    anchor = jnp.where((z == 0) | (z == 3) | (z == 5), anchor, got[0] + got[1])
    anchors = [anchor]
    for i in range(1, n_x):
        anchors.append(swap(anchor, "x", i))
    planes = exchange(planes, "z", down)

    answer = exchange(join([planes], n_xy, 1, False), ("x", "y"))
    context_output, zeros = context_attention(own_len, q, k, v, anchors, own_rows)
    request_output = answer_rows(query_owner, answer, zeros)
    return context_output, request_output


def solution(mesh):
    n_z, n_x, n_y = 8, N_X, N_Y
    grid = jax.sharding.Mesh(mesh.devices.reshape(n_z, n_x, n_y, 2), ("z", "x", "y", "head"))
    ctx = ("z", "x", "y")
    in_specs = (
        P(ctx, "head"),
        P(ctx, "head"),
        P(ctx, "head"),
        P(ctx),
        P(ctx + ("head",), None),
        P(ctx, "head"),
        P(ctx, "head"),
        P(),
    )
    out_specs = (P(ctx, "head"), P(ctx, "head"))
    return jax.shard_map(
        functools.partial(local, n_z, n_x, n_y),
        mesh=grid,
        in_specs=in_specs,
        out_specs=out_specs,
        check_vma=False,
    )
```

```python
import functools

import jax
import jax.numpy as jnp
from jax import lax
from jax.experimental import pallas as pl
from jax.experimental.pallas import tpu as pltpu
from jax.sharding import PartitionSpec as P

HEAD_SIZE = 128
GROUP = 8
SCALE = HEAD_SIZE**-0.5
LOG2E = 1.4426950408889634
LN2 = 0.6931471805599453
MARK = 1024.0
VMEM_LIMIT = 32 * 1024 * 1024
STACK = 4
N_X, N_Y = 4, 4


def place():
    return (lax.axis_index("z") * N_X + lax.axis_index("x")) * N_Y + lax.axis_index("y")


def dot_nt(a, b):
    return lax.dot_general(a, b, (((1,), (1,)), ((), ())), preferred_element_type=jnp.float32)


def dot_nn(a, b):
    return lax.dot_general(a, b, (((1,), (0,)), ((), ())), preferred_element_type=jnp.float32)


def context_kernel(count, len_ref, q_ref, k_ref, v_ref, *refs):
    anchor_refs = refs[:count]
    o_ref, zero_ref, vs_ref, out_ref, sems = refs[-5:]
    zero_ref[...] = jnp.zeros_like(zero_ref)
    rows, width = k_ref.shape
    half = rows // 2
    heads = width // HEAD_SIZE
    own_len = len_ref[0]
    root = place() == 0
    c = SCALE * LOG2E
    row = lax.broadcasted_iota(jnp.int32, (STACK * half, half), 0)
    col = lax.broadcasted_iota(jnp.int32, (STACK * half, half), 1)
    causal = jnp.where(col <= lax.rem(row, half), 0.0, -jnp.inf).astype(jnp.float32)

    def lanes(g):
        return slice(g * HEAD_SIZE, (g + 1) * HEAD_SIZE)

    def load(h):
        ak = jnp.concatenate([ref[:, lanes(h)] for ref in anchor_refs], axis=0)
        ak = jnp.where(root, jnp.broadcast_to(k_ref[0:1, lanes(h)], ak.shape), ak)
        av = jnp.concatenate([ref[:, lanes(heads + h)] for ref in anchor_refs], axis=0)
        hidden = (av > 100.0) | root
        vs_ref[h, 0:rows, :HEAD_SIZE] = jnp.where(hidden, jnp.zeros_like(av), av)
        vs_ref[h, 0:rows, HEAD_SIZE:] = jnp.where(hidden, jnp.zeros_like(av), jnp.ones_like(av))
        vs_ref[h, rows:, :HEAD_SIZE] = v_ref[:, lanes(h)]
        vs_ref[h, rows:, HEAD_SIZE:] = jnp.ones((rows, HEAD_SIZE), jnp.bfloat16)
        return ak

    def scores(h, top, g, ak):
        keys = top + half
        q = jnp.concatenate([q_ref[top:keys, lanes(g + i)] for i in range(STACK)], axis=0)
        sa = dot_nt(q, ak)
        so = dot_nt(q, k_ref[0:keys, lanes(h)])
        tiles = [sa[:, i : i + half] for i in range(0, rows, half)]
        tiles += [so[:, i : i + half] for i in range(0, top, half)]
        return tiles + [so[:, top:keys] + causal]

    def finish(index, h, top, g, tiles):
        keys = top + half
        live = (top + lax.broadcasted_iota(jnp.int32, (half, HEAD_SIZE), 0)) < own_len
        peak = jnp.max(functools.reduce(jnp.maximum, tiles), axis=1, keepdims=True)
        weights = [jnp.exp2((tile - peak) * c).astype(jnp.bfloat16) for tile in tiles]
        acc = dot_nn(jnp.concatenate(weights, axis=1), vs_ref[h, 0 : rows + keys, :])
        total = acc[:, HEAD_SIZE:]
        inverse = pl.reciprocal(total, approx=True)
        inverse = inverse * (2.0 - total * inverse)
        out = acc[:, :HEAD_SIZE] * inverse
        for i in range(STACK):
            part = jnp.where(live, out[i * half : (i + 1) * half], 0.0)
            out_ref[top:keys, lanes(g + i)] = part.astype(jnp.bfloat16)
        where = (slice(top, keys), slice(g * HEAD_SIZE, (g + STACK) * HEAD_SIZE))
        copy = pltpu.make_async_copy(out_ref.at[where], o_ref.at[where], sems.at[index])
        copy.start()
        return copy

    work = [
        (h, top, h * GROUP + g) for h in range(heads) for top in (half, 0) for g in range(0, GROUP, STACK)
    ]
    ak = load(0)
    tiles = scores(*work[0], ak)
    copies = []
    for i, item in enumerate(work):
        later = None
        if i + 1 < len(work):
            if work[i + 1][0] != item[0]:
                ak = load(work[i + 1][0])
            later = scores(*work[i + 1], ak)
        copies.append(finish(i, *item, tiles))
        tiles = later
    for copy in copies:
        copy.wait()


def context_attention(own_len, q, k, v, anchor, own_rows):
    rows, width = q.shape
    heads = k.shape[1] // HEAD_SIZE
    vmem = pl.BlockSpec(memory_space=pltpu.VMEM)
    tiles = 2 * heads * GROUP // STACK
    return pl.pallas_call(
        functools.partial(context_kernel, len(anchor)),
        out_shape=[
            jax.ShapeDtypeStruct((rows, width), jnp.bfloat16),
            jax.ShapeDtypeStruct((own_rows, width), jnp.bfloat16),
        ],
        in_specs=[pl.BlockSpec(memory_space=pltpu.SMEM)] + [vmem] * (3 + len(anchor)),
        out_specs=[pl.BlockSpec(memory_space=pl.ANY), vmem],
        scratch_shapes=[
            pltpu.VMEM((heads, 2 * rows, 2 * HEAD_SIZE), jnp.bfloat16),
            pltpu.VMEM((rows, width), jnp.bfloat16),
            pltpu.SemaphoreType.DMA((tiles,)),
        ],
        compiler_params=pltpu.CompilerParams(vmem_limit_bytes=VMEM_LIMIT),
        cost_estimate=pl.CostEstimate(
            flops=8 * rows * width * rows, bytes_accessed=5 * 2**20, transcendentals=2 * rows * rows * heads * GROUP
        ),
        name="context_attention",
    )(own_len, q, k, v, *anchor)


def mark_kernel(n_x, len_ref, k_ref, v_ref, rk_ref, rv_ref, *o_refs):
    rows, width = k_ref.shape
    own = rk_ref.shape[0]
    slab = rows // n_x
    first = jnp.broadcast_to(k_ref[0:1, :], (slab, width))
    for i, o_ref in enumerate(o_refs[:n_x]):
        span = slice(i * slab, (i + 1) * slab)
        valid = (i * slab + lax.broadcasted_iota(jnp.int32, first.shape, 0)) < len_ref[0]
        o_ref[:, :width] = jnp.where(valid, k_ref[span, :], first)
        o_ref[:, width:] = jnp.where(valid, v_ref[span, :], jnp.full_like(first, MARK))
    lines = o_refs[n_x:]
    valid = lax.broadcasted_iota(jnp.int32, (rows, HEAD_SIZE), 0) < len_ref[0]
    y = lax.axis_index("y")
    for i, o_ref in enumerate(lines):
        head = lax.rem(y + i, len(lines))
        lanes = pl.ds(pl.multiple_of(head * HEAD_SIZE, HEAD_SIZE), HEAD_SIZE)
        first = k_ref[0:1, lanes]
        o_ref[0:rows, :] = jnp.where(valid, k_ref[:, lanes], jnp.broadcast_to(first, valid.shape))
        o_ref[rows : rows + own, :] = rk_ref[:, lanes]
        mark = jnp.full((rows, HEAD_SIZE), MARK, jnp.bfloat16)
        o_ref[rows + own : 2 * rows + own, :] = jnp.where(valid, v_ref[:, lanes], mark)
        o_ref[2 * rows + own :, :] = rv_ref[:, lanes]


def pack_kernel(n_y, rq_ref, o_ref):
    own, width = rq_ref.shape
    targets = o_ref.shape[0] // 2
    some = o_ref.shape[1] // own
    for j in range(targets):
        x, y = j // n_y, j % n_y
        for c in range(2):
            for i in range(some):
                lane = c * (width // 2) + (GROUP * y + some * x + i) * HEAD_SIZE
                o_ref[2 * j + c, i * own : (i + 1) * own, :] = rq_ref[:, lane : lane + HEAD_SIZE]


def prepare_kernel(n_x, n_y, len_ref, rq_ref, k_ref, v_ref, rk_ref, rv_ref, sent_ref, *o_refs):
    pack_kernel(n_y, rq_ref, sent_ref)
    mark_kernel(n_x, len_ref, k_ref, v_ref, rk_ref, rv_ref, *o_refs)


def prepare(own_len, rq, k, v, rk, rv, n_x, n_y):
    rows, width = k.shape
    vmem = pl.BlockSpec(memory_space=pltpu.VMEM)
    targets = 2 * n_x * n_y
    shapes = [jax.ShapeDtypeStruct((targets, rq.size // (targets * HEAD_SIZE), HEAD_SIZE), k.dtype)]
    shapes += [jax.ShapeDtypeStruct((rows // n_x, 2 * width), k.dtype)] * n_x
    shapes += [jax.ShapeDtypeStruct((2 * (rows + rk.shape[0]), HEAD_SIZE), k.dtype)] * n_y
    out = pl.pallas_call(
        functools.partial(prepare_kernel, n_x, n_y),
        out_shape=shapes,
        in_specs=[pl.BlockSpec(memory_space=pltpu.SMEM)] + [vmem] * 5,
        out_specs=[vmem] * len(shapes),
        compiler_params=pltpu.CompilerParams(vmem_limit_bytes=56 * 1024 * 1024),
        cost_estimate=pl.CostEstimate(flops=2**18, bytes_accessed=5 * 2**19, transcendentals=0),
        name="prepare",
    )(own_len, rq, k, v, rk, rv)
    return out[0], out[1 : 1 + n_x], out[1 + n_x :]


def plane_kernel(owner_ref, x_ref, o_ref):
    own = 16
    source = 2 * lax.rem(owner_ref[0], N_X * N_Y)
    parts = []
    for i in range(x_ref.shape[1] // own):
        pick = slice(i * own, (i + 1) * own)
        parts += [x_ref[source, pick, :], x_ref[source + 1, pick, :]]
    part = jnp.concatenate(parts, axis=0)
    for z in range(o_ref.shape[0]):
        o_ref[z] = part


def line_kernel(owner_ref, x_ref, o_ref):
    o_ref[...] = x_ref[x_ref.shape[0] - 1 - lax.div(owner_ref[0], N_X * N_Y)]


def choose(kernel, owner, x, shape, flops):
    vmem = pl.BlockSpec(memory_space=pltpu.VMEM)
    return pl.pallas_call(
        kernel,
        out_shape=jax.ShapeDtypeStruct(shape, x.dtype),
        in_specs=[pl.BlockSpec(memory_space=pltpu.SMEM), vmem],
        out_specs=vmem,
        compiler_params=pltpu.CompilerParams(vmem_limit_bytes=VMEM_LIMIT),
        cost_estimate=pl.CostEstimate(flops=flops, bytes_accessed=2**19, transcendentals=0),
        name="choose",
    )(owner, x)


def split3(x):
    high = x.astype(jnp.bfloat16).astype(jnp.float32)
    rest = x - high
    mid = rest.astype(jnp.bfloat16).astype(jnp.float32)
    low = (rest - mid).astype(jnp.bfloat16).astype(jnp.float32)
    return high, mid, low


def code_rows(pair, last, height):
    row = lax.broadcasted_iota(jnp.int32, (height, HEAD_SIZE), 0)
    return jnp.where(row == 0, pair, jnp.where(row == 1, last, 0.0)).astype(jnp.bfloat16)


def request_kernel(own, count, owner_ref, *refs):
    q_refs, lines = refs[:count], refs[count : -count - 1]
    o_refs, v_ref = refs[-count - 1 : -1], refs[-1]
    piece = q_refs[0].shape[0]
    n = count * piece
    both = lines[0].shape[0] // 2
    rows = both - own
    c = SCALE * LOG2E
    q = jnp.concatenate([ref[...] for ref in q_refs], axis=0)
    for i, ref in enumerate(lines):
        part = ref[both : both + rows, :]
        hidden = part > 100.0
        top = i * rows
        v_ref[top : top + rows, :HEAD_SIZE] = jnp.where(hidden, jnp.zeros_like(part), part)
        v_ref[top : top + rows, HEAD_SIZE:] = jnp.where(hidden, jnp.zeros_like(part), jnp.ones_like(part))
        top = len(lines) * rows + i * own
        v_ref[top : top + own, :HEAD_SIZE] = ref[both + rows :, :]
        v_ref[top : top + own, HEAD_SIZE:] = jnp.ones((own, HEAD_SIZE), jnp.bfloat16)
    owner = owner_ref[0]
    same = lax.div(owner, N_Y) == lax.div(place(), N_Y)
    asked = jnp.where(same, lax.rem(lax.axis_index("y") - lax.rem(owner, N_Y) + N_Y, N_Y), -1)
    own_keys = jnp.concatenate([ref[rows:both, :] for ref in lines], axis=0)
    row = lax.rem(lax.broadcasted_iota(jnp.int32, (n, own_keys.shape[0]), 0), own)
    col = lax.broadcasted_iota(jnp.int32, (n, own_keys.shape[0]), 1) - asked * own
    scores = [dot_nt(q, ref[0:rows, :]) for ref in lines]
    scores.append(jnp.where((asked >= 0) & (col >= 0) & (col <= row), dot_nt(q, own_keys), -jnp.inf))
    tiles = [s[:, i : i + HEAD_SIZE] for s in scores for i in range(0, s.shape[1], HEAD_SIZE)]
    peak = jnp.max(functools.reduce(jnp.maximum, tiles), axis=1, keepdims=True)
    weights = [jnp.exp2((tile - peak) * c).astype(jnp.bfloat16) for tile in tiles]
    acc = dot_nn(jnp.concatenate(weights, axis=1), v_ref[...])
    total = acc[:, HEAD_SIZE:]
    out = acc[:, :HEAD_SIZE] / total
    out_high = out.astype(jnp.bfloat16)
    out_low = (out - out_high.astype(jnp.float32)).astype(jnp.bfloat16)
    lse = peak * SCALE + jnp.log(total)
    high, mid, low = split3(lse)
    row = lax.broadcasted_iota(jnp.int32, (piece, HEAD_SIZE), 0)
    lane = lax.broadcasted_iota(jnp.int32, (piece, HEAD_SIZE), 1)
    for p, o_ref in enumerate(o_refs):
        part = slice(p * piece, (p + 1) * piece)
        pair = jnp.where(row == lane, high[part], jnp.where(row + piece == lane, mid[part], 0.0))
        last = jnp.where(row == lane, low[part], 0.0)
        o_ref[0:piece, :] = out_high[part]
        o_ref[piece : 2 * piece, :] = out_low[part]
        o_ref[2 * piece :, :] = code_rows(
            jnp.sum(pair, axis=0, keepdims=True), jnp.sum(last, axis=0, keepdims=True), 16
        )


def request_partials(owner, queries, lines, own):
    count, piece = len(queries), queries[0].shape[0]
    keys = len(lines) * lines[0].shape[0] // 2
    vmem = pl.BlockSpec(memory_space=pltpu.VMEM)
    return pl.pallas_call(
        functools.partial(request_kernel, own, count),
        out_shape=[jax.ShapeDtypeStruct((2 * piece + 16, HEAD_SIZE), jnp.bfloat16)] * count,
        in_specs=[pl.BlockSpec(memory_space=pltpu.SMEM)] + [vmem] * (count + len(lines)),
        out_specs=[vmem] * count,
        scratch_shapes=[pltpu.VMEM((keys, 2 * HEAD_SIZE), jnp.bfloat16)],
        compiler_params=pltpu.CompilerParams(vmem_limit_bytes=VMEM_LIMIT),
        cost_estimate=pl.CostEstimate(
            flops=3 * 10**9, bytes_accessed=2**20, transcendentals=count * piece * keys
        ),
        name="request_partials",
    )(owner, *queries, *lines)


def join_kernel(parts_in, keep_code, *refs):
    x_refs, o_ref = refs[:-1], refs[-1]
    if len(x_refs) == 1:
        x_refs = [x_refs[0].at[i] for i in range(x_refs[0].shape[0])]
    height = x_refs[0].shape[0]
    top = height - 16
    piece = top // parts_in
    count = max(len(x_refs), 8)
    row = lax.broadcasted_iota(jnp.int32, (count, HEAD_SIZE), 0)
    lane = lax.broadcasted_iota(jnp.int32, (count, HEAD_SIZE), 1)
    pair = jnp.zeros((count, HEAD_SIZE), jnp.float32)
    last = jnp.zeros((count, HEAD_SIZE), jnp.float32)
    for i, ref in enumerate(x_refs):
        code = ref[top:height, :].astype(jnp.float32)
        pair = jnp.where(row == i, code[0:1, :], pair)
        last = jnp.where(row == i, code[1:2, :], last)
    lse = jnp.where(lane < piece, pair + pltpu.roll(pair, piece, 1) + last, 0.0)
    lse = jnp.where(row < len(x_refs), lse, -jnp.inf)
    peak = jnp.max(lse, axis=0, keepdims=True)
    weight = jnp.exp(lse - peak)
    total = jnp.sum(weight, axis=0, keepdims=True)
    column = jnp.transpose(weight / total)
    out = jnp.zeros((piece, HEAD_SIZE), jnp.float32)
    for i, ref in enumerate(x_refs):
        part = ref[0:piece, :].astype(jnp.float32)
        if parts_in > 1:
            part = part + ref[piece:top, :].astype(jnp.float32)
        out = out + column[0:piece, i : i + 1] * part
    parts = [out.astype(jnp.bfloat16)]
    if keep_code:
        high, mid, low = split3(peak + jnp.log(total))
        pair = jnp.where(lane[0:1] < piece, high, pltpu.roll(mid, piece, 1))
        parts.append(code_rows(pair, low, 16))
    part = jnp.concatenate(parts, axis=0)
    if len(o_ref.shape) == 2:
        o_ref[...] = part
    else:
        for i in range(o_ref.shape[0]):
            o_ref[i] = part


def join(arrays, copies, parts_in, keep_code):
    height = (arrays[0].shape[-2] - 16) // parts_in + (16 if keep_code else 0)
    shape = (copies, height, HEAD_SIZE) if copies else (height, HEAD_SIZE)
    return pl.pallas_call(
        functools.partial(join_kernel, parts_in, keep_code),
        out_shape=jax.ShapeDtypeStruct(shape, jnp.bfloat16),
        compiler_params=pltpu.CompilerParams(vmem_limit_bytes=VMEM_LIMIT),
        cost_estimate=pl.CostEstimate(flops=3 * 10**9, bytes_accessed=2**19, transcendentals=1024),
        name="join_pieces",
    )(*arrays)


def answer_kernel(owner_ref, x_ref, _, o_ref, rows_ref, sem):
    own = rows_ref.shape[0]
    some = x_ref.shape[1] // own

    @pl.when(place() == owner_ref[0])
    def _():
        for j in range(x_ref.shape[0]):
            x, y = j // N_Y, j % N_Y
            for i in range(some):
                lane = (GROUP * y + some * x + i) * HEAD_SIZE
                rows_ref[:, lane : lane + HEAD_SIZE] = x_ref[j, i * own : (i + 1) * own, :]
        copy = pltpu.make_async_copy(rows_ref, o_ref, sem)
        copy.start()
        copy.wait()


def answer_rows(owner, x, zeros):
    any_spec = pl.BlockSpec(memory_space=pl.ANY)
    return pl.pallas_call(
        answer_kernel,
        out_shape=jax.ShapeDtypeStruct(zeros.shape, zeros.dtype),
        in_specs=[pl.BlockSpec(memory_space=pltpu.SMEM), pl.BlockSpec(memory_space=pltpu.VMEM), any_spec],
        out_specs=any_spec,
        input_output_aliases={2: 0},
        scratch_shapes=[pltpu.VMEM(zeros.shape, zeros.dtype), pltpu.SemaphoreType.DMA],
        compiler_params=pltpu.CompilerParams(vmem_limit_bytes=VMEM_LIMIT),
        cost_estimate=pl.CostEstimate(flops=2**18, bytes_accessed=2**19, transcendentals=0),
        name="answer_rows",
    )(owner, x, zeros)


def exchange(x, axis, groups=None):
    return lax.all_to_all(x, axis, split_axis=0, concat_axis=0, axis_index_groups=groups, tiled=True)


def local(n_z, n_x, n_y, q, k, v, block_lengths, rq, rk, rv, query_owner):
    n_xy = n_x * n_y
    z, x, y = (lax.axis_index(name) for name in ("z", "x", "y"))
    own_len = block_lengths
    own_rows = rk.shape[0]
    down = [list(range(n_z))[::-1]]

    def move(value, pairs):
        return lax.ppermute(value, ("z", "x", "y"), pairs)

    def shift_x(value, count):
        return lax.ppermute(value, "x", [(a, (a + count) % n_x) for a in range(n_x)])

    sent, pieces, lines = prepare(own_len, rq, k, v, rk, rv, n_x, n_y)
    moved = exchange(sent, ("x", "y", "head"))
    got = [move(pieces[i], [(0, i * n_y)]) for i in range(1, n_x)]
    lines = [lines[0]] + [
        lax.ppermute(lines[i], "y", [(a, (a + i) % n_y) for a in range(n_y)]) for i in range(1, n_y)
    ]

    piece = (2 * moved.shape[1], HEAD_SIZE)
    moved, got = lax.optimization_barrier((moved, got))
    moved = choose(plane_kernel, query_owner, moved, (n_z,) + piece, 8 * 10**8)
    anchor = jnp.where(x == 0, pieces[0], got[0] + got[1] + got[2])
    got = [move(anchor, [(i * n_y, (to * n_x + i) * n_y) for i in range(n_x)]) for to in (3, 5)]
    moved = exchange(moved, "z", down)

    moved = choose(line_kernel, query_owner, moved, piece, 3 * 10**9)
    moved, lines = lax.optimization_barrier((moved, lines))
    anchor = jnp.where(z == 0, anchor, got[0] + got[1])
    rows = [(to * n_x + i) * n_y for to in (0, 3, 5) for i in range(n_x)]
    got = [move(anchor, [(p, p + j) for p in rows]) for j in (3, 2, 1)]
    queries = [moved] + [shift_x(moved, i) for i in range(1, n_x)]

    partials = request_partials(query_owner, queries, lines, own_rows)
    anchor = jnp.where(y == 0, anchor, got[0] + got[1] + got[2])
    plane = range(n_xy)
    steps = (((0, 1), (3, 4), (5, 6)), ((3, 2), (5, 7)))
    got = [move(anchor, [(a * n_xy + p, b * n_xy + p) for a, b in step for p in plane]) for step in steps]
    partials = [partials[0]] + [shift_x(partials[i], n_x - i) for i in range(1, n_x)]

    planes = join(partials, n_z, 2, True)
    anchor = jnp.where((z == 0) | (z == 3) | (z == 5), anchor, got[0] + got[1])
    anchors = [anchor]
    for i in range(1, n_x):
        anchors.append(shift_x(anchor, i))
    planes = exchange(planes, "z", down)

    answer = exchange(join([planes], n_xy, 1, False), ("x", "y"))
    context_output, zeros = context_attention(own_len, q, k, v, anchors, own_rows)
    request_output = answer_rows(query_owner, answer, zeros)
    return context_output, request_output


def solution(mesh):
    n_z, n_x, n_y = 8, N_X, N_Y
    grid = jax.sharding.Mesh(mesh.devices.reshape(n_z, n_x, n_y, 2), ("z", "x", "y", "head"))
    ctx = ("z", "x", "y")
    in_specs = (
        P(ctx, "head"),
        P(ctx, "head"),
        P(ctx, "head"),
        P(ctx),
        P(ctx + ("head",), None),
        P(ctx, "head"),
        P(ctx, "head"),
        P(),
    )
    out_specs = (P(ctx, "head"), P(ctx, "head"))
    return jax.shard_map(
        functools.partial(local, n_z, n_x, n_y),
        mesh=grid,
        in_specs=in_specs,
        out_specs=out_specs,
        check_vma=False,
    )
```

```python
import functools

import jax
import jax.numpy as jnp
from jax import lax
from jax.experimental import pallas as pl
from jax.experimental.pallas import tpu as pltpu
from jax.sharding import PartitionSpec as P

HEAD_SIZE = 128
GROUP = 8
SCALE = HEAD_SIZE**-0.5
LOG2E = 1.4426950408889634
LN2 = 0.6931471805599453
MARK = 1024.0
VMEM_LIMIT = 32 * 1024 * 1024
STACK = 4
N_X, N_Y = 4, 4
PLANES = (4, 2, 1, 7, 5, 6, 3, 0)


def place():
    return (lax.axis_index("z") * N_X + lax.axis_index("x")) * N_Y + lax.axis_index("y")


def dot_nt(a, b):
    return lax.dot_general(a, b, (((1,), (1,)), ((), ())), preferred_element_type=jnp.float32)


def dot_nn(a, b):
    return lax.dot_general(a, b, (((1,), (0,)), ((), ())), preferred_element_type=jnp.float32)


def context_kernel(count, len_ref, q_ref, k_ref, v_ref, *refs):
    anchor_refs = refs[:count]
    o_ref, zero_ref, vs_ref, out_ref, sems = refs[-5:]
    zero_ref[...] = jnp.zeros_like(zero_ref)
    rows, width = k_ref.shape
    half = rows // 2
    heads = width // HEAD_SIZE
    own_len = len_ref[0]
    root = place() == 0
    c = SCALE * LOG2E
    row = lax.broadcasted_iota(jnp.int32, (STACK * half, half), 0)
    col = lax.broadcasted_iota(jnp.int32, (STACK * half, half), 1)
    causal = jnp.where(col <= lax.rem(row, half), 0.0, -jnp.inf).astype(jnp.float32)

    def lanes(g):
        return slice(g * HEAD_SIZE, (g + 1) * HEAD_SIZE)

    def load(h):
        ak = jnp.concatenate([ref[:, lanes(h)] for ref in anchor_refs], axis=0)
        ak = jnp.where(root, jnp.broadcast_to(k_ref[0:1, lanes(h)], ak.shape), ak)
        av = jnp.concatenate([ref[:, lanes(heads + h)] for ref in anchor_refs], axis=0)
        hidden = (av > 100.0) | root
        vs_ref[h, 0:rows, :HEAD_SIZE] = jnp.where(hidden, jnp.zeros_like(av), av)
        vs_ref[h, 0:rows, HEAD_SIZE:] = jnp.where(hidden, jnp.zeros_like(av), jnp.ones_like(av))
        vs_ref[h, rows:, :HEAD_SIZE] = v_ref[:, lanes(h)]
        vs_ref[h, rows:, HEAD_SIZE:] = jnp.ones((rows, HEAD_SIZE), jnp.bfloat16)
        return ak

    def scores(h, top, g, ak):
        keys = top + half
        q = jnp.concatenate([q_ref[top:keys, lanes(g + i)] for i in range(STACK)], axis=0)
        sa = dot_nt(q, ak)
        so = dot_nt(q, k_ref[0:keys, lanes(h)])
        tiles = [sa[:, i : i + half] for i in range(0, rows, half)]
        tiles += [so[:, i : i + half] for i in range(0, top, half)]
        return tiles + [so[:, top:keys] + causal]

    def finish(index, h, top, g, tiles):
        keys = top + half
        live = (top + lax.broadcasted_iota(jnp.int32, (half, HEAD_SIZE), 0)) < own_len
        peak = jnp.max(functools.reduce(jnp.maximum, tiles), axis=1, keepdims=True)
        weights = [jnp.exp2((tile - peak) * c).astype(jnp.bfloat16) for tile in tiles]
        acc = dot_nn(jnp.concatenate(weights, axis=1), vs_ref[h, 0 : rows + keys, :])
        total = acc[:, HEAD_SIZE:]
        inverse = pl.reciprocal(total, approx=True)
        inverse = inverse * (2.0 - total * inverse)
        out = acc[:, :HEAD_SIZE] * inverse
        for i in range(STACK):
            part = jnp.where(live, out[i * half : (i + 1) * half], 0.0)
            out_ref[top:keys, lanes(g + i)] = part.astype(jnp.bfloat16)
        where = (slice(top, keys), slice(g * HEAD_SIZE, (g + STACK) * HEAD_SIZE))
        copy = pltpu.make_async_copy(out_ref.at[where], o_ref.at[where], sems.at[index])
        copy.start()
        return copy

    work = [
        (h, top, h * GROUP + g) for h in range(heads) for top in (half, 0) for g in range(0, GROUP, STACK)
    ]
    ak = load(0)
    tiles = scores(*work[0], ak)
    copies = []
    for i, item in enumerate(work):
        later = None
        if i + 1 < len(work):
            if work[i + 1][0] != item[0]:
                ak = load(work[i + 1][0])
            later = scores(*work[i + 1], ak)
        copies.append(finish(i, *item, tiles))
        tiles = later
    for copy in copies:
        copy.wait()


def context_attention(own_len, q, k, v, anchor, own_rows):
    rows, width = q.shape
    heads = k.shape[1] // HEAD_SIZE
    vmem = pl.BlockSpec(memory_space=pltpu.VMEM)
    tiles = 2 * heads * GROUP // STACK
    return pl.pallas_call(
        functools.partial(context_kernel, len(anchor)),
        out_shape=[
            jax.ShapeDtypeStruct((rows, width), jnp.bfloat16),
            jax.ShapeDtypeStruct((own_rows, width), jnp.bfloat16),
        ],
        in_specs=[pl.BlockSpec(memory_space=pltpu.SMEM)] + [vmem] * (3 + len(anchor)),
        out_specs=[pl.BlockSpec(memory_space=pl.ANY), vmem],
        scratch_shapes=[
            pltpu.VMEM((heads, 2 * rows, 2 * HEAD_SIZE), jnp.bfloat16),
            pltpu.VMEM((rows, width), jnp.bfloat16),
            pltpu.SemaphoreType.DMA((tiles,)),
        ],
        compiler_params=pltpu.CompilerParams(vmem_limit_bytes=VMEM_LIMIT),
        cost_estimate=pl.CostEstimate(
            flops=8 * rows * width * rows, bytes_accessed=5 * 2**20, transcendentals=2 * rows * rows * heads * GROUP
        ),
        name="context_attention",
    )(own_len, q, k, v, *anchor)


def mark_kernel(n_x, len_ref, k_ref, v_ref, rk_ref, rv_ref, *o_refs):
    rows, width = k_ref.shape
    own = rk_ref.shape[0]
    slab = rows // n_x
    first = jnp.broadcast_to(k_ref[0:1, :], (slab, width))
    for i, o_ref in enumerate(o_refs[:n_x]):
        span = slice(i * slab, (i + 1) * slab)
        valid = (i * slab + lax.broadcasted_iota(jnp.int32, first.shape, 0)) < len_ref[0]
        o_ref[:, :width] = jnp.where(valid, k_ref[span, :], first)
        o_ref[:, width:] = jnp.where(valid, v_ref[span, :], jnp.full_like(first, MARK))
    lines = o_refs[n_x:]
    valid = lax.broadcasted_iota(jnp.int32, (rows, HEAD_SIZE), 0) < len_ref[0]
    y = lax.axis_index("y")
    for i, o_ref in enumerate(lines):
        head = lax.rem(y + i, len(lines))
        lanes = pl.ds(pl.multiple_of(head * HEAD_SIZE, HEAD_SIZE), HEAD_SIZE)
        first = k_ref[0:1, lanes]
        o_ref[0:rows, :] = jnp.where(valid, k_ref[:, lanes], jnp.broadcast_to(first, valid.shape))
        o_ref[rows : rows + own, :] = rk_ref[:, lanes]
        mark = jnp.full((rows, HEAD_SIZE), MARK, jnp.bfloat16)
        o_ref[rows + own : 2 * rows + own, :] = jnp.where(valid, v_ref[:, lanes], mark)
        o_ref[2 * rows + own :, :] = rv_ref[:, lanes]


def pack_kernel(n_y, rq_ref, o_ref):
    own, width = rq_ref.shape
    targets = o_ref.shape[0] // 2
    some = o_ref.shape[1] // own
    for j in range(targets):
        x, y = j // n_y, j % n_y
        for c in range(2):
            for i in range(some):
                lane = c * (width // 2) + (GROUP * y + some * x + i) * HEAD_SIZE
                o_ref[2 * j + c, i * own : (i + 1) * own, :] = rq_ref[:, lane : lane + HEAD_SIZE]


def prepare_kernel(n_x, n_y, len_ref, rq_ref, k_ref, v_ref, rk_ref, rv_ref, sent_ref, *o_refs):
    pack_kernel(n_y, rq_ref, sent_ref)
    mark_kernel(n_x, len_ref, k_ref, v_ref, rk_ref, rv_ref, *o_refs)


def prepare(own_len, rq, k, v, rk, rv, n_x, n_y):
    rows, width = k.shape
    vmem = pl.BlockSpec(memory_space=pltpu.VMEM)
    targets = 2 * n_x * n_y
    shapes = [jax.ShapeDtypeStruct((targets, rq.size // (targets * HEAD_SIZE), HEAD_SIZE), k.dtype)]
    shapes += [jax.ShapeDtypeStruct((rows // n_x, 2 * width), k.dtype)] * n_x
    shapes += [jax.ShapeDtypeStruct((2 * (rows + rk.shape[0]), HEAD_SIZE), k.dtype)] * n_y
    out = pl.pallas_call(
        functools.partial(prepare_kernel, n_x, n_y),
        out_shape=shapes,
        in_specs=[pl.BlockSpec(memory_space=pltpu.SMEM)] + [vmem] * 5,
        out_specs=[vmem] * len(shapes),
        compiler_params=pltpu.CompilerParams(vmem_limit_bytes=56 * 1024 * 1024),
        cost_estimate=pl.CostEstimate(flops=2**18, bytes_accessed=5 * 2**19, transcendentals=0),
        name="prepare",
    )(own_len, rq, k, v, rk, rv)
    return out[0], out[1 : 1 + n_x], out[1 + n_x :]


def plane_kernel(owner_ref, x_ref, o_ref):
    own = 16
    source = 2 * lax.rem(owner_ref[0], N_X * N_Y)
    parts = []
    for i in range(x_ref.shape[1] // own):
        pick = slice(i * own, (i + 1) * own)
        parts += [x_ref[source, pick, :], x_ref[source + 1, pick, :]]
    part = jnp.concatenate(parts, axis=0)
    for z in range(o_ref.shape[0]):
        o_ref[z] = part


def line_kernel(owner_ref, x_ref, o_ref):
    owner_z = lax.div(owner_ref[0], N_X * N_Y)
    spot = 0
    for i, z in enumerate(PLANES):
        spot = jnp.where(owner_z == z, i, spot)
    o_ref[...] = x_ref[spot]


def choose(kernel, owner, x, shape, flops):
    vmem = pl.BlockSpec(memory_space=pltpu.VMEM)
    return pl.pallas_call(
        kernel,
        out_shape=jax.ShapeDtypeStruct(shape, x.dtype),
        in_specs=[pl.BlockSpec(memory_space=pltpu.SMEM), vmem],
        out_specs=vmem,
        compiler_params=pltpu.CompilerParams(vmem_limit_bytes=VMEM_LIMIT),
        cost_estimate=pl.CostEstimate(flops=flops, bytes_accessed=2**19, transcendentals=0),
        name="choose",
    )(owner, x)


def split3(x):
    high = x.astype(jnp.bfloat16).astype(jnp.float32)
    rest = x - high
    mid = rest.astype(jnp.bfloat16).astype(jnp.float32)
    low = (rest - mid).astype(jnp.bfloat16).astype(jnp.float32)
    return high, mid, low


def code_rows(pair, last, height):
    row = lax.broadcasted_iota(jnp.int32, (height, HEAD_SIZE), 0)
    return jnp.where(row == 0, pair, jnp.where(row == 1, last, 0.0)).astype(jnp.bfloat16)


def request_kernel(own, count, owner_ref, *refs):
    q_refs, lines = refs[:count], refs[count : -count - 1]
    o_refs, v_ref = refs[-count - 1 : -1], refs[-1]
    piece = q_refs[0].shape[0]
    n = count * piece
    both = lines[0].shape[0] // 2
    rows = both - own
    c = SCALE * LOG2E
    q = jnp.concatenate([ref[...] for ref in q_refs], axis=0)
    for i, ref in enumerate(lines):
        part = ref[both : both + rows, :]
        hidden = part > 100.0
        top = i * rows
        v_ref[top : top + rows, :HEAD_SIZE] = jnp.where(hidden, jnp.zeros_like(part), part)
        v_ref[top : top + rows, HEAD_SIZE:] = jnp.where(hidden, jnp.zeros_like(part), jnp.ones_like(part))
        top = len(lines) * rows + i * own
        v_ref[top : top + own, :HEAD_SIZE] = ref[both + rows :, :]
        v_ref[top : top + own, HEAD_SIZE:] = jnp.ones((own, HEAD_SIZE), jnp.bfloat16)
    owner = owner_ref[0]
    same = lax.div(owner, N_Y) == lax.div(place(), N_Y)
    asked = jnp.where(same, lax.rem(lax.axis_index("y") - lax.rem(owner, N_Y) + N_Y, N_Y), -1)
    own_keys = jnp.concatenate([ref[rows:both, :] for ref in lines], axis=0)
    row = lax.rem(lax.broadcasted_iota(jnp.int32, (n, own_keys.shape[0]), 0), own)
    col = lax.broadcasted_iota(jnp.int32, (n, own_keys.shape[0]), 1) - asked * own
    scores = [dot_nt(q, ref[0:rows, :]) for ref in lines]
    scores.append(jnp.where((asked >= 0) & (col >= 0) & (col <= row), dot_nt(q, own_keys), -jnp.inf))
    tiles = [s[:, i : i + HEAD_SIZE] for s in scores for i in range(0, s.shape[1], HEAD_SIZE)]
    peak = jnp.max(functools.reduce(jnp.maximum, tiles), axis=1, keepdims=True)
    weights = [jnp.exp2((tile - peak) * c).astype(jnp.bfloat16) for tile in tiles]
    acc = dot_nn(jnp.concatenate(weights, axis=1), v_ref[...])
    total = acc[:, HEAD_SIZE:]
    out = acc[:, :HEAD_SIZE] / total
    out_high = out.astype(jnp.bfloat16)
    out_low = (out - out_high.astype(jnp.float32)).astype(jnp.bfloat16)
    lse = peak * SCALE + jnp.log(total)
    high, mid, low = split3(lse)
    row = lax.broadcasted_iota(jnp.int32, (piece, HEAD_SIZE), 0)
    lane = lax.broadcasted_iota(jnp.int32, (piece, HEAD_SIZE), 1)
    for p, o_ref in enumerate(o_refs):
        part = slice(p * piece, (p + 1) * piece)
        pair = jnp.where(row == lane, high[part], jnp.where(row + piece == lane, mid[part], 0.0))
        last = jnp.where(row == lane, low[part], 0.0)
        o_ref[0:piece, :] = out_high[part]
        o_ref[piece : 2 * piece, :] = out_low[part]
        o_ref[2 * piece :, :] = code_rows(
            jnp.sum(pair, axis=0, keepdims=True), jnp.sum(last, axis=0, keepdims=True), 16
        )


def request_partials(owner, queries, lines, own):
    count, piece = len(queries), queries[0].shape[0]
    keys = len(lines) * lines[0].shape[0] // 2
    vmem = pl.BlockSpec(memory_space=pltpu.VMEM)
    return pl.pallas_call(
        functools.partial(request_kernel, own, count),
        out_shape=[jax.ShapeDtypeStruct((2 * piece + 16, HEAD_SIZE), jnp.bfloat16)] * count,
        in_specs=[pl.BlockSpec(memory_space=pltpu.SMEM)] + [vmem] * (count + len(lines)),
        out_specs=[vmem] * count,
        scratch_shapes=[pltpu.VMEM((keys, 2 * HEAD_SIZE), jnp.bfloat16)],
        compiler_params=pltpu.CompilerParams(vmem_limit_bytes=VMEM_LIMIT),
        cost_estimate=pl.CostEstimate(
            flops=3 * 10**9, bytes_accessed=2**20, transcendentals=count * piece * keys
        ),
        name="request_partials",
    )(owner, *queries, *lines)


def join_kernel(parts_in, keep_code, *refs):
    x_refs, o_ref = refs[:-1], refs[-1]
    if len(x_refs) == 1:
        x_refs = [x_refs[0].at[i] for i in range(x_refs[0].shape[0])]
    height = x_refs[0].shape[0]
    top = height - 16
    piece = top // parts_in
    count = max(len(x_refs), 8)
    row = lax.broadcasted_iota(jnp.int32, (count, HEAD_SIZE), 0)
    lane = lax.broadcasted_iota(jnp.int32, (count, HEAD_SIZE), 1)
    pair = jnp.zeros((count, HEAD_SIZE), jnp.float32)
    last = jnp.zeros((count, HEAD_SIZE), jnp.float32)
    for i, ref in enumerate(x_refs):
        code = ref[top:height, :].astype(jnp.float32)
        pair = jnp.where(row == i, code[0:1, :], pair)
        last = jnp.where(row == i, code[1:2, :], last)
    lse = jnp.where(lane < piece, pair + pltpu.roll(pair, piece, 1) + last, 0.0)
    lse = jnp.where(row < len(x_refs), lse, -jnp.inf)
    peak = jnp.max(lse, axis=0, keepdims=True)
    weight = jnp.exp(lse - peak)
    total = jnp.sum(weight, axis=0, keepdims=True)
    column = jnp.transpose(weight / total)
    out = jnp.zeros((piece, HEAD_SIZE), jnp.float32)
    for i, ref in enumerate(x_refs):
        part = ref[0:piece, :].astype(jnp.float32)
        if parts_in > 1:
            part = part + ref[piece:top, :].astype(jnp.float32)
        out = out + column[0:piece, i : i + 1] * part
    parts = [out.astype(jnp.bfloat16)]
    if keep_code:
        high, mid, low = split3(peak + jnp.log(total))
        pair = jnp.where(lane[0:1] < piece, high, pltpu.roll(mid, piece, 1))
        parts.append(code_rows(pair, low, 16))
    part = jnp.concatenate(parts, axis=0)
    if len(o_ref.shape) == 2:
        o_ref[...] = part
    else:
        for i in range(o_ref.shape[0]):
            o_ref[i] = part


def join(arrays, copies, parts_in, keep_code):
    height = (arrays[0].shape[-2] - 16) // parts_in + (16 if keep_code else 0)
    shape = (copies, height, HEAD_SIZE) if copies else (height, HEAD_SIZE)
    return pl.pallas_call(
        functools.partial(join_kernel, parts_in, keep_code),
        out_shape=jax.ShapeDtypeStruct(shape, jnp.bfloat16),
        compiler_params=pltpu.CompilerParams(vmem_limit_bytes=VMEM_LIMIT),
        cost_estimate=pl.CostEstimate(flops=3 * 10**9, bytes_accessed=2**19, transcendentals=1024),
        name="join_pieces",
    )(*arrays)


def answer_kernel(owner_ref, x_ref, _, o_ref, rows_ref, sem):
    own = rows_ref.shape[0]
    some = x_ref.shape[1] // own

    @pl.when(place() == owner_ref[0])
    def _():
        for j in range(x_ref.shape[0]):
            x, y = j // N_Y, j % N_Y
            for i in range(some):
                lane = (GROUP * y + some * x + i) * HEAD_SIZE
                rows_ref[:, lane : lane + HEAD_SIZE] = x_ref[j, i * own : (i + 1) * own, :]
        copy = pltpu.make_async_copy(rows_ref, o_ref, sem)
        copy.start()
        copy.wait()


def answer_rows(owner, x, zeros):
    any_spec = pl.BlockSpec(memory_space=pl.ANY)
    return pl.pallas_call(
        answer_kernel,
        out_shape=jax.ShapeDtypeStruct(zeros.shape, zeros.dtype),
        in_specs=[pl.BlockSpec(memory_space=pltpu.SMEM), pl.BlockSpec(memory_space=pltpu.VMEM), any_spec],
        out_specs=any_spec,
        input_output_aliases={2: 0},
        scratch_shapes=[pltpu.VMEM(zeros.shape, zeros.dtype), pltpu.SemaphoreType.DMA],
        compiler_params=pltpu.CompilerParams(vmem_limit_bytes=VMEM_LIMIT),
        cost_estimate=pl.CostEstimate(flops=2**18, bytes_accessed=2**19, transcendentals=0),
        name="answer_rows",
    )(owner, x, zeros)


def exchange(x, axis, groups=None):
    return lax.all_to_all(x, axis, split_axis=0, concat_axis=0, axis_index_groups=groups, tiled=True)


def local(n_z, n_x, n_y, q, k, v, block_lengths, rq, rk, rv, query_owner):
    n_xy = n_x * n_y
    z, x, y = (lax.axis_index(name) for name in ("z", "x", "y"))
    own_len = block_lengths
    own_rows = rk.shape[0]
    down = [list(range(n_z))[::-1]]

    def move(value, pairs):
        return lax.ppermute(value, ("z", "x", "y"), pairs)

    def shift_x(value, count):
        return lax.ppermute(value, "x", [(a, (a + count) % n_x) for a in range(n_x)])

    sent, pieces, lines = prepare(own_len, rq, k, v, rk, rv, n_x, n_y)
    moved = exchange(sent, ("x", "y", "head"))
    got = [move(pieces[i], [(0, i * n_y)]) for i in range(1, n_x)]
    lines = [lines[0]] + [
        lax.ppermute(lines[i], "y", [(a, (a + i) % n_y) for a in range(n_y)]) for i in range(1, n_y)
    ]

    piece = (2 * moved.shape[1], HEAD_SIZE)
    moved, got = lax.optimization_barrier((moved, got))
    moved = choose(plane_kernel, query_owner, moved, (n_z,) + piece, 8 * 10**8)
    anchor = jnp.where(x == 0, pieces[0], got[0] + got[1] + got[2])
    got = [move(anchor, [(i * n_y, (to * n_x + i) * n_y) for i in range(n_x)]) for to in (6, 3)]
    moved = exchange(moved, "z", [list(PLANES)])

    moved = choose(line_kernel, query_owner, moved, piece, 3 * 10**9)
    moved, lines = lax.optimization_barrier((moved, lines))
    anchor = jnp.where(z == 0, anchor, got[0] + got[1])
    rows = [(to * n_x + i) * n_y for to in (0, 3, 6) for i in range(n_x)]
    got = [move(anchor, [(p, p + j) for p in rows]) for j in (3, 2, 1)]
    queries = [moved] + [shift_x(moved, i) for i in range(1, n_x)]

    partials = request_partials(query_owner, queries, lines, own_rows)
    anchor = jnp.where(y == 0, anchor, got[0] + got[1] + got[2])
    plane = range(n_xy)
    steps = (((0, 1), (3, 4), (6, 7)), ((3, 2), (6, 5)))
    got = [move(anchor, [(a * n_xy + p, b * n_xy + p) for a, b in step for p in plane]) for step in steps]
    partials = [partials[0]] + [shift_x(partials[i], n_x - i) for i in range(1, n_x)]

    planes = join(partials, n_z, 2, True)
    anchor = jnp.where((z == 0) | (z == 3) | (z == 6), anchor, got[0] + got[1])
    anchors = [anchor]
    for i in range(1, n_x):
        anchors.append(shift_x(anchor, i))
    planes = exchange(planes, "z", down)

    answer = exchange(join([planes], n_xy, 1, False), ("x", "y"))
    context_output, zeros = context_attention(own_len, q, k, v, anchors, own_rows)
    request_output = answer_rows(query_owner, answer, zeros)
    return context_output, request_output


def solution(mesh):
    n_z, n_x, n_y = 8, N_X, N_Y
    grid = jax.sharding.Mesh(mesh.devices.reshape(n_z, n_x, n_y, 2), ("z", "x", "y", "head"))
    ctx = ("z", "x", "y")
    in_specs = (
        P(ctx, "head"),
        P(ctx, "head"),
        P(ctx, "head"),
        P(ctx),
        P(ctx + ("head",), None),
        P(ctx, "head"),
        P(ctx, "head"),
        P(),
    )
    out_specs = (P(ctx, "head"), P(ctx, "head"))
    return jax.shard_map(
        functools.partial(local, n_z, n_x, n_y),
        mesh=grid,
        in_specs=in_specs,
        out_specs=out_specs,
        check_vma=False,
    )
```

```python
import functools

import jax
import jax.numpy as jnp
from jax import lax
from jax.experimental import pallas as pl
from jax.experimental.pallas import tpu as pltpu
from jax.sharding import PartitionSpec as P

HEAD_SIZE = 128
GROUP = 8
SCALE = HEAD_SIZE**-0.5
LOG2E = 1.4426950408889634
LN2 = 0.6931471805599453
MARK = 1024.0
VMEM_LIMIT = 32 * 1024 * 1024
STACK = 4
N_X, N_Y = 4, 4


def place():
    return (lax.axis_index("z") * N_X + lax.axis_index("x")) * N_Y + lax.axis_index("y")


def dot_nt(a, b):
    return lax.dot_general(a, b, (((1,), (1,)), ((), ())), preferred_element_type=jnp.float32)


def dot_nn(a, b):
    return lax.dot_general(a, b, (((1,), (0,)), ((), ())), preferred_element_type=jnp.float32)


def context_kernel(count, len_ref, q_ref, k_ref, v_ref, *refs):
    anchor_refs = refs[:count]
    o_ref, zero_ref, vs_ref, out_ref, sems = refs[-5:]
    zero_ref[...] = jnp.zeros_like(zero_ref)
    rows, width = k_ref.shape
    half = rows // 2
    heads = width // HEAD_SIZE
    own_len = len_ref[0]
    root = place() == 0
    c = SCALE * LOG2E
    row = lax.broadcasted_iota(jnp.int32, (STACK * half, half), 0)
    col = lax.broadcasted_iota(jnp.int32, (STACK * half, half), 1)
    causal = jnp.where(col <= lax.rem(row, half), 0.0, -jnp.inf).astype(jnp.float32)

    def lanes(g):
        return slice(g * HEAD_SIZE, (g + 1) * HEAD_SIZE)

    def load(h):
        ak = jnp.concatenate([ref[:, lanes(h)] for ref in anchor_refs], axis=0)
        ak = jnp.where(root, jnp.broadcast_to(k_ref[0:1, lanes(h)], ak.shape), ak)
        av = jnp.concatenate([ref[:, lanes(heads + h)] for ref in anchor_refs], axis=0)
        hidden = (av > 100.0) | root
        vs_ref[h, 0:rows, :HEAD_SIZE] = jnp.where(hidden, jnp.zeros_like(av), av)
        vs_ref[h, 0:rows, HEAD_SIZE:] = jnp.where(hidden, jnp.zeros_like(av), jnp.ones_like(av))
        vs_ref[h, rows:, :HEAD_SIZE] = v_ref[:, lanes(h)]
        vs_ref[h, rows:, HEAD_SIZE:] = jnp.ones((rows, HEAD_SIZE), jnp.bfloat16)
        return ak

    def scores(h, top, g, ak):
        keys = top + half
        q = jnp.concatenate([q_ref[top:keys, lanes(g + i)] for i in range(STACK)], axis=0)
        sa = dot_nt(q, ak)
        so = dot_nt(q, k_ref[0:keys, lanes(h)])
        tiles = [sa[:, i : i + half] for i in range(0, rows, half)]
        tiles += [so[:, i : i + half] for i in range(0, top, half)]
        return tiles + [so[:, top:keys] + causal]

    def finish(index, h, top, g, tiles):
        keys = top + half
        live = (top + lax.broadcasted_iota(jnp.int32, (half, HEAD_SIZE), 0)) < own_len
        peak = jnp.max(functools.reduce(jnp.maximum, tiles), axis=1, keepdims=True)
        weights = [jnp.exp2((tile - peak) * c).astype(jnp.bfloat16) for tile in tiles]
        acc = dot_nn(jnp.concatenate(weights, axis=1), vs_ref[h, 0 : rows + keys, :])
        total = acc[:, HEAD_SIZE:]
        inverse = pl.reciprocal(total, approx=True)
        inverse = inverse * (2.0 - total * inverse)
        out = acc[:, :HEAD_SIZE] * inverse
        for i in range(STACK):
            part = jnp.where(live, out[i * half : (i + 1) * half], 0.0)
            out_ref[top:keys, lanes(g + i)] = part.astype(jnp.bfloat16)
        where = (slice(top, keys), slice(g * HEAD_SIZE, (g + STACK) * HEAD_SIZE))
        copy = pltpu.make_async_copy(out_ref.at[where], o_ref.at[where], sems.at[index])
        copy.start()
        return copy

    work = [
        (h, top, h * GROUP + g) for h in range(heads) for top in (half, 0) for g in range(0, GROUP, STACK)
    ]
    ak = load(0)
    tiles = scores(*work[0], ak)
    copies = []
    for i, item in enumerate(work):
        later = None
        if i + 1 < len(work):
            if work[i + 1][0] != item[0]:
                ak = load(work[i + 1][0])
            later = scores(*work[i + 1], ak)
        copies.append(finish(i, *item, tiles))
        tiles = later
    for copy in copies:
        copy.wait()


def context_attention(own_len, q, k, v, anchor, own_rows):
    rows, width = q.shape
    heads = k.shape[1] // HEAD_SIZE
    vmem = pl.BlockSpec(memory_space=pltpu.VMEM)
    tiles = 2 * heads * GROUP // STACK
    return pl.pallas_call(
        functools.partial(context_kernel, len(anchor)),
        out_shape=[
            jax.ShapeDtypeStruct((rows, width), jnp.bfloat16),
            jax.ShapeDtypeStruct((own_rows, width), jnp.bfloat16),
        ],
        in_specs=[pl.BlockSpec(memory_space=pltpu.SMEM)] + [vmem] * (3 + len(anchor)),
        out_specs=[pl.BlockSpec(memory_space=pl.ANY), vmem],
        scratch_shapes=[
            pltpu.VMEM((heads, 2 * rows, 2 * HEAD_SIZE), jnp.bfloat16),
            pltpu.VMEM((rows, width), jnp.bfloat16),
            pltpu.SemaphoreType.DMA((tiles,)),
        ],
        compiler_params=pltpu.CompilerParams(vmem_limit_bytes=VMEM_LIMIT),
        cost_estimate=pl.CostEstimate(
            flops=8 * rows * width * rows, bytes_accessed=5 * 2**20, transcendentals=2 * rows * rows * heads * GROUP
        ),
        name="context_attention",
    )(own_len, q, k, v, *anchor)


def mark_kernel(n_x, len_ref, k_ref, v_ref, rk_ref, rv_ref, *o_refs):
    rows, width = k_ref.shape
    own = rk_ref.shape[0]
    slab = rows // n_x
    first = jnp.broadcast_to(k_ref[0:1, :], (slab, width))
    for i, o_ref in enumerate(o_refs[:n_x]):
        span = slice(i * slab, (i + 1) * slab)
        valid = (i * slab + lax.broadcasted_iota(jnp.int32, first.shape, 0)) < len_ref[0]
        o_ref[:, :width] = jnp.where(valid, k_ref[span, :], first)
        o_ref[:, width:] = jnp.where(valid, v_ref[span, :], jnp.full_like(first, MARK))
    lines = o_refs[n_x:]
    valid = lax.broadcasted_iota(jnp.int32, (rows, HEAD_SIZE), 0) < len_ref[0]
    y = lax.axis_index("y")
    for i, o_ref in enumerate(lines):
        head = lax.rem(y + i, len(lines))
        lanes = pl.ds(pl.multiple_of(head * HEAD_SIZE, HEAD_SIZE), HEAD_SIZE)
        first = k_ref[0:1, lanes]
        o_ref[0:rows, :] = jnp.where(valid, k_ref[:, lanes], jnp.broadcast_to(first, valid.shape))
        o_ref[rows : rows + own, :] = rk_ref[:, lanes]
        mark = jnp.full((rows, HEAD_SIZE), MARK, jnp.bfloat16)
        o_ref[rows + own : 2 * rows + own, :] = jnp.where(valid, v_ref[:, lanes], mark)
        o_ref[2 * rows + own :, :] = rv_ref[:, lanes]


def pack_kernel(n_y, rq_ref, o_ref):
    own, width = rq_ref.shape
    targets = o_ref.shape[0] // 2
    some = o_ref.shape[1] // own
    for j in range(targets):
        x, y = j // n_y, j % n_y
        for c in range(2):
            for i in range(some):
                lane = c * (width // 2) + (GROUP * y + some * x + i) * HEAD_SIZE
                o_ref[2 * j + c, i * own : (i + 1) * own, :] = rq_ref[:, lane : lane + HEAD_SIZE]


def prepare_kernel(n_x, n_y, len_ref, rq_ref, k_ref, v_ref, rk_ref, rv_ref, sent_ref, *o_refs):
    pack_kernel(n_y, rq_ref, sent_ref)
    mark_kernel(n_x, len_ref, k_ref, v_ref, rk_ref, rv_ref, *o_refs)


def prepare(own_len, rq, k, v, rk, rv, n_x, n_y):
    rows, width = k.shape
    vmem = pl.BlockSpec(memory_space=pltpu.VMEM)
    targets = 2 * n_x * n_y
    shapes = [jax.ShapeDtypeStruct((targets, rq.size // (targets * HEAD_SIZE), HEAD_SIZE), k.dtype)]
    shapes += [jax.ShapeDtypeStruct((rows // n_x, 2 * width), k.dtype)] * n_x
    shapes += [jax.ShapeDtypeStruct((2 * (rows + rk.shape[0]), HEAD_SIZE), k.dtype)] * n_y
    out = pl.pallas_call(
        functools.partial(prepare_kernel, n_x, n_y),
        out_shape=shapes,
        in_specs=[pl.BlockSpec(memory_space=pltpu.SMEM)] + [vmem] * 5,
        out_specs=[vmem] * len(shapes),
        compiler_params=pltpu.CompilerParams(vmem_limit_bytes=56 * 1024 * 1024),
        cost_estimate=pl.CostEstimate(flops=2**18, bytes_accessed=5 * 2**19, transcendentals=0),
        name="prepare",
    )(own_len, rq, k, v, rk, rv)
    return out[0], out[1 : 1 + n_x], out[1 + n_x :]


def plane_kernel(owner_ref, x_ref, o_ref):
    own = 16
    source = 2 * lax.rem(owner_ref[0], N_X * N_Y)
    parts = []
    for i in range(x_ref.shape[1] // own):
        pick = slice(i * own, (i + 1) * own)
        parts += [x_ref[source, pick, :], x_ref[source + 1, pick, :]]
    part = jnp.concatenate(parts, axis=0)
    for z in range(o_ref.shape[0]):
        o_ref[z] = part


def line_kernel(owner_ref, x_ref, o_ref):
    o_ref[...] = x_ref[x_ref.shape[0] - 1 - lax.div(owner_ref[0], N_X * N_Y)]


def choose(kernel, owner, x, shape, flops):
    vmem = pl.BlockSpec(memory_space=pltpu.VMEM)
    return pl.pallas_call(
        kernel,
        out_shape=jax.ShapeDtypeStruct(shape, x.dtype),
        in_specs=[pl.BlockSpec(memory_space=pltpu.SMEM), vmem],
        out_specs=vmem,
        compiler_params=pltpu.CompilerParams(vmem_limit_bytes=VMEM_LIMIT),
        cost_estimate=pl.CostEstimate(flops=flops, bytes_accessed=2**19, transcendentals=0),
        name="choose",
    )(owner, x)


def split3(x):
    high = x.astype(jnp.bfloat16).astype(jnp.float32)
    rest = x - high
    mid = rest.astype(jnp.bfloat16).astype(jnp.float32)
    low = (rest - mid).astype(jnp.bfloat16).astype(jnp.float32)
    return high, mid, low


def code_rows(pair, last, height):
    row = lax.broadcasted_iota(jnp.int32, (height, HEAD_SIZE), 0)
    return jnp.where(row == 0, pair, jnp.where(row == 1, last, 0.0)).astype(jnp.bfloat16)


def request_kernel(own, count, owner_ref, *refs):
    q_refs, lines = refs[:count], refs[count : -count - 1]
    o_refs, v_ref = refs[-count - 1 : -1], refs[-1]
    piece = q_refs[0].shape[0]
    n = count * piece
    both = lines[0].shape[0] // 2
    rows = both - own
    c = SCALE * LOG2E
    q = jnp.concatenate([ref[...] for ref in q_refs], axis=0)
    for i, ref in enumerate(lines):
        part = ref[both : both + rows, :]
        hidden = part > 100.0
        top = i * rows
        v_ref[top : top + rows, :HEAD_SIZE] = jnp.where(hidden, jnp.zeros_like(part), part)
        v_ref[top : top + rows, HEAD_SIZE:] = jnp.where(hidden, jnp.zeros_like(part), jnp.ones_like(part))
        top = len(lines) * rows + i * own
        v_ref[top : top + own, :HEAD_SIZE] = ref[both + rows :, :]
        v_ref[top : top + own, HEAD_SIZE:] = jnp.ones((own, HEAD_SIZE), jnp.bfloat16)
    owner = owner_ref[0]
    same = lax.div(owner, N_Y) == lax.div(place(), N_Y)
    asked = jnp.where(same, lax.rem(lax.axis_index("y") - lax.rem(owner, N_Y) + N_Y, N_Y), -1)
    own_keys = jnp.concatenate([ref[rows:both, :] for ref in lines], axis=0)
    row = lax.rem(lax.broadcasted_iota(jnp.int32, (n, own_keys.shape[0]), 0), own)
    col = lax.broadcasted_iota(jnp.int32, (n, own_keys.shape[0]), 1) - asked * own
    scores = [dot_nt(q, ref[0:rows, :]) for ref in lines]
    scores.append(jnp.where((asked >= 0) & (col >= 0) & (col <= row), dot_nt(q, own_keys), -jnp.inf))
    tiles = [s[:, i : i + HEAD_SIZE] for s in scores for i in range(0, s.shape[1], HEAD_SIZE)]
    peak = jnp.max(functools.reduce(jnp.maximum, tiles), axis=1, keepdims=True)
    weights = [jnp.exp2((tile - peak) * c).astype(jnp.bfloat16) for tile in tiles]
    acc = dot_nn(jnp.concatenate(weights, axis=1), v_ref[...])
    total = acc[:, HEAD_SIZE:]
    out = acc[:, :HEAD_SIZE] / total
    out_high = out.astype(jnp.bfloat16)
    out_low = (out - out_high.astype(jnp.float32)).astype(jnp.bfloat16)
    lse = peak * SCALE + jnp.log(total)
    high, mid, low = split3(lse)
    row = lax.broadcasted_iota(jnp.int32, (piece, HEAD_SIZE), 0)
    lane = lax.broadcasted_iota(jnp.int32, (piece, HEAD_SIZE), 1)
    for p, o_ref in enumerate(o_refs):
        part = slice(p * piece, (p + 1) * piece)
        pair = jnp.where(row == lane, high[part], jnp.where(row + piece == lane, mid[part], 0.0))
        last = jnp.where(row == lane, low[part], 0.0)
        o_ref[0:piece, :] = out_high[part]
        o_ref[piece : 2 * piece, :] = out_low[part]
        o_ref[2 * piece :, :] = code_rows(
            jnp.sum(pair, axis=0, keepdims=True), jnp.sum(last, axis=0, keepdims=True), 16
        )


def request_partials(owner, queries, lines, own):
    count, piece = len(queries), queries[0].shape[0]
    keys = len(lines) * lines[0].shape[0] // 2
    vmem = pl.BlockSpec(memory_space=pltpu.VMEM)
    return pl.pallas_call(
        functools.partial(request_kernel, own, count),
        out_shape=[jax.ShapeDtypeStruct((2 * piece + 16, HEAD_SIZE), jnp.bfloat16)] * count,
        in_specs=[pl.BlockSpec(memory_space=pltpu.SMEM)] + [vmem] * (count + len(lines)),
        out_specs=[vmem] * count,
        scratch_shapes=[pltpu.VMEM((keys, 2 * HEAD_SIZE), jnp.bfloat16)],
        compiler_params=pltpu.CompilerParams(vmem_limit_bytes=VMEM_LIMIT),
        cost_estimate=pl.CostEstimate(
            flops=3 * 10**9, bytes_accessed=2**20, transcendentals=count * piece * keys
        ),
        name="request_partials",
    )(owner, *queries, *lines)


def join_kernel(parts_in, keep_code, *refs):
    x_refs, o_ref = refs[:-1], refs[-1]
    if len(x_refs) == 1:
        x_refs = [x_refs[0].at[i] for i in range(x_refs[0].shape[0])]
    height = x_refs[0].shape[0]
    top = height - 16
    piece = top // parts_in
    count = max(len(x_refs), 8)
    row = lax.broadcasted_iota(jnp.int32, (count, HEAD_SIZE), 0)
    lane = lax.broadcasted_iota(jnp.int32, (count, HEAD_SIZE), 1)
    pair = jnp.zeros((count, HEAD_SIZE), jnp.float32)
    last = jnp.zeros((count, HEAD_SIZE), jnp.float32)
    for i, ref in enumerate(x_refs):
        code = ref[top:height, :].astype(jnp.float32)
        pair = jnp.where(row == i, code[0:1, :], pair)
        last = jnp.where(row == i, code[1:2, :], last)
    lse = jnp.where(lane < piece, pair + pltpu.roll(pair, piece, 1) + last, 0.0)
    lse = jnp.where(row < len(x_refs), lse, -jnp.inf)
    peak = jnp.max(lse, axis=0, keepdims=True)
    weight = jnp.exp(lse - peak)
    total = jnp.sum(weight, axis=0, keepdims=True)
    column = jnp.transpose(weight / total)
    out = jnp.zeros((piece, HEAD_SIZE), jnp.float32)
    for i, ref in enumerate(x_refs):
        part = ref[0:piece, :].astype(jnp.float32)
        if parts_in > 1:
            part = part + ref[piece:top, :].astype(jnp.float32)
        out = out + column[0:piece, i : i + 1] * part
    parts = [out.astype(jnp.bfloat16)]
    if keep_code:
        high, mid, low = split3(peak + jnp.log(total))
        pair = jnp.where(lane[0:1] < piece, high, pltpu.roll(mid, piece, 1))
        parts.append(code_rows(pair, low, 16))
    part = jnp.concatenate(parts, axis=0)
    if len(o_ref.shape) == 2:
        o_ref[...] = part
    else:
        for i in range(o_ref.shape[0]):
            o_ref[i] = part


def join(arrays, copies, parts_in, keep_code):
    height = (arrays[0].shape[-2] - 16) // parts_in + (16 if keep_code else 0)
    shape = (copies, height, HEAD_SIZE) if copies else (height, HEAD_SIZE)
    return pl.pallas_call(
        functools.partial(join_kernel, parts_in, keep_code),
        out_shape=jax.ShapeDtypeStruct(shape, jnp.bfloat16),
        compiler_params=pltpu.CompilerParams(vmem_limit_bytes=VMEM_LIMIT),
        cost_estimate=pl.CostEstimate(flops=3 * 10**9, bytes_accessed=2**19, transcendentals=1024),
        name="join_pieces",
    )(*arrays)


def answer_kernel(owner_ref, x_ref, _, o_ref, rows_ref, sem):
    own = rows_ref.shape[0]
    some = x_ref.shape[1] // own

    @pl.when(place() == owner_ref[0])
    def _():
        for j in range(x_ref.shape[0]):
            x, y = j // N_Y, j % N_Y
            for i in range(some):
                lane = (GROUP * y + some * x + i) * HEAD_SIZE
                rows_ref[:, lane : lane + HEAD_SIZE] = x_ref[j, i * own : (i + 1) * own, :]
        copy = pltpu.make_async_copy(rows_ref, o_ref, sem)
        copy.start()
        copy.wait()


def answer_rows(owner, x, zeros):
    any_spec = pl.BlockSpec(memory_space=pl.ANY)
    return pl.pallas_call(
        answer_kernel,
        out_shape=jax.ShapeDtypeStruct(zeros.shape, zeros.dtype),
        in_specs=[pl.BlockSpec(memory_space=pltpu.SMEM), pl.BlockSpec(memory_space=pltpu.VMEM), any_spec],
        out_specs=any_spec,
        input_output_aliases={2: 0},
        scratch_shapes=[pltpu.VMEM(zeros.shape, zeros.dtype), pltpu.SemaphoreType.DMA],
        compiler_params=pltpu.CompilerParams(vmem_limit_bytes=VMEM_LIMIT),
        cost_estimate=pl.CostEstimate(flops=2**18, bytes_accessed=2**19, transcendentals=0),
        name="answer_rows",
    )(owner, x, zeros)


def exchange(x, axis, groups=None):
    return lax.all_to_all(x, axis, split_axis=0, concat_axis=0, axis_index_groups=groups, tiled=True)


def local(n_z, n_x, n_y, q, k, v, block_lengths, rq, rk, rv, query_owner):
    n_xy = n_x * n_y
    z, x, y = (lax.axis_index(name) for name in ("z", "x", "y"))
    own_len = block_lengths
    own_rows = rk.shape[0]
    down = [list(range(n_z))[::-1]]

    def move(value, pairs):
        return lax.ppermute(value, ("z", "x", "y"), pairs)

    def shift_x(value, count):
        return lax.ppermute(value, "x", [(a, (a + count) % n_x) for a in range(n_x)])

    sent, pieces, lines = prepare(own_len, rq, k, v, rk, rv, n_x, n_y)
    moved = exchange(sent, ("x", "y", "head"))
    got = [move(pieces[i], [(0, i * n_y)]) for i in range(1, n_x)]
    lines = [lines[0]] + [
        lax.ppermute(lines[i], "y", [(a, (a + i) % n_y) for a in range(n_y)]) for i in range(1, n_y)
    ]

    piece = (2 * moved.shape[1], HEAD_SIZE)
    moved, got = lax.optimization_barrier((moved, got))
    moved = choose(plane_kernel, query_owner, moved, (n_z,) + piece, 8 * 10**8)
    anchor = jnp.where(x == 0, pieces[0], got[0] + got[1] + got[2])
    got = [move(anchor, [(i * n_y, (to * n_x + i) * n_y) for i in range(n_x)]) for to in (6, 4, 2)]
    moved = exchange(moved, "z", down)

    moved = choose(line_kernel, query_owner, moved, piece, 3 * 10**9)
    moved, lines = lax.optimization_barrier((moved, lines))
    anchor = jnp.where(z == 0, anchor, got[0] + got[1] + got[2])
    rows = [(to * n_x + i) * n_y for to in (0, 2, 4, 6) for i in range(n_x)]
    got = [move(anchor, [(p, p + j) for p in rows]) for j in (3, 2, 1)]
    queries = [moved] + [shift_x(moved, i) for i in range(1, n_x)]

    partials = request_partials(query_owner, queries, lines, own_rows)
    anchor = jnp.where(y == 0, anchor, got[0] + got[1] + got[2])
    plane = range(n_xy)
    got = move(anchor, [(a * n_xy + p, (a + 1) * n_xy + p) for a in range(0, n_z, 2) for p in plane])
    partials = [partials[0]] + [shift_x(partials[i], n_x - i) for i in range(1, n_x)]

    planes = join(partials, n_z, 2, True)
    anchor = jnp.where(z % 2 == 0, anchor, got)
    anchors = [anchor]
    for i in range(1, n_x):
        anchors.append(shift_x(anchor, i))
    planes = exchange(planes, "z", down)

    answer = exchange(join([planes], n_xy, 1, False), ("x", "y"))
    context_output, zeros = context_attention(own_len, q, k, v, anchors, own_rows)
    request_output = answer_rows(query_owner, answer, zeros)
    return context_output, request_output


def solution(mesh):
    n_z, n_x, n_y = 8, N_X, N_Y
    grid = jax.sharding.Mesh(mesh.devices.reshape(n_z, n_x, n_y, 2), ("z", "x", "y", "head"))
    ctx = ("z", "x", "y")
    in_specs = (
        P(ctx, "head"),
        P(ctx, "head"),
        P(ctx, "head"),
        P(ctx),
        P(ctx + ("head",), None),
        P(ctx, "head"),
        P(ctx, "head"),
        P(),
    )
    out_specs = (P(ctx, "head"), P(ctx, "head"))
    return jax.shard_map(
        functools.partial(local, n_z, n_x, n_y),
        mesh=grid,
        in_specs=in_specs,
        out_specs=out_specs,
        check_vma=False,
    )
```

```python
import functools

import jax
import jax.numpy as jnp
from jax import lax
from jax.experimental import pallas as pl
from jax.experimental.pallas import tpu as pltpu
from jax.sharding import PartitionSpec as P

HEAD_SIZE = 128
GROUP = 8
SCALE = HEAD_SIZE**-0.5
LOG2E = 1.4426950408889634
LN2 = 0.6931471805599453
MARK = 1024.0
VMEM_LIMIT = 32 * 1024 * 1024
STACK = 4
N_X, N_Y = 4, 4


def place():
    return (lax.axis_index("z") * N_X + lax.axis_index("x")) * N_Y + lax.axis_index("y")


def dot_nt(a, b):
    return lax.dot_general(a, b, (((1,), (1,)), ((), ())), preferred_element_type=jnp.float32)


def dot_nn(a, b):
    return lax.dot_general(a, b, (((1,), (0,)), ((), ())), preferred_element_type=jnp.float32)


def context_kernel(count, len_ref, q_ref, k_ref, v_ref, *refs):
    anchor_refs = refs[:count]
    o_ref, zero_ref, vs_ref, out_ref, sems = refs[-5:]
    zero_ref[...] = jnp.zeros_like(zero_ref)
    rows, width = k_ref.shape
    half = rows // 2
    heads = width // HEAD_SIZE
    own_len = len_ref[0]
    root = place() == 0
    c = SCALE * LOG2E
    row = lax.broadcasted_iota(jnp.int32, (STACK * half, half), 0)
    col = lax.broadcasted_iota(jnp.int32, (STACK * half, half), 1)
    causal = jnp.where(col <= lax.rem(row, half), 0.0, -jnp.inf).astype(jnp.float32)

    def lanes(g):
        return slice(g * HEAD_SIZE, (g + 1) * HEAD_SIZE)

    def load(h):
        ak = jnp.concatenate([ref[:, lanes(h)] for ref in anchor_refs], axis=0)
        ak = jnp.where(root, jnp.broadcast_to(k_ref[0:1, lanes(h)], ak.shape), ak)
        av = jnp.concatenate([ref[:, lanes(heads + h)] for ref in anchor_refs], axis=0)
        hidden = (av > 100.0) | root
        vs_ref[h, 0:rows, :HEAD_SIZE] = jnp.where(hidden, jnp.zeros_like(av), av)
        vs_ref[h, 0:rows, HEAD_SIZE:] = jnp.where(hidden, jnp.zeros_like(av), jnp.ones_like(av))
        vs_ref[h, rows:, :HEAD_SIZE] = v_ref[:, lanes(h)]
        vs_ref[h, rows:, HEAD_SIZE:] = jnp.ones((rows, HEAD_SIZE), jnp.bfloat16)
        return ak

    def scores(h, top, g, ak):
        keys = top + half
        q = jnp.concatenate([q_ref[top:keys, lanes(g + i)] for i in range(STACK)], axis=0)
        sa = dot_nt(q, ak)
        so = dot_nt(q, k_ref[0:keys, lanes(h)])
        tiles = [sa[:, i : i + half] for i in range(0, rows, half)]
        tiles += [so[:, i : i + half] for i in range(0, top, half)]
        return tiles + [so[:, top:keys] + causal]

    def finish(index, h, top, g, tiles):
        keys = top + half
        live = (top + lax.broadcasted_iota(jnp.int32, (half, HEAD_SIZE), 0)) < own_len
        peak = jnp.max(functools.reduce(jnp.maximum, tiles), axis=1, keepdims=True)
        weights = [jnp.exp2((tile - peak) * c).astype(jnp.bfloat16) for tile in tiles]
        acc = dot_nn(jnp.concatenate(weights, axis=1), vs_ref[h, 0 : rows + keys, :])
        total = acc[:, HEAD_SIZE:]
        inverse = pl.reciprocal(total, approx=True)
        inverse = inverse * (2.0 - total * inverse)
        out = acc[:, :HEAD_SIZE] * inverse
        for i in range(STACK):
            part = jnp.where(live, out[i * half : (i + 1) * half], 0.0)
            out_ref[top:keys, lanes(g + i)] = part.astype(jnp.bfloat16)
        where = (slice(top, keys), slice(g * HEAD_SIZE, (g + STACK) * HEAD_SIZE))
        copy = pltpu.make_async_copy(out_ref.at[where], o_ref.at[where], sems.at[index])
        copy.start()
        return copy

    work = [
        (h, top, h * GROUP + g) for h in range(heads) for top in (half, 0) for g in range(0, GROUP, STACK)
    ]
    ak = load(0)
    tiles = scores(*work[0], ak)
    copies = []
    for i, item in enumerate(work):
        later = None
        if i + 1 < len(work):
            if work[i + 1][0] != item[0]:
                ak = load(work[i + 1][0])
            later = scores(*work[i + 1], ak)
        copies.append(finish(i, *item, tiles))
        tiles = later
    for copy in copies:
        copy.wait()


def context_attention(own_len, q, k, v, anchor, own_rows):
    rows, width = q.shape
    heads = k.shape[1] // HEAD_SIZE
    vmem = pl.BlockSpec(memory_space=pltpu.VMEM)
    tiles = 2 * heads * GROUP // STACK
    return pl.pallas_call(
        functools.partial(context_kernel, len(anchor)),
        out_shape=[
            jax.ShapeDtypeStruct((rows, width), jnp.bfloat16),
            jax.ShapeDtypeStruct((own_rows, width), jnp.bfloat16),
        ],
        in_specs=[pl.BlockSpec(memory_space=pltpu.SMEM)] + [vmem] * (3 + len(anchor)),
        out_specs=[pl.BlockSpec(memory_space=pl.ANY), vmem],
        scratch_shapes=[
            pltpu.VMEM((heads, 2 * rows, 2 * HEAD_SIZE), jnp.bfloat16),
            pltpu.VMEM((rows, width), jnp.bfloat16),
            pltpu.SemaphoreType.DMA((tiles,)),
        ],
        compiler_params=pltpu.CompilerParams(vmem_limit_bytes=VMEM_LIMIT),
        cost_estimate=pl.CostEstimate(
            flops=8 * rows * width * rows, bytes_accessed=5 * 2**20, transcendentals=2 * rows * rows * heads * GROUP
        ),
        name="context_attention",
    )(own_len, q, k, v, *anchor)


def pieces_kernel(len_ref, k_ref, v_ref, *o_refs):
    rows, width = k_ref.shape
    slab = rows // len(o_refs)
    first = jnp.broadcast_to(k_ref[0:1, :], (slab, width))
    for i, o_ref in enumerate(o_refs):
        span = slice(i * slab, (i + 1) * slab)
        valid = (i * slab + lax.broadcasted_iota(jnp.int32, first.shape, 0)) < len_ref[0]
        o_ref[:, :width] = jnp.where(valid, k_ref[span, :], first)
        o_ref[:, width:] = jnp.where(valid, v_ref[span, :], jnp.full_like(first, MARK))


def mark_kernel(len_ref, k_ref, v_ref, rk_ref, rv_ref, *lines):
    rows = k_ref.shape[0]
    own = rk_ref.shape[0]
    valid = lax.broadcasted_iota(jnp.int32, (rows, HEAD_SIZE), 0) < len_ref[0]
    y = lax.axis_index("y")
    for i, o_ref in enumerate(lines):
        head = lax.rem(y + i, len(lines))
        lanes = pl.ds(pl.multiple_of(head * HEAD_SIZE, HEAD_SIZE), HEAD_SIZE)
        first = k_ref[0:1, lanes]
        o_ref[0:rows, :] = jnp.where(valid, k_ref[:, lanes], jnp.broadcast_to(first, valid.shape))
        o_ref[rows : rows + own, :] = rk_ref[:, lanes]
        mark = jnp.full((rows, HEAD_SIZE), MARK, jnp.bfloat16)
        o_ref[rows + own : 2 * rows + own, :] = jnp.where(valid, v_ref[:, lanes], mark)
        o_ref[2 * rows + own :, :] = rv_ref[:, lanes]


def pack_kernel(n_y, rq_ref, o_ref):
    own, width = rq_ref.shape
    targets = o_ref.shape[0] // 2
    some = o_ref.shape[1] // own
    for j in range(targets):
        x, y = j // n_y, j % n_y
        for c in range(2):
            for i in range(some):
                lane = c * (width // 2) + (GROUP * y + some * x + i) * HEAD_SIZE
                o_ref[2 * j + c, i * own : (i + 1) * own, :] = rq_ref[:, lane : lane + HEAD_SIZE]


def prepare_kernel(n_x, n_y, len_ref, rq_ref, k_ref, v_ref, rk_ref, rv_ref, sent_ref, *refs):
    pieces, lines = refs[:n_x], refs[n_x : n_x + n_y]
    held_ref, sems = refs[n_x + n_y :]

    @pl.when(place() == 0)
    def _():
        pieces_kernel(len_ref, k_ref, v_ref, *[held_ref.at[i] for i in range(n_x)])
        copies = [pltpu.make_async_copy(held_ref.at[i], pieces[i], sems.at[i]) for i in range(n_x)]
        for copy in copies:
            copy.start()
        for copy in copies:
            copy.wait()

    pack_kernel(n_y, rq_ref, sent_ref)
    mark_kernel(len_ref, k_ref, v_ref, rk_ref, rv_ref, *lines)


def prepare(own_len, rq, k, v, rk, rv, n_x, n_y):
    rows, width = k.shape
    vmem = pl.BlockSpec(memory_space=pltpu.VMEM)
    targets = 2 * n_x * n_y
    shapes = [jax.ShapeDtypeStruct((targets, rq.size // (targets * HEAD_SIZE), HEAD_SIZE), k.dtype)]
    shapes += [jax.ShapeDtypeStruct((rows // n_x, 2 * width), k.dtype)] * n_x
    shapes += [jax.ShapeDtypeStruct((2 * (rows + rk.shape[0]), HEAD_SIZE), k.dtype)] * n_y
    out = pl.pallas_call(
        functools.partial(prepare_kernel, n_x, n_y),
        out_shape=shapes,
        in_specs=[pl.BlockSpec(memory_space=pltpu.SMEM)] + [vmem] * 5,
        out_specs=[vmem] + [pl.BlockSpec(memory_space=pl.ANY)] * n_x + [vmem] * n_y,
        scratch_shapes=[pltpu.VMEM((n_x, rows // n_x, 2 * width), k.dtype), pltpu.SemaphoreType.DMA((n_x,))],
        compiler_params=pltpu.CompilerParams(vmem_limit_bytes=56 * 1024 * 1024),
        cost_estimate=pl.CostEstimate(flops=2**18, bytes_accessed=5 * 2**19, transcendentals=0),
        name="prepare",
    )(own_len, rq, k, v, rk, rv)
    return out[0], out[1 : 1 + n_x], out[1 + n_x :]


def plane_kernel(owner_ref, x_ref, o_ref):
    own = 16
    source = 2 * lax.rem(owner_ref[0], N_X * N_Y)
    parts = []
    for i in range(x_ref.shape[1] // own):
        pick = slice(i * own, (i + 1) * own)
        parts += [x_ref[source, pick, :], x_ref[source + 1, pick, :]]
    part = jnp.concatenate(parts, axis=0)
    for z in range(o_ref.shape[0]):
        o_ref[z] = part


def line_kernel(owner_ref, x_ref, o_ref):
    o_ref[...] = x_ref[x_ref.shape[0] - 1 - lax.div(owner_ref[0], N_X * N_Y)]


def choose(kernel, owner, x, shape, flops):
    vmem = pl.BlockSpec(memory_space=pltpu.VMEM)
    return pl.pallas_call(
        kernel,
        out_shape=jax.ShapeDtypeStruct(shape, x.dtype),
        in_specs=[pl.BlockSpec(memory_space=pltpu.SMEM), vmem],
        out_specs=vmem,
        compiler_params=pltpu.CompilerParams(vmem_limit_bytes=VMEM_LIMIT),
        cost_estimate=pl.CostEstimate(flops=flops, bytes_accessed=2**19, transcendentals=0),
        name="choose",
    )(owner, x)


def split3(x):
    high = x.astype(jnp.bfloat16).astype(jnp.float32)
    rest = x - high
    mid = rest.astype(jnp.bfloat16).astype(jnp.float32)
    low = (rest - mid).astype(jnp.bfloat16).astype(jnp.float32)
    return high, mid, low


def code_rows(pair, last, height):
    row = lax.broadcasted_iota(jnp.int32, (height, HEAD_SIZE), 0)
    return jnp.where(row == 0, pair, jnp.where(row == 1, last, 0.0)).astype(jnp.bfloat16)


def request_kernel(own, count, owner_ref, *refs):
    q_refs, lines = refs[:count], refs[count : -count - 1]
    o_refs, v_ref = refs[-count - 1 : -1], refs[-1]
    piece = q_refs[0].shape[0]
    n = count * piece
    both = lines[0].shape[0] // 2
    rows = both - own
    c = SCALE * LOG2E
    q = jnp.concatenate([ref[...] for ref in q_refs], axis=0)
    for i, ref in enumerate(lines):
        part = ref[both : both + rows, :]
        hidden = part > 100.0
        top = i * rows
        v_ref[top : top + rows, :HEAD_SIZE] = jnp.where(hidden, jnp.zeros_like(part), part)
        v_ref[top : top + rows, HEAD_SIZE:] = jnp.where(hidden, jnp.zeros_like(part), jnp.ones_like(part))
        top = len(lines) * rows + i * own
        v_ref[top : top + own, :HEAD_SIZE] = ref[both + rows :, :]
        v_ref[top : top + own, HEAD_SIZE:] = jnp.ones((own, HEAD_SIZE), jnp.bfloat16)
    owner = owner_ref[0]
    same = lax.div(owner, N_Y) == lax.div(place(), N_Y)
    asked = jnp.where(same, lax.rem(lax.axis_index("y") - lax.rem(owner, N_Y) + N_Y, N_Y), -1)
    own_keys = jnp.concatenate([ref[rows:both, :] for ref in lines], axis=0)
    row = lax.rem(lax.broadcasted_iota(jnp.int32, (n, own_keys.shape[0]), 0), own)
    col = lax.broadcasted_iota(jnp.int32, (n, own_keys.shape[0]), 1) - asked * own
    scores = [dot_nt(q, ref[0:rows, :]) for ref in lines]
    scores.append(jnp.where((asked >= 0) & (col >= 0) & (col <= row), dot_nt(q, own_keys), -jnp.inf))
    tiles = [s[:, i : i + HEAD_SIZE] for s in scores for i in range(0, s.shape[1], HEAD_SIZE)]
    peak = jnp.max(functools.reduce(jnp.maximum, tiles), axis=1, keepdims=True)
    weights = [jnp.exp2((tile - peak) * c).astype(jnp.bfloat16) for tile in tiles]
    acc = dot_nn(jnp.concatenate(weights, axis=1), v_ref[...])
    total = acc[:, HEAD_SIZE:]
    out = acc[:, :HEAD_SIZE] / total
    out_high = out.astype(jnp.bfloat16)
    out_low = (out - out_high.astype(jnp.float32)).astype(jnp.bfloat16)
    lse = peak * SCALE + jnp.log(total)
    high, mid, low = split3(lse)
    row = lax.broadcasted_iota(jnp.int32, (piece, HEAD_SIZE), 0)
    lane = lax.broadcasted_iota(jnp.int32, (piece, HEAD_SIZE), 1)
    for p, o_ref in enumerate(o_refs):
        part = slice(p * piece, (p + 1) * piece)
        pair = jnp.where(row == lane, high[part], jnp.where(row + piece == lane, mid[part], 0.0))
        last = jnp.where(row == lane, low[part], 0.0)
        o_ref[0:piece, :] = out_high[part]
        o_ref[piece : 2 * piece, :] = out_low[part]
        o_ref[2 * piece :, :] = code_rows(
            jnp.sum(pair, axis=0, keepdims=True), jnp.sum(last, axis=0, keepdims=True), 16
        )


def request_partials(owner, queries, lines, own):
    count, piece = len(queries), queries[0].shape[0]
    keys = len(lines) * lines[0].shape[0] // 2
    vmem = pl.BlockSpec(memory_space=pltpu.VMEM)
    return pl.pallas_call(
        functools.partial(request_kernel, own, count),
        out_shape=[jax.ShapeDtypeStruct((2 * piece + 16, HEAD_SIZE), jnp.bfloat16)] * count,
        in_specs=[pl.BlockSpec(memory_space=pltpu.SMEM)] + [vmem] * (count + len(lines)),
        out_specs=[vmem] * count,
        scratch_shapes=[pltpu.VMEM((keys, 2 * HEAD_SIZE), jnp.bfloat16)],
        compiler_params=pltpu.CompilerParams(vmem_limit_bytes=VMEM_LIMIT),
        cost_estimate=pl.CostEstimate(
            flops=3 * 10**9, bytes_accessed=2**20, transcendentals=count * piece * keys
        ),
        name="request_partials",
    )(owner, *queries, *lines)


def join_kernel(parts_in, keep_code, *refs):
    x_refs, o_ref = refs[:-1], refs[-1]
    if len(x_refs) == 1:
        x_refs = [x_refs[0].at[i] for i in range(x_refs[0].shape[0])]
    height = x_refs[0].shape[0]
    top = height - 16
    piece = top // parts_in
    count = max(len(x_refs), 8)
    row = lax.broadcasted_iota(jnp.int32, (count, HEAD_SIZE), 0)
    lane = lax.broadcasted_iota(jnp.int32, (count, HEAD_SIZE), 1)
    pair = jnp.zeros((count, HEAD_SIZE), jnp.float32)
    last = jnp.zeros((count, HEAD_SIZE), jnp.float32)
    for i, ref in enumerate(x_refs):
        code = ref[top:height, :].astype(jnp.float32)
        pair = jnp.where(row == i, code[0:1, :], pair)
        last = jnp.where(row == i, code[1:2, :], last)
    lse = jnp.where(lane < piece, pair + pltpu.roll(pair, piece, 1) + last, 0.0)
    lse = jnp.where(row < len(x_refs), lse, -jnp.inf)
    peak = jnp.max(lse, axis=0, keepdims=True)
    weight = jnp.exp(lse - peak)
    total = jnp.sum(weight, axis=0, keepdims=True)
    column = jnp.transpose(weight / total)
    out = jnp.zeros((piece, HEAD_SIZE), jnp.float32)
    for i, ref in enumerate(x_refs):
        part = ref[0:piece, :].astype(jnp.float32)
        if parts_in > 1:
            part = part + ref[piece:top, :].astype(jnp.float32)
        out = out + column[0:piece, i : i + 1] * part
    parts = [out.astype(jnp.bfloat16)]
    if keep_code:
        high, mid, low = split3(peak + jnp.log(total))
        pair = jnp.where(lane[0:1] < piece, high, pltpu.roll(mid, piece, 1))
        parts.append(code_rows(pair, low, 16))
    part = jnp.concatenate(parts, axis=0)
    if len(o_ref.shape) == 2:
        o_ref[...] = part
    else:
        for i in range(o_ref.shape[0]):
            o_ref[i] = part


def join(arrays, copies, parts_in, keep_code):
    height = (arrays[0].shape[-2] - 16) // parts_in + (16 if keep_code else 0)
    shape = (copies, height, HEAD_SIZE) if copies else (height, HEAD_SIZE)
    return pl.pallas_call(
        functools.partial(join_kernel, parts_in, keep_code),
        out_shape=jax.ShapeDtypeStruct(shape, jnp.bfloat16),
        compiler_params=pltpu.CompilerParams(vmem_limit_bytes=VMEM_LIMIT),
        cost_estimate=pl.CostEstimate(flops=3 * 10**9, bytes_accessed=2**19, transcendentals=1024),
        name="join_pieces",
    )(*arrays)


def answer_kernel(owner_ref, x_ref, _, o_ref, rows_ref, sem):
    own = rows_ref.shape[0]
    some = x_ref.shape[1] // own

    @pl.when(place() == owner_ref[0])
    def _():
        for j in range(x_ref.shape[0]):
            x, y = j // N_Y, j % N_Y
            for i in range(some):
                lane = (GROUP * y + some * x + i) * HEAD_SIZE
                rows_ref[:, lane : lane + HEAD_SIZE] = x_ref[j, i * own : (i + 1) * own, :]
        copy = pltpu.make_async_copy(rows_ref, o_ref, sem)
        copy.start()
        copy.wait()


def answer_rows(owner, x, zeros):
    any_spec = pl.BlockSpec(memory_space=pl.ANY)
    return pl.pallas_call(
        answer_kernel,
        out_shape=jax.ShapeDtypeStruct(zeros.shape, zeros.dtype),
        in_specs=[pl.BlockSpec(memory_space=pltpu.SMEM), pl.BlockSpec(memory_space=pltpu.VMEM), any_spec],
        out_specs=any_spec,
        input_output_aliases={2: 0},
        scratch_shapes=[pltpu.VMEM(zeros.shape, zeros.dtype), pltpu.SemaphoreType.DMA],
        compiler_params=pltpu.CompilerParams(vmem_limit_bytes=VMEM_LIMIT),
        cost_estimate=pl.CostEstimate(flops=2**18, bytes_accessed=2**19, transcendentals=0),
        name="answer_rows",
    )(owner, x, zeros)


def exchange(x, axis, groups=None):
    return lax.all_to_all(x, axis, split_axis=0, concat_axis=0, axis_index_groups=groups, tiled=True)


def local(n_z, n_x, n_y, q, k, v, block_lengths, rq, rk, rv, query_owner):
    n_xy = n_x * n_y
    z, x, y = (lax.axis_index(name) for name in ("z", "x", "y"))
    own_len = block_lengths
    own_rows = rk.shape[0]
    down = [list(range(n_z))[::-1]]

    def move(value, pairs):
        return lax.ppermute(value, ("z", "x", "y"), pairs)

    def shift_x(value, count):
        return lax.ppermute(value, "x", [(a, (a + count) % n_x) for a in range(n_x)])

    sent, pieces, lines = prepare(own_len, rq, k, v, rk, rv, n_x, n_y)
    moved = exchange(sent, ("x", "y", "head"))
    got = [move(pieces[i], [(0, i * n_y)]) for i in range(1, n_x)]
    lines = [lines[0]] + [
        lax.ppermute(lines[i], "y", [(a, (a + i) % n_y) for a in range(n_y)]) for i in range(1, n_y)
    ]

    piece = (2 * moved.shape[1], HEAD_SIZE)
    moved, got = lax.optimization_barrier((moved, got))
    moved = choose(plane_kernel, query_owner, moved, (n_z,) + piece, 8 * 10**8)
    anchor = jnp.where(x == 0, pieces[0], got[0] + got[1] + got[2])
    got = [move(anchor, [(i * n_y, (to * n_x + i) * n_y) for i in range(n_x)]) for to in (3, 5)]
    moved = exchange(moved, "z", down)

    moved = choose(line_kernel, query_owner, moved, piece, 3 * 10**9)
    moved, lines = lax.optimization_barrier((moved, lines))
    anchor = jnp.where(z == 0, anchor, got[0] + got[1])
    rows = [(to * n_x + i) * n_y for to in (0, 3, 5) for i in range(n_x)]
    got = [move(anchor, [(p, p + j) for p in rows]) for j in (3, 2, 1)]
    queries = [moved] + [shift_x(moved, i) for i in range(1, n_x)]

    partials = request_partials(query_owner, queries, lines, own_rows)
    anchor = jnp.where(y == 0, anchor, got[0] + got[1] + got[2])
    plane = range(n_xy)
    steps = (((0, 1), (3, 4), (5, 6)), ((3, 2), (5, 7)))
    got = [move(anchor, [(a * n_xy + p, b * n_xy + p) for a, b in step for p in plane]) for step in steps]
    partials = [partials[0]] + [shift_x(partials[i], n_x - i) for i in range(1, n_x)]

    planes = join(partials, n_z, 2, True)
    anchor = jnp.where((z == 0) | (z == 3) | (z == 5), anchor, got[0] + got[1])
    anchors = [anchor]
    for i in range(1, n_x):
        anchors.append(shift_x(anchor, i))
    planes = exchange(planes, "z", down)

    answer = exchange(join([planes], n_xy, 1, False), ("x", "y"))
    context_output, zeros = context_attention(own_len, q, k, v, anchors, own_rows)
    request_output = answer_rows(query_owner, answer, zeros)
    return context_output, request_output


def solution(mesh):
    n_z, n_x, n_y = 8, N_X, N_Y
    grid = jax.sharding.Mesh(mesh.devices.reshape(n_z, n_x, n_y, 2), ("z", "x", "y", "head"))
    ctx = ("z", "x", "y")
    in_specs = (
        P(ctx, "head"),
        P(ctx, "head"),
        P(ctx, "head"),
        P(ctx),
        P(ctx + ("head",), None),
        P(ctx, "head"),
        P(ctx, "head"),
        P(),
    )
    out_specs = (P(ctx, "head"), P(ctx, "head"))
    return jax.shard_map(
        functools.partial(local, n_z, n_x, n_y),
        mesh=grid,
        in_specs=in_specs,
        out_specs=out_specs,
        check_vma=False,
    )
```
